256 devices in a mesh: mem: 16 (over y, x_lo, core), lat: 16 (over z, x_hi).
Axes of the slice: x: 4 (x_hi: 2, x_lo: 2; x = x_hi * 2 + x_lo), y: 4, z: 8, core: 2. Of those that a mesh axis runs over, the one named last changes fastest.
Arguments:
- coarse_weights: bfloat16 [128, 64, 8, 256], P('lat', 'mem'), may hold values from -6 to 6
- perturbations: bfloat16 [64, 8, 512, 1024], P('mem', None, 'lat'), may hold values from -6 to 6
- lat_matrix: bfloat16 [512, 128], P('lat'), may hold values from -0.5 to 0.5
- lon_matrix: bfloat16 [256, 1024], replicated, may hold values from -0.375 to 0.375
- wind_field: float32 [2, 512, 1024], P(None, 'lat', 'mem'), may hold values from -0.4 to 0.4
- observed_cell: int32 [4, 8, 512, 128], P(None, None, 'lat', 'mem'), may hold values from 0 to 7
- observed_value: float32 [4, 8, 512, 128], P(None, None, 'lat', 'mem'), may hold values from -6 to 6
- observed_weight: float32 [4, 8, 512, 128], P(None, None, 'lat', 'mem'), may hold values from 0.5 to 4
Outputs:
- gradient: float32 [128, 64, 8, 256], P('lat', 'mem')
- increment: float32 [8, 512, 1024], P(None, 'lat', 'mem')
The draws below stay inside these ranges and needn't reach their ends.
Inputs may be any that keep to these rules, and one draw needn't show every extreme that they name: `observed_cell`: the observed cell is an offset within its block of 8 longitudes.
All inputs are finite; a program needn't handle non-finite values.
Results may differ from the reference program's by a relative error of at most 0.0003.
Values may be sent and summed in bfloat16 or wider, within the bound.
No kernel may reach another device: no remote copies, remote signals or barrier semaphores. Data moves between devices by JAX's collectives and lax.ppermute only.
A program may use at most 64 MiB of HBM per device.

```python
import math
import jax
import jax.numpy as jnp
from jax import lax

LEV = 8
STEPS = 4
OBLK = 8
MEMBERS = 64
FLAT = 512
FLON = 1024
CLAT = 128
CLON = 256


def touch_ends(result, key, smallest, high):
    longest = result.shape.index(max(result.shape))
    spots = []
    for shift in (0, 1):
        where = [jax.random.randint(jax.random.fold_in(key, axis), (), 0, length) for axis, length in enumerate(result.shape)]
        where[longest] = (where[longest] + shift) % result.shape[longest]
        spots.append(tuple(where))
    return result.at[spots[0]].set(smallest).at[spots[1]].set(high)


def block_scale(own_key, shape, pieces, least, largest):
    level = 1.0
    for axis_at, shards_of in pieces:
        steps = jax.random.uniform(jax.random.fold_in(jax.random.fold_in(own_key, 6), axis_at), (shards_of,), jnp.float32, least / len(pieces), largest / len(pieces))
        level = level * jnp.repeat(jnp.exp(steps), shape[axis_at] // shards_of).reshape((-1,) + (1,) * (len(shape) - 1 - axis_at))
    return level


def centred(own_key, dims, width, limit, pieces=(), kind=jnp.bfloat16):
    drawn = width * jax.random.normal(own_key, dims, jnp.float32)
    if pieces:
        drawn = drawn * block_scale(own_key, dims, pieces, -0.22, 0.18)
    return jnp.clip(drawn, -limit, limit).astype(kind)


def setup_inputs(seed: int = 0) -> dict:
    arg_keys = jax.random.split(jax.random.key(seed), 9)
    coarse_weights = centred(arg_keys[0], (CLAT, MEMBERS, LEV, CLON), 1.0, 6.0, ((0, 16), (1, 16)))
    perturbations = centred(arg_keys[1], (MEMBERS, LEV, FLAT, FLON), 1.0, 6.0, ((0, 16), (2, 16)))
    lat_matrix = centred(arg_keys[2], (FLAT, CLAT), CLAT ** -0.5, 0.5, ((0, 16),))
    lon_matrix = centred(arg_keys[3], (CLON, FLON), CLON ** -0.5, 0.375)
    wind_field = jnp.clip(jax.random.uniform(arg_keys[4], (2, FLAT, FLON), jnp.float32, -0.4, 0.4) * block_scale(arg_keys[4], (2, FLAT, FLON), ((1, 16), (2, 16)), -0.4, 0.0), -0.4, 0.4)
    observed_cell = touch_ends(jax.random.randint(arg_keys[5], (STEPS, LEV, FLAT, FLON // OBLK), 0, OBLK), jax.random.fold_in(arg_keys[5], 1), 0, OBLK - 1).astype(jnp.int32)
    observed_value = centred(arg_keys[6], (STEPS, LEV, FLAT, FLON // OBLK), 1.0, 6.0, ((2, 16), (3, 16)), jnp.float32)
    observed_weight = jnp.clip(jnp.exp(math.log(4.0) - 2.0794415 * jax.random.uniform(arg_keys[7], (STEPS, LEV, FLAT, FLON // OBLK), jnp.float32) ** block_scale(arg_keys[7], (STEPS, LEV, FLAT, FLON // OBLK), ((2, 16), (3, 16)), -0.2, 0.2)), 0.5, 4.0)
    return dict(coarse_weights=coarse_weights, perturbations=perturbations, lat_matrix=lat_matrix, lon_matrix=lon_matrix, wind_field=wind_field, observed_cell=observed_cell, observed_value=observed_value, observed_weight=observed_weight)


diffusion = 0.2
highest = lax.Precision.HIGHEST

def stencil_parts(padded):
    center = padded[:, 1:-1, 1:-1]
    north_cell = padded[:, 2:, 1:-1]
    south_cell = padded[:, :-2, 1:-1]
    east_cell = padded[:, 1:-1, 2:]
    west_cell = padded[:, 1:-1, :-2]
    return (center, north_cell, south_cell, east_cell, west_cell)

def advance(padded, wind_out):
    center, north_cell, south_cell, east_cell, west_cell = stencil_parts(padded)
    spread = north_cell + south_cell + east_cell + west_cell - 4.0 * center
    return center + diffusion * spread - 0.5 * wind_out[1] * (north_cell - south_cell) - 0.5 * wind_out[0] * (east_cell - west_cell)

def retreat(padded, wind_in):
    center, north_cell, south_cell, east_cell, west_cell = stencil_parts(padded)
    spread = north_cell + south_cell + east_cell + west_cell - 4.0 * center
    along_lon = wind_in[0] * padded
    along_lat = wind_in[1] * padded
    return center + diffusion * spread + 0.5 * (along_lat[:, 2:, 1:-1] - along_lat[:, :-2, 1:-1]) + 0.5 * (along_lon[:, 1:-1, 2:] - along_lon[:, 1:-1, :-2])

def observe(tangent, picked, observed, weighting):
    levels, row_count, col_count = tangent.shape
    blocks = tangent.reshape(levels, row_count, col_count // OBLK, OBLK)
    onehot = (picked[..., None] == jnp.arange(OBLK, dtype=jnp.int32)).astype(jnp.float32)
    looked = lax.optimization_barrier(jnp.sum(blocks * onehot, axis=-1))
    misfit = weighting * (looked - observed)
    return (misfit[..., None] * onehot).reshape(levels, row_count, col_count)

def reference(coarse_weights, perturbations, lat_matrix, lon_matrix, wind_field, observed_cell, observed_value, observed_weight):
    member_scale = 1.0 / jnp.sqrt(jnp.float32(MEMBERS - 1))
    lat_full = lat_matrix.astype(jnp.float32)
    lon_full = lon_matrix.astype(jnp.float32)
    by_member = jnp.transpose(coarse_weights, (1, 0, 2, 3))

    def member_term(running, inputs):
        coarse, member = inputs
        partly = jnp.einsum('rc,clw->lrw', lat_full, coarse.astype(jnp.float32), precision=highest)
        localized = jnp.einsum('lrw,wf->lrf', partly, lon_full, precision=highest)
        return (running + localized * member.astype(jnp.float32), None)
    summed, _ = lax.scan(member_term, jnp.zeros((LEV, FLAT, FLON), jnp.float32), (by_member, perturbations))
    increment = summed * member_scale
    margin_one = ((0, 0), (1, 1), (1, 1))
    wind_padded = jnp.pad(wind_field, margin_one)
    tangent = increment
    forcings = []
    for step_index in range(STEPS):
        tangent = advance(jnp.pad(tangent, margin_one), wind_field)
        forcings.append(observe(tangent, observed_cell[step_index], observed_value[step_index], observed_weight[step_index]))
    adjoint = jnp.zeros_like(increment)
    for step_index in reversed(range(STEPS)):
        adjoint = retreat(jnp.pad(adjoint + forcings[step_index], margin_one), wind_padded)

    def member_grad(unused, inputs):
        coarse, member = inputs
        product = member.astype(jnp.float32) * adjoint
        partly = jnp.einsum('lrf,wf->lrw', product, lon_full, precision=highest)
        gradient = jnp.einsum('rc,lrw->clw', lat_full, partly, precision=highest)
        return (unused, gradient * member_scale + coarse.astype(jnp.float32))
    _, grads = lax.scan(member_grad, jnp.float32(0.0), (by_member, perturbations))
    return (jnp.transpose(grads, (1, 0, 2, 3)), increment)
```

```python
import jax
import jax.numpy as jnp
from jax import lax
from jax.experimental import pallas as pl
from jax.experimental.pallas import tpu as pltpu
from jax.sharding import Mesh
from jax.sharding import PartitionSpec as P

STEPS = 4
OBLK = 8
HALO = 8
LAT = ("lat_0", "lat_1")
ALL = ("mem", "lat_0", "lat_1")

highest = lax.Precision.HIGHEST


def swapped(value, axis, dim):
    return lax.all_to_all(value, axis, split_axis=dim, concat_axis=dim, tiled=True)


def ring_blocks(block, axis):
    size = lax.axis_size(axis)
    up = [(i, (i + 1) % size) for i in range(size)]
    down = [(j, i) for i, j in up]
    blocks = {0: block}
    rising = falling = block
    for hop in range(1, size // 2 + 1):
        rising = lax.ppermute(rising, axis, up)
        blocks[(-hop) % size] = rising
        if hop < size - hop:
            falling = lax.ppermute(falling, axis, down)
            blocks[hop] = falling
    return blocks


def stencil_kernel(place_ref, own_ref, inner_ref, outer_ref, wind_ref, gain_ref, value_ref, adjoint_ref):
    rows, cols = wind_ref.shape[1:]
    half = place_ref[0]
    first_row = place_ref[1]
    last_row = place_ref[2]
    inner = inner_ref[...]
    outer = outer_ref[...]
    lower = half == 0
    state = jnp.concatenate(
        [jnp.where(lower, outer, inner), own_ref[...], jnp.where(lower, inner, outer)], axis=0
    )
    row = lax.broadcasted_iota(jnp.int32, (rows, cols), 0) + first_row
    col = lax.broadcasted_iota(jnp.int32, (rows, cols), 1)
    inside = ((row >= 0) & (row < last_row)).astype(jnp.float32)
    not_first = (col > 0).astype(jnp.float32)
    not_last = (col < cols - 1).astype(jnp.float32)
    lon_wind = 0.5 * wind_ref[0]
    lat_wind = 0.5 * wind_ref[1]

    def north(x):
        return pltpu.roll(x, rows - 1, 0)

    def south(x):
        return pltpu.roll(x, 1, 0)

    def east(x):
        return pltpu.roll(x, cols - 1, 1)

    def west(x):
        return pltpu.roll(x, 1, 1)

    from_north = (0.2 - lat_wind) * inside
    from_south = (0.2 + lat_wind) * inside
    from_east = (0.2 - lon_wind) * inside * not_last
    from_west = (0.2 + lon_wind) * inside * not_first
    centre = 0.2 * inside
    forcings = []
    for step in range(STEPS):
        state = (
            centre * state
            + from_north * north(state)
            + from_south * south(state)
            + from_east * east(state)
            + from_west * west(state)
        )
        forcings.append(gain_ref[step] * (state - value_ref[step]))
    to_south = 0.2 + lat_wind
    to_north = 0.2 - lat_wind
    to_west = (0.2 + lon_wind) * not_first
    to_east = (0.2 - lon_wind) * not_last
    adjoint = None
    for step in reversed(range(STEPS)):
        pushed = forcings[step] if adjoint is None else adjoint + forcings[step]
        adjoint = inside * (
            0.2 * pushed
            + north(to_south * pushed)
            + south(to_north * pushed)
            + east(to_west * pushed)
            + west(to_east * pushed)
        )
    adjoint_ref[...] = adjoint[HALO : rows - HALO]


def body(
    coarse_weights,
    perturbations,
    lat_matrix,
    lon_matrix,
    wind_field,
    observed_cell,
    observed_value,
    observed_weight,
):
    members_here, levels, row_count, lon_total = perturbations.shape
    coarse_rows, _, _, coarse_lons = coarse_weights.shape
    col_count = wind_field.shape[2]
    peers = lax.axis_size("mem")
    bands = lax.axis_size(LAT)
    rings = lax.axis_size("lat_0")
    pairs = members_here * levels
    halves = peers // levels
    own_rows = row_count // halves
    member_scale = 1.0 / jnp.sqrt(jnp.float32(members_here * peers - 1))
    lon_full = lon_matrix.astype(jnp.float32)
    half = lax.axis_index("mem") % halves
    band = lax.axis_index(LAT)
    lower = half == 0

    beside = [(m, m ^ 1) for m in range(peers)]
    beyond = []
    for m in range(peers):
        for b in range(bands):
            if m % 2 == 0 and b > 0:
                beyond.append((m * bands + b, (m + 1) * bands + b - 1))
            if m % 2 == 1 and b < bands - 1:
                beyond.append((m * bands + b, (m - 1) * bands + b + 1))

    other = lax.ppermute(coarse_weights, "lat_1", [(0, 1), (1, 0)])
    both = jnp.concatenate([coarse_weights, other], axis=0)
    blocks = ring_blocks(both, "lat_0")
    columns = lat_matrix.reshape(row_count, rings, 2, coarse_rows)
    columns = jnp.where(lax.axis_index("lat_1") == 0, columns, columns[:, :, ::-1])
    columns = columns.reshape(row_count, rings, 2 * coarse_rows)
    columns = lax.dynamic_slice_in_dim(
        jnp.concatenate([columns, columns], axis=1), lax.axis_index("lat_0"), rings, axis=1
    ).reshape(row_count, rings * 2 * coarse_rows)

    packed = jnp.concatenate(
        [observed_cell.astype(jnp.float32), observed_value, observed_weight], axis=0
    )
    kinds, _, _, block_count = packed.shape
    packed = jnp.transpose(packed, (1, 2, 0, 3)).reshape(levels, row_count, kinds * block_count)
    winds = jnp.transpose(wind_field, (1, 0, 2)).reshape(1, row_count, 2 * col_count)
    winds = jnp.broadcast_to(winds, (levels, row_count, 2 * col_count))
    filler = jnp.zeros((levels, row_count, 256 - kinds * block_count - 2 * col_count), jnp.float32)
    packed = jnp.concatenate([winds, packed, filler], axis=2)
    packed = jnp.broadcast_to(packed[:, None], (levels, halves, row_count, 256))
    packed = swapped(packed.reshape(peers, row_count, 256), "mem", 0)
    winds = packed[:, :, : 2 * col_count].reshape(peers, row_count, 2, col_count)
    winds = jnp.transpose(winds, (1, 2, 0, 3)).reshape(row_count, 2 * lon_total)
    sights = packed[:, :, 2 * col_count : 2 * col_count + kinds * block_count]
    sights = sights.reshape(peers, row_count, kinds, block_count)
    sights = jnp.transpose(sights, (1, 2, 0, 3)).reshape(row_count, kinds * peers * block_count)
    local = jnp.concatenate([winds, sights], axis=1)
    outgoing = jnp.where(lower, local[:HALO], local[-HALO:])
    margin = lax.ppermute(outgoing, ALL, beyond)
    local = jnp.where(
        lower,
        jnp.concatenate([margin, local[: row_count - HALO]], axis=0),
        jnp.concatenate([local[HALO:], margin], axis=0),
    )
    wide_rows = own_rows + 2 * HALO
    wide_wind = jnp.transpose(local[:, : 2 * lon_total].reshape(wide_rows, 2, lon_total), (1, 0, 2))
    sights = local[:, 2 * lon_total :].reshape(wide_rows, kinds, peers * block_count)
    sights = jnp.transpose(sights, (1, 0, 2))
    spread = jnp.arange(lon_total)[None, :] // OBLK == jnp.arange(lon_total // OBLK)[:, None]
    sights = jnp.einsum("krb,bf->krf", sights, spread.astype(jnp.float32), precision=highest)
    cells = sights[:STEPS]
    values = sights[STEPS : 2 * STEPS]
    offset = (jnp.arange(lon_total) % OBLK).astype(jnp.float32)
    gains = jnp.where(jnp.abs(cells - offset) < 0.5, sights[2 * STEPS :], 0.0)

    lat_all = lax.all_gather(lat_matrix, LAT, axis=0, tiled=True)

    order = [0] + [d for d in blocks if d != 0]
    gathered = jnp.concatenate([blocks[d] for d in order], axis=0)
    columns = columns.reshape(row_count, rings, 2 * coarse_rows)
    columns = jnp.concatenate([columns[:, d] for d in order], axis=1)
    narrow = jnp.einsum(
        "rc,cmlw->mlrw", columns, gathered, preferred_element_type=jnp.float32
    )
    localized = jnp.einsum("mlrw,wf->mlrf", narrow, lon_full, precision=highest)
    partial_sum = jnp.sum(localized * perturbations, axis=0)
    arrived = swapped(partial_sum.reshape(peers, own_rows, lon_total), "mem", 0)
    own = arrived.sum(axis=0) * member_scale

    inner = lax.ppermute(jnp.where(lower, own[-HALO:], own[:HALO]), "mem", beside)
    outer = lax.ppermute(jnp.where(lower, own[:HALO], own[-HALO:]), ALL, beyond)
    place = jnp.stack(
        [half, band * row_count + half * own_rows - HALO, jnp.int32(row_count * bands)]
    ).astype(jnp.int32)
    whole = pl.BlockSpec(memory_space=pltpu.VMEM)
    adjoint = pl.pallas_call(
        stencil_kernel,
        out_shape=jax.ShapeDtypeStruct((own_rows, lon_total), jnp.float32),
        in_specs=[pl.BlockSpec(memory_space=pltpu.SMEM)] + [whole] * 6,
        out_specs=whole,
        compiler_params=pltpu.CompilerParams(vmem_limit_bytes=32 * 1024 * 1024),
    )(place, own, inner, outer, wide_wind, gains, values)

    copies = jnp.broadcast_to(adjoint, (peers, own_rows, lon_total))
    adjoint_all = swapped(copies, "mem", 0).reshape(levels, row_count, lon_total)
    product = perturbations * adjoint_all[None]
    projected = jnp.einsum("mlrf,wf->mlrw", product, lon_full, precision=highest)
    by_pair = projected.reshape(bands, pairs // bands, row_count, coarse_lons)
    by_pair = swapped(by_pair, LAT, 0)
    full = jnp.einsum(
        "bqrw,brc->qcw",
        by_pair,
        lat_all.reshape(bands, row_count, bands * coarse_rows).astype(jnp.float32),
        precision=highest,
    )
    full = full.reshape(pairs // bands, bands, coarse_rows, coarse_lons)
    full = swapped(jnp.transpose(full, (1, 0, 2, 3)), LAT, 0)
    full = full.reshape(members_here, levels, coarse_rows, coarse_lons)
    full = jnp.transpose(full, (2, 0, 1, 3))
    gradient = full * member_scale + coarse_weights.astype(jnp.float32)

    tiles = jnp.transpose(own.reshape(own_rows, peers, col_count), (1, 0, 2))
    increment = swapped(tiles, "mem", 0).reshape(levels, row_count, col_count)
    return (gradient, increment)


def solution(mesh):
    split = Mesh(mesh.devices.reshape(mesh.shape["mem"], 8, 2), ("mem", "lat_0", "lat_1"))
    placed = (
        P(LAT, "mem", None, None),
        P("mem", None, LAT, None),
        P(LAT, None),
        P(),
        P(None, LAT, "mem"),
        P(None, None, LAT, "mem"),
        P(None, None, LAT, "mem"),
        P(None, None, LAT, "mem"),
    )
    return jax.shard_map(
        body,
        mesh=split,
        in_specs=placed,
        out_specs=(P(LAT, "mem", None, None), P(None, LAT, "mem")),
        check_vma=False,
    )
```

```python
import jax
import jax.numpy as jnp
from jax import lax
from jax.experimental import pallas as pl
from jax.experimental.pallas import tpu as pltpu
from jax.sharding import Mesh
from jax.sharding import PartitionSpec as P

STEPS = 4
OBLK = 8
HALO = 8
LAT = ("lat_0", "lat_1")
ALL = ("mem", "lat_0", "lat_1")

highest = lax.Precision.HIGHEST


def swapped(value, axis, dim):
    return lax.all_to_all(value, axis, split_axis=dim, concat_axis=dim, tiled=True)


def ring_blocks(block, axis):
    size = lax.axis_size(axis)
    up = [(i, (i + 1) % size) for i in range(size)]
    down = [(j, i) for i, j in up]
    blocks = {0: block}
    rising = falling = block
    for hop in range(1, size // 2 + 1):
        rising = lax.ppermute(rising, axis, up)
        blocks[(-hop) % size] = rising
        if hop < size - hop:
            falling = lax.ppermute(falling, axis, down)
            blocks[hop] = falling
    return blocks


def stencil_kernel(place_ref, own_ref, before_ref, after_ref, wind_ref, gain_ref, value_ref, adjoint_ref):
    rows, cols = wind_ref.shape[1:]
    first_row = place_ref[0]
    last_row = place_ref[1]
    state = jnp.concatenate([before_ref[...], own_ref[...], after_ref[...]], axis=0)
    row = lax.broadcasted_iota(jnp.int32, (rows, cols), 0) + first_row
    col = lax.broadcasted_iota(jnp.int32, (rows, cols), 1)
    inside = ((row >= 0) & (row < last_row)).astype(jnp.float32)
    not_first = (col > 0).astype(jnp.float32)
    not_last = (col < cols - 1).astype(jnp.float32)
    lon_wind = 0.5 * wind_ref[0]
    lat_wind = 0.5 * wind_ref[1]

    def north(x):
        return pltpu.roll(x, rows - 1, 0)

    def south(x):
        return pltpu.roll(x, 1, 0)

    def east(x):
        return pltpu.roll(x, cols - 1, 1)

    def west(x):
        return pltpu.roll(x, 1, 1)

    from_north = (0.2 - lat_wind) * inside
    from_south = (0.2 + lat_wind) * inside
    from_east = (0.2 - lon_wind) * inside * not_last
    from_west = (0.2 + lon_wind) * inside * not_first
    centre = 0.2 * inside
    forcings = []
    for step in range(STEPS):
        state = (
            centre * state
            + from_north * north(state)
            + from_south * south(state)
            + from_east * east(state)
            + from_west * west(state)
        )
        forcings.append(gain_ref[step] * (state - value_ref[step]))
    to_south = 0.2 + lat_wind
    to_north = 0.2 - lat_wind
    to_west = (0.2 + lon_wind) * not_first
    to_east = (0.2 - lon_wind) * not_last
    adjoint = None
    for step in reversed(range(STEPS)):
        pushed = forcings[step] if adjoint is None else adjoint + forcings[step]
        adjoint = inside * (
            0.2 * pushed
            + north(to_south * pushed)
            + south(to_north * pushed)
            + east(to_west * pushed)
            + west(to_east * pushed)
        )
    adjoint_ref[...] = adjoint[HALO : rows - HALO]


def body(
    coarse_weights,
    perturbations,
    lat_matrix,
    lon_matrix,
    wind_field,
    observed_cell,
    observed_value,
    observed_weight,
):
    members_here, levels, row_count, lon_total = perturbations.shape
    coarse_rows, _, _, coarse_lons = coarse_weights.shape
    col_count = wind_field.shape[2]
    peers = lax.axis_size("mem")
    rings = lax.axis_size("lat_0")
    sides = lax.axis_size("lat_1")
    bands = rings * sides
    levels_here = levels // sides
    wide_count = row_count * sides
    pairs = members_here * levels_here
    quarters = peers // levels_here
    own_rows = wide_count // quarters
    member_scale = 1.0 / jnp.sqrt(jnp.float32(members_here * peers - 1))
    lon_full = lon_matrix.astype(jnp.float32)
    quarter = lax.axis_index("mem") % quarters
    ring = lax.axis_index("lat_0")
    first = lax.axis_index("lat_1") == 0
    across = [(0, 1), (1, 0)]

    forward = []
    for m in range(peers):
        for z in range(rings):
            for x in range(sides):
                here = (m * rings + z) * sides + x
                if m % quarters < quarters - 1:
                    forward.append((here, here + bands))
                elif z < rings - 1:
                    forward.append((here, here - (quarters - 1) * bands + sides))
    backward = [(b, a) for a, b in forward]

    def halves(value, dim):
        low = lax.slice_in_dim(value, 0, levels_here, axis=dim)
        high = lax.slice_in_dim(value, levels_here, levels, axis=dim)
        return jnp.where(first, low, high), jnp.where(first, high, low)

    def in_order(mine, theirs, dim):
        return jnp.where(
            first, jnp.concatenate([mine, theirs], dim), jnp.concatenate([theirs, mine], dim)
        )

    mine, theirs = halves(coarse_weights, 2)
    lat_rows = jnp.concatenate([lat_matrix[: row_count // 2], lat_matrix[row_count // 2 :]], axis=1)

    def with_lat(value):
        value = value.reshape(coarse_rows, pairs, coarse_lons)
        return jnp.concatenate([value, lat_rows[None]], axis=0)[None]

    from_side = lax.ppermute(with_lat(theirs), "lat_1", across)
    both = in_order(with_lat(mine), from_side, 0)
    blocks = ring_blocks(both, "lat_0")

    def lat_of(block):
        rows = block[:, coarse_rows]
        rows = jnp.concatenate([rows[..., : bands * coarse_rows], rows[..., bands * coarse_rows :]], 1)
        return rows.reshape(1, wide_count, bands * coarse_rows)

    lat_ring = jnp.concatenate([lat_of(blocks[d]) for d in range(rings)], axis=0)
    lat_all = lax.dynamic_slice_in_dim(
        jnp.concatenate([lat_ring, lat_ring], axis=0), rings - ring, rings, axis=0
    )
    columns = lat_of(both)[0].reshape(wide_count, rings, sides * coarse_rows)
    columns = lax.dynamic_slice_in_dim(
        jnp.concatenate([columns, columns], axis=1), ring, rings, axis=1
    )

    mine, theirs = halves(perturbations, 1)
    members = in_order(mine, lax.ppermute(theirs, "lat_1", across), 2)

    packed = jnp.concatenate(
        [observed_cell.astype(jnp.float32), observed_value, observed_weight], axis=0
    )
    kinds, _, _, block_count = packed.shape
    lanes = 2 * col_count
    packed = jnp.transpose(packed, (1, 2, 0, 3)).reshape(levels, row_count, kinds * block_count)
    packed = jnp.pad(packed, ((0, 0), (0, 0), (0, lanes - kinds * block_count)))
    winds = jnp.transpose(wind_field, (1, 0, 2)).reshape(1, row_count, lanes)
    mine, theirs = halves(packed, 0)
    from_side = lax.ppermute(jnp.concatenate([theirs, winds], axis=0), "lat_1", across)
    packed = in_order(jnp.concatenate([mine, winds], axis=0), from_side, 1)
    packed = packed.reshape(levels_here + 1, quarters, own_rows, lanes)
    winds = jnp.broadcast_to(packed[levels_here:], (levels_here, quarters, own_rows, lanes))
    packed = jnp.stack([packed[:levels_here], winds], axis=2)
    packed = swapped(packed.reshape(peers, 2, own_rows, lanes), "mem", 0)
    winds = packed[:, 1].reshape(peers, own_rows, 2, col_count)
    winds = jnp.transpose(winds, (1, 2, 0, 3)).reshape(own_rows, 2 * lon_total)
    sights = packed[:, 0, :, : kinds * block_count].reshape(peers, own_rows, kinds, block_count)
    sights = jnp.transpose(sights, (1, 2, 0, 3)).reshape(own_rows, kinds * peers * block_count)
    local = jnp.concatenate([winds, sights], axis=1)
    before = lax.ppermute(local[-HALO:], ALL, forward)
    after = lax.ppermute(local[:HALO], ALL, backward)
    local = jnp.concatenate([before, local, after], axis=0)
    wide_rows = own_rows + 2 * HALO
    wide_wind = jnp.transpose(local[:, : 2 * lon_total].reshape(wide_rows, 2, lon_total), (1, 0, 2))
    sights = local[:, 2 * lon_total :].reshape(wide_rows, kinds, peers * block_count)
    sights = jnp.transpose(sights, (1, 0, 2))
    spread = jnp.arange(lon_total)[None, :] // OBLK == jnp.arange(lon_total // OBLK)[:, None]
    sights = jnp.einsum("krb,bf->krf", sights, spread.astype(jnp.float32), precision=highest)
    cells = sights[:STEPS]
    values = sights[STEPS : 2 * STEPS]
    offset = (jnp.arange(lon_total) % OBLK).astype(jnp.float32)
    gains = jnp.where(jnp.abs(cells - offset) < 0.5, sights[2 * STEPS :], 0.0)

    def narrowed(parts):
        chosen = jnp.concatenate([columns[:, d] for d in parts], axis=1)
        weights = jnp.concatenate(
            [blocks[d][:, :coarse_rows].reshape(-1, pairs, coarse_lons) for d in parts], axis=0
        )
        return jnp.einsum("rc,cpw->prw", chosen, weights, preferred_element_type=jnp.float32)

    narrow = narrowed(range(rings))
    localized = jnp.einsum("prw,wf->prf", narrow, lon_full, precision=highest)
    localized = localized.reshape(members_here, levels_here, wide_count, lon_total)
    partial_sum = jnp.sum(localized * members, axis=0)
    arrived = swapped(partial_sum.reshape(peers, own_rows, lon_total), "mem", 0)
    own = arrived.sum(axis=0) * member_scale

    before = lax.ppermute(own[-HALO:], ALL, forward)
    after = lax.ppermute(own[:HALO], ALL, backward)
    place = jnp.stack(
        [ring * wide_count + quarter * own_rows - HALO, jnp.int32(row_count * bands)]
    ).astype(jnp.int32)
    whole = pl.BlockSpec(memory_space=pltpu.VMEM)
    adjoint = pl.pallas_call(
        stencil_kernel,
        out_shape=jax.ShapeDtypeStruct((own_rows, lon_total), jnp.float32),
        in_specs=[pl.BlockSpec(memory_space=pltpu.SMEM)] + [whole] * 6,
        out_specs=whole,
        compiler_params=pltpu.CompilerParams(vmem_limit_bytes=32 * 1024 * 1024),
    )(place, own, before, after, wide_wind, gains, values)

    copies = jnp.broadcast_to(adjoint, (peers, own_rows, lon_total))
    adjoint_all = swapped(copies, "mem", 0).reshape(levels_here, wide_count, lon_total)
    product = members * adjoint_all[None]
    projected = jnp.einsum("mlrf,wf->mlrw", product, lon_full, precision=highest)
    by_pair = projected.reshape(rings, pairs // rings, wide_count, coarse_lons)
    by_pair = swapped(by_pair, "lat_0", 0)
    full = jnp.einsum(
        "zqrw,zrc->qcw", by_pair, lat_all.astype(jnp.float32), precision=highest
    )
    full = full.reshape(pairs // rings, bands, coarse_rows, coarse_lons)
    full = swapped(jnp.transpose(full, (1, 0, 2, 3)), LAT, 0)
    full = full.reshape(
        members_here, rings // members_here, sides, pairs // rings, coarse_rows, coarse_lons
    )
    full = jnp.transpose(full, (4, 0, 2, 1, 3, 5)).reshape(coarse_weights.shape)
    gradient = full * member_scale + coarse_weights.astype(jnp.float32)

    tiles = jnp.transpose(own.reshape(own_rows, peers, col_count), (1, 0, 2))
    tiles = swapped(tiles, "mem", 0).reshape(levels_here, sides, row_count, col_count)
    kept = jnp.where(first, tiles[:, 0], tiles[:, 1])
    sent = jnp.where(first, tiles[:, 1], tiles[:, 0])
    increment = in_order(kept, lax.ppermute(sent, "lat_1", across), 0)
    return (gradient, increment)


def solution(mesh):
    split = Mesh(mesh.devices.reshape(mesh.shape["mem"], 8, 2), ("mem", "lat_0", "lat_1"))
    placed = (
        P(LAT, "mem", None, None),
        P("mem", None, LAT, None),
        P(LAT, None),
        P(),
        P(None, LAT, "mem"),
        P(None, None, LAT, "mem"),
        P(None, None, LAT, "mem"),
        P(None, None, LAT, "mem"),
    )
    return jax.shard_map(
        body,
        mesh=split,
        in_specs=placed,
        out_specs=(P(LAT, "mem", None, None), P(None, LAT, "mem")),
        check_vma=False,
    )
```

```python
import jax
import jax.numpy as jnp
from jax import lax
from jax.experimental import pallas as pl
from jax.experimental.pallas import tpu as pltpu
from jax.sharding import Mesh
from jax.sharding import PartitionSpec as P

STEPS = 4
OBLK = 8
HALO = 8
LAT = ("lat_0", "lat_1")
ALL = ("mem", "lat_0", "lat_1")

highest = lax.Precision.HIGHEST


def swapped(value, axis, dim):
    return lax.all_to_all(value, axis, split_axis=dim, concat_axis=dim, tiled=True)


def two_terms(value):
    high = value.astype(jnp.bfloat16)
    low = (value - high.astype(jnp.float32)).astype(jnp.bfloat16)
    return jnp.concatenate([high, low], axis=0)


def dot(a, b):
    return jnp.dot(a, b, preferred_element_type=jnp.float32)


def member_rows(side, own_ref, other_ref, member, level):
    levels_here = other_ref.shape[1]
    own = own_ref[member, side * levels_here + level].astype(jnp.float32)
    other = other_ref[member, level].astype(jnp.float32)
    low = jnp.where(side == 0, own, other)
    high = jnp.where(side == 0, other, own)
    return jnp.concatenate([low, high], axis=0)


def localize_kernel(side_ref, columns_ref, lon_ref, own_ref, other_ref, *refs):
    block_refs, sum_ref = refs[:-1], refs[-1]
    members, levels_here, row_count, lon_total = other_ref.shape
    tall = 2 * row_count
    side = side_ref[0]
    per_block = columns_ref.shape[1] // len(block_refs)
    columns = columns_ref[...]
    lon = lon_ref[...]
    for level in range(levels_here):
        narrow = []
        for member in range(members):
            start = (member * levels_here + level) * per_block
            weights = jnp.concatenate([ref[start : start + per_block] for ref in block_refs], axis=0)
            narrow.append(dot(columns, weights))
        localized = dot(two_terms(jnp.concatenate(narrow, axis=0)), lon)
        total = None
        for member in range(members):
            at = member * tall
            term = localized[at : at + tall] + localized[at + members * tall : at + (members + 1) * tall]
            term = term * member_rows(side, own_ref, other_ref, member, level)
            total = term if total is None else total + term
        count = sum_ref.shape[0] // levels_here
        sum_ref[level * count : (level + 1) * count] = total.reshape(count, tall // count, lon_total)


def project_kernel(side_ref, adjoint_ref, lon_ref, own_ref, other_ref, out_ref):
    members, levels_here, row_count, lon_total = other_ref.shape
    tall = 2 * row_count
    side = side_ref[0]
    lon = lon_ref[...]
    count = adjoint_ref.shape[0] // levels_here
    for level in range(levels_here):
        adjoint = adjoint_ref[level * count : (level + 1) * count].reshape(tall, lon_total)
        product = [
            member_rows(side, own_ref, other_ref, member, level) * adjoint for member in range(members)
        ]
        projected = dot(two_terms(jnp.concatenate(product, axis=0)), lon)
        for member in range(members):
            at = member * tall
            out_ref[member * levels_here + level] = (
                projected[at : at + tall] + projected[at + members * tall : at + (members + 1) * tall]
            )


def stencil_kernel(place_ref, own_ref, before_ref, after_ref, wind_ref, gain_ref, value_ref, adjoint_ref):
    rows, cols = wind_ref.shape[1:]
    first_row = place_ref[0]
    last_row = place_ref[1]
    state = jnp.concatenate([before_ref[...], own_ref[...], after_ref[...]], axis=0)
    row = lax.broadcasted_iota(jnp.int32, (rows, cols), 0) + first_row
    col = lax.broadcasted_iota(jnp.int32, (rows, cols), 1)
    inside = ((row >= 0) & (row < last_row)).astype(jnp.float32)
    not_first = (col > 0).astype(jnp.float32)
    not_last = (col < cols - 1).astype(jnp.float32)
    lon_wind = 0.5 * wind_ref[0]
    lat_wind = 0.5 * wind_ref[1]

    def north(x):
        return pltpu.roll(x, rows - 1, 0)

    def south(x):
        return pltpu.roll(x, 1, 0)

    def east(x):
        return pltpu.roll(x, cols - 1, 1)

    def west(x):
        return pltpu.roll(x, 1, 1)

    from_north = (0.2 - lat_wind) * inside
    from_south = (0.2 + lat_wind) * inside
    from_east = (0.2 - lon_wind) * inside * not_last
    from_west = (0.2 + lon_wind) * inside * not_first
    centre = 0.2 * inside
    forcings = []
    for step in range(STEPS):
        state = (
            centre * state
            + from_north * north(state)
            + from_south * south(state)
            + from_east * east(state)
            + from_west * west(state)
        )
        forcings.append(gain_ref[step] * (state - value_ref[step]))
    to_south = 0.2 + lat_wind
    to_north = 0.2 - lat_wind
    to_west = (0.2 + lon_wind) * not_first
    to_east = (0.2 - lon_wind) * not_last
    adjoint = None
    for step in reversed(range(STEPS)):
        pushed = forcings[step] if adjoint is None else adjoint + forcings[step]
        adjoint = inside * (
            0.2 * pushed
            + north(to_south * pushed)
            + south(to_north * pushed)
            + east(to_west * pushed)
            + west(to_east * pushed)
        )
    adjoint = adjoint[HALO : rows - HALO]
    for copy in range(adjoint_ref.shape[0]):
        adjoint_ref[copy] = adjoint


def body(
    coarse_weights,
    perturbations,
    lat_matrix,
    lon_matrix,
    wind_field,
    observed_cell,
    observed_value,
    observed_weight,
):
    members_here, levels, row_count, lon_total = perturbations.shape
    coarse_rows, _, _, coarse_lons = coarse_weights.shape
    col_count = wind_field.shape[2]
    peers = lax.axis_size("mem")
    rings = lax.axis_size("lat_0")
    sides = lax.axis_size("lat_1")
    bands = rings * sides
    levels_here = levels // sides
    wide_count = row_count * sides
    pairs = members_here * levels_here
    quarters = peers // levels_here
    own_rows = wide_count // quarters
    member_scale = 1.0 / jnp.sqrt(jnp.float32(members_here * peers - 1))
    quarter = lax.axis_index("mem") % quarters
    ring = lax.axis_index("lat_0")
    first = lax.axis_index("lat_1") == 0
    across = [(0, 1), (1, 0)]

    forward = []
    for m in range(peers):
        for z in range(rings):
            for x in range(sides):
                here = (m * rings + z) * sides + x
                if m % quarters < quarters - 1:
                    forward.append((here, here + bands))
                elif z < rings - 1:
                    forward.append((here, here - (quarters - 1) * bands + sides))
    backward = [(b, a) for a, b in forward]

    def halves(value, dim):
        low = lax.slice_in_dim(value, 0, levels_here, axis=dim)
        high = lax.slice_in_dim(value, levels_here, levels, axis=dim)
        return jnp.where(first, low, high), jnp.where(first, high, low)

    def in_order(mine, theirs, dim):
        return jnp.where(
            first, jnp.concatenate([mine, theirs], dim), jnp.concatenate([theirs, mine], dim)
        )

    weight_rows = pairs * coarse_rows
    coarse_total = bands * coarse_rows
    mine, theirs = halves(coarse_weights, 2)
    lat_rows = jnp.concatenate([lat_matrix[: row_count // 2], lat_matrix[row_count // 2 :]], axis=1)

    def by_pair_first(value):
        value = value.reshape(coarse_rows, pairs, coarse_lons)
        return jnp.transpose(value, (1, 0, 2))

    theirs = by_pair_first(theirs).reshape(weight_rows, coarse_lons)
    from_side = lax.ppermute(jnp.concatenate([theirs, lat_rows], axis=0), "lat_1", across)
    both = in_order(
        by_pair_first(mine), from_side[:weight_rows].reshape(pairs, coarse_rows, coarse_lons), 1
    ).reshape(sides * weight_rows, coarse_lons)
    both = jnp.concatenate([both, in_order(lat_rows, from_side[weight_rows:], 0)], axis=0)

    packed = jnp.concatenate(
        [observed_cell.astype(jnp.float32), observed_value, observed_weight], axis=0
    )
    kinds, _, _, block_count = packed.shape
    lanes = 2 * col_count
    packed = jnp.transpose(packed, (1, 2, 0, 3)).reshape(levels, row_count, kinds * block_count)
    packed = jnp.pad(packed, ((0, 0), (0, 0), (0, lanes - kinds * block_count)))
    winds = jnp.transpose(wind_field, (1, 0, 2)).reshape(1, row_count, lanes)
    mine_seen, theirs_seen = halves(packed, 0)
    mine_seen = jnp.concatenate([mine_seen, winds], axis=0)
    theirs_seen = lax.ppermute(jnp.concatenate([theirs_seen, winds], axis=0), "lat_1", across)

    side = lax.axis_index("lat_1")
    up = [(i, (i + 1) % rings) for i in range(rings)]
    down = [(b, a) for a, b in up]
    blocks = {0: both}
    rising = falling = both
    for hop in range(1, rings // 2 + 1):
        rising = lax.ppermute(rising, "lat_0", up)
        if hop < rings - hop:
            falling = lax.ppermute(falling, "lat_0", down)
        if hop == 1:
            rising, falling, perturbed = lax.optimization_barrier((rising, falling, perturbations))
            other_members = lax.dynamic_slice_in_dim(
                perturbed, (1 - side) * levels_here, levels_here, axis=1
            )
            other_members = lax.ppermute(other_members, "lat_1", across)
        if hop == 2:
            rising, falling, mine_seen, theirs_seen = lax.optimization_barrier(
                (rising, falling, mine_seen, theirs_seen)
            )
            packed = in_order(mine_seen, theirs_seen, 1)
            packed = packed.reshape(levels_here + 1, quarters, own_rows, lanes)
            winds = jnp.broadcast_to(packed[levels_here:], (levels_here, quarters, own_rows, lanes))
            packed = jnp.stack([packed[:levels_here], winds], axis=2)
            packed = swapped(packed.reshape(peers, 2, own_rows, lanes), "mem", 0)
        blocks[-hop % rings] = rising
        if hop < rings - hop:
            blocks[hop] = falling
    last, packed = lax.optimization_barrier((blocks[rings // 2], packed))
    blocks[rings // 2] = last

    def lat_of(block):
        rows = block[sides * weight_rows :].reshape(sides, row_count // 2, coarse_lons)
        rows = jnp.concatenate([rows[..., :coarse_total], rows[..., coarse_total:]], 1)
        return rows.reshape(1, wide_count, coarse_total)

    lat_ring = jnp.concatenate([lat_of(blocks[d]) for d in range(rings)], axis=0)
    lat_all = lax.dynamic_slice_in_dim(
        jnp.concatenate([lat_ring, lat_ring], axis=0), rings - ring, rings, axis=0
    )
    columns = lat_of(both)[0].reshape(wide_count, rings, sides * coarse_rows)
    columns = lax.dynamic_slice_in_dim(
        jnp.concatenate([columns, columns], axis=1), ring, rings, axis=1
    ).reshape(wide_count, coarse_total)

    winds = packed[:, 1].reshape(peers, own_rows, 2, col_count)
    winds = jnp.transpose(winds, (1, 2, 0, 3)).reshape(own_rows, 2 * lon_total)
    sights = packed[:, 0, :, : kinds * block_count].reshape(peers, own_rows, kinds, block_count)
    sights = jnp.transpose(sights, (1, 2, 0, 3)).reshape(own_rows, kinds * peers * block_count)
    local = jnp.concatenate([winds, sights], axis=1)
    before = lax.ppermute(local[-HALO:], ALL, forward)
    after = lax.ppermute(local[:HALO], ALL, backward)
    local = jnp.concatenate([before, local, after], axis=0)
    wide_rows = own_rows + 2 * HALO
    wide_wind = jnp.transpose(local[:, : 2 * lon_total].reshape(wide_rows, 2, lon_total), (1, 0, 2))
    sights = local[:, 2 * lon_total :].reshape(wide_rows, kinds, peers * block_count)
    sights = jnp.transpose(sights, (1, 0, 2))
    spread = jnp.arange(lon_total)[None, :] // OBLK == jnp.arange(lon_total // OBLK)[:, None]
    sights = jnp.einsum("krb,bf->krf", sights, spread.astype(jnp.float32), precision=highest)
    cells = sights[:STEPS]
    values = sights[STEPS : 2 * STEPS]
    offset = (jnp.arange(lon_total) % OBLK).astype(jnp.float32)
    gains = jnp.where(jnp.abs(cells - offset) < 0.5, sights[2 * STEPS :], 0.0)

    scalars = pl.BlockSpec(memory_space=pltpu.SMEM)
    whole = pl.BlockSpec(memory_space=pltpu.VMEM)
    roomy = pltpu.CompilerParams(vmem_limit_bytes=48 * 1024 * 1024)
    where_side = jnp.reshape(side, (1,)).astype(jnp.int32)
    partial_sum = pl.pallas_call(
        localize_kernel,
        out_shape=jax.ShapeDtypeStruct((peers, own_rows, lon_total), jnp.float32),
        in_specs=[scalars] + [whole] * (4 + rings),
        out_specs=whole,
        compiler_params=roomy,
    )(
        where_side,
        columns,
        lon_matrix,
        perturbations,
        other_members,
        *[blocks[d] for d in range(rings)],
    )
    arrived = swapped(partial_sum, "mem", 0)
    own = arrived.sum(axis=0) * member_scale

    before = lax.ppermute(own[-HALO:], ALL, forward)
    after = lax.ppermute(own[:HALO], ALL, backward)
    place = jnp.stack(
        [ring * wide_count + quarter * own_rows - HALO, jnp.int32(row_count * bands)]
    ).astype(jnp.int32)
    copies = pl.pallas_call(
        stencil_kernel,
        out_shape=jax.ShapeDtypeStruct((peers, own_rows, lon_total), jnp.float32),
        in_specs=[scalars] + [whole] * 6,
        out_specs=whole,
        compiler_params=roomy,
    )(place, own, before, after, wide_wind, gains, values)

    adjoint_all = swapped(copies, "mem", 0)
    projected = pl.pallas_call(
        project_kernel,
        out_shape=jax.ShapeDtypeStruct((pairs, wide_count, coarse_lons), jnp.float32),
        in_specs=[scalars] + [whole] * 4,
        out_specs=whole,
        compiler_params=roomy,
    )(where_side, adjoint_all, jnp.transpose(lon_matrix), perturbations, other_members)
    by_pair = projected.reshape(rings, pairs // rings, wide_count, coarse_lons)
    by_pair = swapped(by_pair, "lat_0", 0)
    full = jnp.einsum(
        "zqrw,zrc->qcw", by_pair, lat_all.astype(jnp.float32), precision=highest
    )
    full = full.reshape(pairs // rings, bands, coarse_rows, coarse_lons)
    full = swapped(jnp.transpose(full, (1, 0, 2, 3)), LAT, 0)
    full = full.reshape(
        members_here, rings // members_here, sides, pairs // rings, coarse_rows, coarse_lons
    )
    full = jnp.transpose(full, (4, 0, 2, 1, 3, 5)).reshape(coarse_weights.shape)
    gradient = full * member_scale + coarse_weights.astype(jnp.float32)

    tiles = jnp.transpose(own.reshape(own_rows, peers, col_count), (1, 0, 2))
    tiles = swapped(tiles, "mem", 0).reshape(levels_here, sides, row_count, col_count)
    kept = jnp.where(first, tiles[:, 0], tiles[:, 1])
    sent = jnp.where(first, tiles[:, 1], tiles[:, 0])
    increment = in_order(kept, lax.ppermute(sent, "lat_1", across), 0)
    return (gradient, increment)


def solution(mesh):
    split = Mesh(mesh.devices.reshape(mesh.shape["mem"], 8, 2), ("mem", "lat_0", "lat_1"))
    placed = (
        P(LAT, "mem", None, None),
        P("mem", None, LAT, None),
        P(LAT, None),
        P(),
        P(None, LAT, "mem"),
        P(None, None, LAT, "mem"),
        P(None, None, LAT, "mem"),
        P(None, None, LAT, "mem"),
    )
    return jax.shard_map(
        body,
        mesh=split,
        in_specs=placed,
        out_specs=(P(LAT, "mem", None, None), P(None, LAT, "mem")),
        check_vma=False,
    )
```

```python
import jax
import jax.numpy as jnp
from jax import lax
from jax.experimental import pallas as pl
from jax.experimental.pallas import tpu as pltpu
from jax.sharding import Mesh
from jax.sharding import PartitionSpec as P

STEPS = 4
OBLK = 8
HALO = 8
LAT = ("lat_0", "lat_1")
ALL = ("mem", "lat_0", "lat_1")

highest = lax.Precision.HIGHEST


def swapped(value, axis, dim):
    return lax.all_to_all(value, axis, split_axis=dim, concat_axis=dim, tiled=True)


def two_terms(value):
    high = value.astype(jnp.bfloat16)
    low = (value - high.astype(jnp.float32)).astype(jnp.bfloat16)
    return jnp.concatenate([high, low], axis=0)


def dot(a, b):
    return jnp.dot(a, b, preferred_element_type=jnp.float32)


def member_rows(side, own_ref, other_ref, member, level):
    levels_here = other_ref.shape[1]
    own = own_ref[member, side * levels_here + level].astype(jnp.float32)
    other = other_ref[member, level].astype(jnp.float32)
    low = jnp.where(side == 0, own, other)
    high = jnp.where(side == 0, other, own)
    return jnp.concatenate([low, high], axis=0)


def localize_kernel(side_ref, columns_ref, lon_ref, own_ref, other_ref, *refs):
    block_refs, sum_ref = refs[:-1], refs[-1]
    members, levels_here, row_count, lon_total = other_ref.shape
    tall = 2 * row_count
    side = side_ref[0]
    per_block = columns_ref.shape[1] // len(block_refs)
    columns = columns_ref[...]
    lon = lon_ref[...]
    for level in range(levels_here):
        narrow = []
        for member in range(members):
            start = (member * levels_here + level) * per_block
            weights = jnp.concatenate([ref[start : start + per_block] for ref in block_refs], axis=0)
            narrow.append(dot(columns, weights))
        localized = dot(two_terms(jnp.concatenate(narrow, axis=0)), lon)
        total = None
        for member in range(members):
            at = member * tall
            term = localized[at : at + tall] + localized[at + members * tall : at + (members + 1) * tall]
            term = term * member_rows(side, own_ref, other_ref, member, level)
            total = term if total is None else total + term
        count = sum_ref.shape[0] // levels_here
        sum_ref[level * count : (level + 1) * count] = total.reshape(count, tall // count, lon_total)


def project_kernel(side_ref, adjoint_ref, lon_ref, own_ref, other_ref, out_ref):
    members, levels_here, row_count, lon_total = other_ref.shape
    tall = 2 * row_count
    side = side_ref[0]
    lon = lon_ref[...]
    count = adjoint_ref.shape[0] // levels_here
    for level in range(levels_here):
        adjoint = adjoint_ref[level * count : (level + 1) * count].reshape(tall, lon_total)
        product = [
            member_rows(side, own_ref, other_ref, member, level) * adjoint for member in range(members)
        ]
        projected = dot(two_terms(jnp.concatenate(product, axis=0)), lon)
        for member in range(members):
            at = member * tall
            out_ref[member * levels_here + level] = (
                projected[at : at + tall] + projected[at + members * tall : at + (members + 1) * tall]
            )


def arrange_kernel(side_ref, own_ref, other_ref, out_ref):
    peers, _, row_count, lanes = own_ref.shape
    side = side_ref[0]
    is_own = side_ref[1] == 1
    lane = lax.broadcasted_iota(jnp.int32, (row_count, lanes), 1)
    width = lanes // 2
    pick = lambda peer, which, mine: jnp.where(is_own, own_ref[peer, mine], other_ref[peer, which])
    winds = [pick(peer, 1, 2) for peer in range(peers)]
    seen = [pick(peer, 0, side) for peer in range(peers)]
    lon_total = peers * width
    for at in range(peers // 2):
        even, odd = winds[2 * at], winds[2 * at + 1]
        spot = slice(at * lanes, (at + 1) * lanes)
        out_ref[:, spot] = jnp.where(lane < width, even, pltpu.roll(odd, width, 1))
        spot = slice(lon_total + at * lanes, lon_total + (at + 1) * lanes)
        out_ref[:, spot] = jnp.where(lane < width, pltpu.roll(even, width, 1), odd)
    blocks = lanes // peers
    kinds = (out_ref.shape[1] - 2 * lon_total) // lanes
    owner = lane // blocks
    for kind in range(kinds):
        total = jnp.zeros((row_count, lanes), jnp.float32)
        for peer in range(peers):
            shift = (peer - kind) * blocks % lanes
            value = seen[peer] if shift == 0 else pltpu.roll(seen[peer], shift, 1)
            total = jnp.where(owner == peer, value, total)
        spot = slice(2 * lon_total + kind * lanes, 2 * lon_total + (kind + 1) * lanes)
        out_ref[:, spot] = total


def spread_kernel(before_ref, local_ref, after_ref, wind_ref, gain_ref, value_ref):
    _, rows, cols = wind_ref.shape
    lanes = cols // OBLK
    local = jnp.concatenate([before_ref[...], local_ref[...], after_ref[...]], axis=0)
    wind_ref[0] = local[:, :cols]
    wind_ref[1] = local[:, cols : 2 * cols]
    sights = [local[:, 2 * cols + k * lanes : 2 * cols + (k + 1) * lanes] for k in range(3 * STEPS)]
    cells = jnp.concatenate(sights[:STEPS], axis=0).astype(jnp.bfloat16)
    others = jnp.concatenate(sights[STEPS:], axis=0)
    high = others.astype(jnp.bfloat16)
    rest = others - high.astype(jnp.float32)
    middle = rest.astype(jnp.bfloat16)
    low = (rest - middle.astype(jnp.float32)).astype(jnp.bfloat16)
    block = lax.broadcasted_iota(jnp.int32, (lanes, cols), 0)
    spread = (lax.broadcasted_iota(jnp.int32, (lanes, cols), 1) // OBLK == block).astype(jnp.bfloat16)
    cells = dot(cells, spread)
    wide = dot(high, spread) + (dot(middle, spread) + dot(low, spread))
    offset = lax.broadcasted_iota(jnp.int32, (rows, cols), 1) % OBLK
    offset = offset.astype(jnp.float32)
    for step in range(STEPS):
        value_ref[step] = wide[step * rows : (step + 1) * rows]
        hit = jnp.abs(cells[step * rows : (step + 1) * rows] - offset) < 0.5
        weight = wide[(STEPS + step) * rows : (STEPS + step + 1) * rows]
        gain_ref[step] = jnp.where(hit, weight, 0.0)


def stencil_kernel(place_ref, own_ref, before_ref, after_ref, wind_ref, gain_ref, value_ref, adjoint_ref):
    rows, cols = wind_ref.shape[1:]
    first_row = place_ref[0]
    last_row = place_ref[1]
    state = jnp.concatenate([before_ref[...], own_ref[...], after_ref[...]], axis=0)
    row = lax.broadcasted_iota(jnp.int32, (rows, cols), 0) + first_row
    col = lax.broadcasted_iota(jnp.int32, (rows, cols), 1)
    inside = ((row >= 0) & (row < last_row)).astype(jnp.float32)
    not_first = (col > 0).astype(jnp.float32)
    not_last = (col < cols - 1).astype(jnp.float32)
    lon_wind = 0.5 * wind_ref[0]
    lat_wind = 0.5 * wind_ref[1]

    def north(x):
        return pltpu.roll(x, rows - 1, 0)

    def south(x):
        return pltpu.roll(x, 1, 0)

    def east(x):
        return pltpu.roll(x, cols - 1, 1)

    def west(x):
        return pltpu.roll(x, 1, 1)

    from_north = (0.2 - lat_wind) * inside
    from_south = (0.2 + lat_wind) * inside
    from_east = (0.2 - lon_wind) * inside * not_last
    from_west = (0.2 + lon_wind) * inside * not_first
    centre = 0.2 * inside
    forcings = []
    for step in range(STEPS):
        state = (
            centre * state
            + from_north * north(state)
            + from_south * south(state)
            + from_east * east(state)
            + from_west * west(state)
        )
        forcings.append(gain_ref[step] * (state - value_ref[step]))
    to_south = 0.2 + lat_wind
    to_north = 0.2 - lat_wind
    to_west = (0.2 + lon_wind) * not_first
    to_east = (0.2 - lon_wind) * not_last
    adjoint = None
    for step in reversed(range(STEPS)):
        pushed = forcings[step] if adjoint is None else adjoint + forcings[step]
        adjoint = inside * (
            0.2 * pushed
            + north(to_south * pushed)
            + south(to_north * pushed)
            + east(to_west * pushed)
            + west(to_east * pushed)
        )
    adjoint = adjoint[HALO : rows - HALO]
    for copy in range(adjoint_ref.shape[0]):
        adjoint_ref[copy] = adjoint


def body(
    coarse_weights,
    perturbations,
    lat_matrix,
    lon_matrix,
    wind_field,
    observed_cell,
    observed_value,
    observed_weight,
):
    members_here, levels, row_count, lon_total = perturbations.shape
    coarse_rows, _, _, coarse_lons = coarse_weights.shape
    col_count = wind_field.shape[2]
    peers = lax.axis_size("mem")
    rings = lax.axis_size("lat_0")
    sides = lax.axis_size("lat_1")
    bands = rings * sides
    levels_here = levels // sides
    wide_count = row_count * sides
    pairs = members_here * levels_here
    quarters = peers // levels_here
    own_rows = wide_count // quarters
    member_scale = 1.0 / jnp.sqrt(jnp.float32(members_here * peers - 1))
    quarter = lax.axis_index("mem") % quarters
    ring = lax.axis_index("lat_0")
    first = lax.axis_index("lat_1") == 0
    across = [(0, 1), (1, 0)]

    forward = []
    for m in range(peers):
        for z in range(rings):
            for x in range(sides):
                here = (m * rings + z) * sides + x
                if m % quarters < quarters - 1:
                    forward.append((here, here + bands))
                elif z < rings - 1:
                    forward.append((here, here - (quarters - 1) * bands + sides))
    backward = [(b, a) for a, b in forward]

    def halves(value, dim):
        low = lax.slice_in_dim(value, 0, levels_here, axis=dim)
        high = lax.slice_in_dim(value, levels_here, levels, axis=dim)
        return jnp.where(first, low, high), jnp.where(first, high, low)

    def in_order(mine, theirs, dim):
        return jnp.where(
            first, jnp.concatenate([mine, theirs], dim), jnp.concatenate([theirs, mine], dim)
        )

    weight_rows = pairs * coarse_rows
    coarse_total = bands * coarse_rows
    mine, theirs = halves(coarse_weights, 2)
    lat_rows = jnp.concatenate([lat_matrix[: row_count // 2], lat_matrix[row_count // 2 :]], axis=1)

    def by_pair_first(value):
        value = value.reshape(coarse_rows, pairs, coarse_lons)
        return jnp.transpose(value, (1, 0, 2))

    theirs = by_pair_first(theirs).reshape(weight_rows, coarse_lons)
    from_side = lax.ppermute(jnp.concatenate([theirs, lat_rows], axis=0), "lat_1", across)
    both = in_order(
        by_pair_first(mine), from_side[:weight_rows].reshape(pairs, coarse_rows, coarse_lons), 1
    ).reshape(sides * weight_rows, coarse_lons)
    both = jnp.concatenate([both, in_order(lat_rows, from_side[weight_rows:], 0)], axis=0)

    packed = jnp.concatenate(
        [observed_cell.astype(jnp.float32), observed_value, observed_weight], axis=0
    )
    kinds, _, _, block_count = packed.shape
    lanes = 2 * col_count
    packed = jnp.transpose(packed, (1, 2, 0, 3)).reshape(levels, row_count, kinds * block_count)
    packed = jnp.pad(packed, ((0, 0), (0, 0), (0, lanes - kinds * block_count)))
    winds = jnp.transpose(wind_field, (1, 0, 2)).reshape(1, row_count, lanes)
    parts = row_count // own_rows
    packed = packed.reshape(sides, levels_here, 1, parts, own_rows, lanes)
    winds = jnp.broadcast_to(
        winds.reshape(1, 1, 1, parts, own_rows, lanes), (1, levels_here, 1, parts, own_rows, lanes)
    )
    packed = jnp.transpose(jnp.concatenate([packed, winds], axis=0), (1, 2, 3, 0, 4, 5))
    packed = jnp.broadcast_to(
        packed, (levels_here, quarters // parts, parts, sides + 1, own_rows, lanes)
    )
    packed = swapped(packed.reshape(peers, sides + 1, own_rows, lanes), "mem", 0)

    side = lax.axis_index("lat_1")
    up = [(i, (i + 1) % rings) for i in range(rings)]
    down = [(b, a) for a, b in up]
    blocks = {0: both}
    rising = falling = both
    for hop in range(1, rings // 2 + 1):
        rising = lax.ppermute(rising, "lat_0", up)
        if hop < rings - hop:
            falling = lax.ppermute(falling, "lat_0", down)
        if hop == 1:
            rising, falling, perturbed = lax.optimization_barrier((rising, falling, perturbations))
            other_members = lax.dynamic_slice_in_dim(
                perturbed, (1 - side) * levels_here, levels_here, axis=1
            )
            other_members = lax.ppermute(other_members, "lat_1", across)
        if hop == 2:
            rising, falling, packed = lax.optimization_barrier((rising, falling, packed))
            passed = jnp.where(first, packed[:, 1:], jnp.stack([packed[:, 0], packed[:, 2]], axis=1))
            passed = lax.ppermute(passed, "lat_1", across)
        blocks[-hop % rings] = rising
        if hop < rings - hop:
            blocks[hop] = falling

    def lat_of(block):
        rows = block[sides * weight_rows :].reshape(sides, row_count // 2, coarse_lons)
        rows = jnp.concatenate([rows[..., :coarse_total], rows[..., coarse_total:]], 1)
        return rows.reshape(1, wide_count, coarse_total)

    lat_ring = jnp.concatenate([lat_of(blocks[d]) for d in range(rings)], axis=0)
    lat_all = lax.dynamic_slice_in_dim(
        jnp.concatenate([lat_ring, lat_ring], axis=0), rings - ring, rings, axis=0
    )
    columns = lat_of(both)[0].reshape(wide_count, rings, sides * coarse_rows)
    columns = lax.dynamic_slice_in_dim(
        jnp.concatenate([columns, columns], axis=1), ring, rings, axis=1
    ).reshape(wide_count, coarse_total)

    scalars = pl.BlockSpec(memory_space=pltpu.SMEM)
    whole = pl.BlockSpec(memory_space=pltpu.VMEM)
    roomy = pltpu.CompilerParams(vmem_limit_bytes=48 * 1024 * 1024)
    where_side = jnp.reshape(side, (1,)).astype(jnp.int32)
    partial_sum = pl.pallas_call(
        localize_kernel,
        out_shape=jax.ShapeDtypeStruct((peers, own_rows, lon_total), jnp.float32),
        in_specs=[scalars] + [whole] * (4 + rings),
        out_specs=whole,
        compiler_params=roomy,
    )(
        where_side,
        columns,
        lon_matrix,
        perturbations,
        other_members,
        *[blocks[d] for d in range(rings)],
    )
    partial_sum, packed, passed = lax.optimization_barrier((partial_sum, packed, passed))
    arrived = swapped(partial_sum, "mem", 0)

    is_own = (quarter // parts == side).astype(jnp.int32)
    local = pl.pallas_call(
        arrange_kernel,
        out_shape=jax.ShapeDtypeStruct(
            (own_rows, 2 * lon_total + kinds * peers * block_count), jnp.float32
        ),
        in_specs=[scalars, whole, whole],
        out_specs=whole,
        compiler_params=roomy,
    )(jnp.stack([side.astype(jnp.int32), is_own]), packed, passed)
    before = lax.ppermute(local[-HALO:], ALL, forward)
    after = lax.ppermute(local[:HALO], ALL, backward)
    wide_rows = own_rows + 2 * HALO
    wide_wind, gains, values = pl.pallas_call(
        spread_kernel,
        out_shape=[
            jax.ShapeDtypeStruct((count, wide_rows, lon_total), jnp.float32)
            for count in (2, STEPS, STEPS)
        ],
        in_specs=[whole] * 3,
        out_specs=[whole] * 3,
        compiler_params=roomy,
    )(before, local, after)

    own = arrived.sum(axis=0) * member_scale

    before = lax.ppermute(own[-HALO:], ALL, forward)
    after = lax.ppermute(own[:HALO], ALL, backward)
    place = jnp.stack(
        [ring * wide_count + quarter * own_rows - HALO, jnp.int32(row_count * bands)]
    ).astype(jnp.int32)
    copies = pl.pallas_call(
        stencil_kernel,
        out_shape=jax.ShapeDtypeStruct((peers, own_rows, lon_total), jnp.float32),
        in_specs=[scalars] + [whole] * 6,
        out_specs=whole,
        compiler_params=roomy,
    )(place, own, before, after, wide_wind, gains, values)

    adjoint_all = swapped(copies, "mem", 0)
    projected = pl.pallas_call(
        project_kernel,
        out_shape=jax.ShapeDtypeStruct((pairs, wide_count, coarse_lons), jnp.float32),
        in_specs=[scalars] + [whole] * 4,
        out_specs=whole,
        compiler_params=roomy,
    )(where_side, adjoint_all, jnp.transpose(lon_matrix), perturbations, other_members)
    projected, own = lax.optimization_barrier((projected, own))
    by_pair = projected.reshape(rings, pairs // rings, wide_count, coarse_lons)
    by_pair = swapped(by_pair, "lat_0", 0)
    full = jnp.einsum(
        "zqrw,zrc->qcw", by_pair, lat_all.astype(jnp.float32), precision=highest
    )
    full = full.reshape(pairs // rings, bands, coarse_rows, coarse_lons)
    full = swapped(jnp.transpose(full, (1, 0, 2, 3)), LAT, 0)
    full = full.reshape(
        members_here, rings // members_here, sides, pairs // rings, coarse_rows, coarse_lons
    )
    full = jnp.transpose(full, (4, 0, 2, 1, 3, 5)).reshape(coarse_weights.shape)
    gradient = full * member_scale + coarse_weights.astype(jnp.float32)

    tiles = jnp.transpose(own.reshape(own_rows, peers, col_count), (1, 0, 2))
    tiles = swapped(tiles, "mem", 0).reshape(levels_here, sides, row_count, col_count)
    kept = jnp.where(first, tiles[:, 0], tiles[:, 1])
    sent = jnp.where(first, tiles[:, 1], tiles[:, 0])
    increment = in_order(kept, lax.ppermute(sent, "lat_1", across), 0)
    return (gradient, increment)


def solution(mesh):
    split = Mesh(mesh.devices.reshape(mesh.shape["mem"], 8, 2), ("mem", "lat_0", "lat_1"))
    placed = (
        P(LAT, "mem", None, None),
        P("mem", None, LAT, None),
        P(LAT, None),
        P(),
        P(None, LAT, "mem"),
        P(None, None, LAT, "mem"),
        P(None, None, LAT, "mem"),
        P(None, None, LAT, "mem"),
    )
    return jax.shard_map(
        body,
        mesh=split,
        in_specs=placed,
        out_specs=(P(LAT, "mem", None, None), P(None, LAT, "mem")),
        check_vma=False,
    )
```

```python
import functools

import jax
import jax.numpy as jnp
from jax import lax
from jax.experimental import pallas as pl
from jax.experimental.pallas import tpu as pltpu
from jax.sharding import Mesh
from jax.sharding import PartitionSpec as P

STEPS = 4
OBLK = 8
HALO = 8
LN2 = 0.6931471805599453
STEPS_16 = 32767.0
LAT = ("lat_0", "lat_1")
ALL = ("mem", "lat_0", "lat_1")

def swapped(value, axis, dim):
    return lax.all_to_all(value, axis, split_axis=dim, concat_axis=dim, tiled=True)


def two_terms(value):
    high = value.astype(jnp.bfloat16)
    low = (value - high.astype(jnp.float32)).astype(jnp.bfloat16)
    return jnp.concatenate([high, low], axis=0)


def dot(a, b):
    return jnp.dot(a, b, preferred_element_type=jnp.float32)


def member_rows(side, own_ref, other_ref, member, level):
    levels_here = other_ref.shape[1]
    own = own_ref[member, side * levels_here + level].astype(jnp.float32)
    other = other_ref[member, level].astype(jnp.float32)
    low = jnp.where(side == 0, own, other)
    high = jnp.where(side == 0, other, own)
    return jnp.concatenate([low, high], axis=0)


def localize_kernel(side_ref, columns_ref, lon_ref, own_ref, other_ref, *refs):
    block_refs, sum_ref = refs[:-1], refs[-1]
    members, levels_here, row_count, lon_total = other_ref.shape
    tall = 2 * row_count
    side = side_ref[0]
    per_block = columns_ref.shape[1] // len(block_refs)
    columns = columns_ref[...]
    lon = lon_ref[...]
    for level in range(levels_here):
        narrow = []
        for member in range(members):
            start = (member * levels_here + level) * per_block
            weights = jnp.concatenate([ref[start : start + per_block] for ref in block_refs], axis=0)
            narrow.append(dot(columns, weights))
        localized = dot(two_terms(jnp.concatenate(narrow, axis=0)), lon)
        total = None
        for member in range(members):
            at = member * tall
            term = localized[at : at + tall] + localized[at + members * tall : at + (members + 1) * tall]
            term = term * member_rows(side, own_ref, other_ref, member, level)
            total = term if total is None else total + term
        count = sum_ref.shape[0] // levels_here
        sum_ref[level * count : (level + 1) * count] = total.reshape(count, tall // count, lon_total)


def row_codes(value):
    largest = jnp.maximum(jnp.max(jnp.abs(value), axis=1, keepdims=True), 1e-30)
    return jnp.ceil(jnp.log(largest) * (256.0 / LN2)) + 1.0


def code_scale(codes):
    return jnp.exp(codes * (LN2 / 256.0))


def project_kernel(side_ref, adjoint_ref, lon_ref, own_ref, other_ref, out_ref, tile_ref):
    members, levels_here, row_count, lon_total = other_ref.shape
    rings, _, coarse_lons = out_ref.shape
    tall = 2 * row_count
    side = side_ref[0]
    lon = lon_ref[...]
    quarters = adjoint_ref.shape[0] // levels_here
    row_tiles = tall // quarters // 8
    lane_tiles = lon_total // 128
    per_message = members * levels_here // rings
    row = lax.broadcasted_iota(jnp.int32, (tall, 128), 0)
    lane = lax.broadcasted_iota(jnp.int32, (tall, 128), 1)
    tails = [jnp.zeros((1, 128), jnp.float32) for _ in range(rings)]
    for level in range(levels_here):
        strips = []
        for at in range(lane_tiles):
            strips.append(
                jnp.concatenate(
                    [
                        adjoint_ref[
                            level * quarters + q, (t * lane_tiles + at) * 8 : (t * lane_tiles + at + 1) * 8
                        ]
                        for q in range(quarters)
                        for t in range(row_tiles)
                    ],
                    axis=0,
                )
            )
        adjoint = jnp.concatenate(strips, axis=1)
        product = [
            member_rows(side, own_ref, other_ref, member, level) * adjoint for member in range(members)
        ]
        projected = dot(two_terms(jnp.concatenate(product, axis=0)), lon)
        for member in range(members):
            at = member * tall
            value = projected[at : at + tall] + projected[at + members * tall : at + (members + 1) * tall]
            pair = member * levels_here + level
            ring, place = pair // per_message, pair % per_message
            codes = row_codes(value)
            whole = jnp.round(value * (STEPS_16 / code_scale(codes))).astype(jnp.int32)
            out_ref[ring, place * tall : (place + 1) * tall] = whole.astype(jnp.int16)
            mark = jnp.where(lane == row + place * tall, codes, 0.0)
            tails[ring] = tails[ring] + jnp.sum(mark, axis=0, keepdims=True)
        for q in range(quarters):
            piece = adjoint_ref[level * quarters + q, row_tiles * lane_tiles * 8 :]
            band, start = q * row_tiles * 8 // row_count, q * row_tiles * 8 % row_count
            width = tile_ref.shape[3]
            tile_ref[band, level, start : start + 8] = piece[:, :width]
            tile_ref[band, level, start + 8 : start + 16] = piece[:, width:]
    data = per_message * tall
    for ring in range(rings):
        tail = jnp.broadcast_to(tails[ring], (16, 128)).astype(jnp.int32).astype(jnp.int16)
        out_ref[ring, data : data + 16] = jnp.concatenate([tail] * (coarse_lons // 128), axis=1)


def gather_kernel(scale, message_ref, lat_ref, out_ref):
    rings, rows, lons = message_ref.shape
    bands, places, coarse_rows, _ = out_ref.shape
    data = rows - 16
    coarse = bands * coarse_rows
    high, low, scales = [], [], []
    for ring in range(rings):
        value = message_ref[ring, :data].astype(jnp.int32).astype(jnp.float32)
        upper = jnp.floor(value * (1.0 / 256.0)) * 256.0
        high.append(upper.astype(jnp.bfloat16))
        low.append((value - upper).astype(jnp.bfloat16))
        codes = message_ref[ring, data:].astype(jnp.int32).astype(jnp.float32)[:1, :data]
        scales.append(code_scale(codes) * (scale / STEPS_16))
    high = jnp.concatenate(high, axis=0)
    low = jnp.concatenate(low, axis=0)
    lat = lat_ref[...].astype(jnp.float32) * jnp.concatenate(scales, axis=1)
    place = lax.broadcasted_iota(jnp.int32, lat.shape, 1) % data // (data // places)
    lat = jnp.concatenate([jnp.where(place == p, lat, 0.0) for p in range(places)], axis=0)
    terms = two_terms(lat)
    total = dot(terms, high)
    total = total[: places * coarse] + (total[places * coarse :] + dot(terms[: places * coarse], low))
    for band in range(bands):
        for p in range(places):
            at = p * coarse + band * coarse_rows
            out_ref[band, p] = total[at : at + coarse_rows]


def arrange_kernel(side_ref, own_ref, other_ref, out_ref):
    peers, _, row_count, lanes = own_ref.shape
    side = side_ref[0]
    is_own = side_ref[1] == 1
    lane = lax.broadcasted_iota(jnp.int32, (row_count, lanes), 1)
    width = lanes // 2
    pick = lambda peer, which, mine: jnp.where(is_own, own_ref[peer, mine], other_ref[peer, which])
    winds = [pick(peer, 1, 2) for peer in range(peers)]
    seen = [pick(peer, 0, side) for peer in range(peers)]
    lon_total = peers * width
    for at in range(peers // 2):
        even, odd = winds[2 * at], winds[2 * at + 1]
        spot = slice(at * lanes, (at + 1) * lanes)
        out_ref[:, spot] = jnp.where(lane < width, even, pltpu.roll(odd, width, 1))
        spot = slice(lon_total + at * lanes, lon_total + (at + 1) * lanes)
        out_ref[:, spot] = jnp.where(lane < width, pltpu.roll(even, width, 1), odd)
    blocks = lanes // peers
    kinds = (out_ref.shape[1] - 2 * lon_total) // lanes
    owner = lane // blocks
    for kind in range(kinds):
        total = jnp.zeros((row_count, lanes), jnp.float32)
        for peer in range(peers):
            shift = (peer - kind) * blocks % lanes
            value = seen[peer] if shift == 0 else pltpu.roll(seen[peer], shift, 1)
            total = jnp.where(owner == peer, value, total)
        spot = slice(2 * lon_total + kind * lanes, 2 * lon_total + (kind + 1) * lanes)
        out_ref[:, spot] = total


def spread_kernel(before_ref, local_ref, after_ref, wind_ref, gain_ref, value_ref):
    _, rows, cols = wind_ref.shape
    lanes = cols // OBLK
    local = jnp.concatenate([before_ref[...], local_ref[...], after_ref[...]], axis=0)
    wind_ref[0] = local[:, :cols]
    wind_ref[1] = local[:, cols : 2 * cols]
    sights = [local[:, 2 * cols + k * lanes : 2 * cols + (k + 1) * lanes] for k in range(3 * STEPS)]
    cells = jnp.concatenate(sights[:STEPS], axis=0).astype(jnp.bfloat16)
    others = jnp.concatenate(sights[STEPS:], axis=0)
    high = others.astype(jnp.bfloat16)
    rest = others - high.astype(jnp.float32)
    middle = rest.astype(jnp.bfloat16)
    low = (rest - middle.astype(jnp.float32)).astype(jnp.bfloat16)
    block = lax.broadcasted_iota(jnp.int32, (lanes, cols), 0)
    spread = (lax.broadcasted_iota(jnp.int32, (lanes, cols), 1) // OBLK == block).astype(jnp.bfloat16)
    cells = dot(cells, spread)
    wide = dot(high, spread) + (dot(middle, spread) + dot(low, spread))
    offset = lax.broadcasted_iota(jnp.int32, (rows, cols), 1) % OBLK
    offset = offset.astype(jnp.float32)
    for step in range(STEPS):
        value_ref[step] = wide[step * rows : (step + 1) * rows]
        hit = jnp.abs(cells[step * rows : (step + 1) * rows] - offset) < 0.5
        weight = wide[(STEPS + step) * rows : (STEPS + step + 1) * rows]
        gain_ref[step] = jnp.where(hit, weight, 0.0)


def stencil_kernel(place_ref, own_ref, before_ref, after_ref, wind_ref, gain_ref, value_ref, adjoint_ref):
    rows, cols = wind_ref.shape[1:]
    first_row = place_ref[0]
    last_row = place_ref[1]
    state = jnp.concatenate([before_ref[...], own_ref[...], after_ref[...]], axis=0)
    row = lax.broadcasted_iota(jnp.int32, (rows, cols), 0) + first_row
    col = lax.broadcasted_iota(jnp.int32, (rows, cols), 1)
    inside = ((row >= 0) & (row < last_row)).astype(jnp.float32)
    not_first = (col > 0).astype(jnp.float32)
    not_last = (col < cols - 1).astype(jnp.float32)
    lon_wind = 0.5 * wind_ref[0]
    lat_wind = 0.5 * wind_ref[1]

    def north(x):
        return pltpu.roll(x, rows - 1, 0)

    def south(x):
        return pltpu.roll(x, 1, 0)

    def east(x):
        return pltpu.roll(x, cols - 1, 1)

    def west(x):
        return pltpu.roll(x, 1, 1)

    from_north = (0.2 - lat_wind) * inside
    from_south = (0.2 + lat_wind) * inside
    from_east = (0.2 - lon_wind) * inside * not_last
    from_west = (0.2 + lon_wind) * inside * not_first
    centre = 0.2 * inside
    forcings = []
    for step in range(STEPS):
        state = (
            centre * state
            + from_north * north(state)
            + from_south * south(state)
            + from_east * east(state)
            + from_west * west(state)
        )
        forcings.append(gain_ref[step] * (state - value_ref[step]))
    to_south = 0.2 + lat_wind
    to_north = 0.2 - lat_wind
    to_west = (0.2 + lon_wind) * not_first
    to_east = (0.2 - lon_wind) * not_last
    adjoint = None
    for step in reversed(range(STEPS)):
        pushed = forcings[step] if adjoint is None else adjoint + forcings[step]
        adjoint = inside * (
            0.2 * pushed
            + north(to_south * pushed)
            + south(to_north * pushed)
            + east(to_west * pushed)
            + west(to_east * pushed)
        )
    adjoint = adjoint[HALO : rows - HALO]
    row_tiles, lane_tiles = (rows - 2 * HALO) // 8, cols // 128
    packed = jnp.concatenate(
        [
            adjoint[t * 8 : (t + 1) * 8, at * 128 : (at + 1) * 128]
            for t in range(row_tiles)
            for at in range(lane_tiles)
        ],
        axis=0,
    )
    count = adjoint_ref.shape[0]
    width = cols // count
    lane = lax.broadcasted_iota(jnp.int32, (8, 128), 1)
    for copy in range(count):
        adjoint_ref[copy, : row_tiles * lane_tiles * 8] = packed
        strip = slice(copy * width // 128 * 128, copy * width // 128 * 128 + 128)
        top, bottom = own_ref[0:8, strip], own_ref[8:16, strip]
        if copy % 2 == 0:
            piece = jnp.where(lane < width, top, pltpu.roll(bottom, width, 1))
        else:
            piece = jnp.where(lane < width, pltpu.roll(top, width, 1), bottom)
        adjoint_ref[copy, row_tiles * lane_tiles * 8 :] = piece


def body(
    coarse_weights,
    perturbations,
    lat_matrix,
    lon_matrix,
    wind_field,
    observed_cell,
    observed_value,
    observed_weight,
):
    members_here, levels, row_count, lon_total = perturbations.shape
    coarse_rows, _, _, coarse_lons = coarse_weights.shape
    col_count = wind_field.shape[2]
    peers = lax.axis_size("mem")
    rings = lax.axis_size("lat_0")
    sides = lax.axis_size("lat_1")
    bands = rings * sides
    levels_here = levels // sides
    wide_count = row_count * sides
    pairs = members_here * levels_here
    quarters = peers // levels_here
    own_rows = wide_count // quarters
    member_scale = 1.0 / jnp.sqrt(jnp.float32(members_here * peers - 1))
    quarter = lax.axis_index("mem") % quarters
    ring = lax.axis_index("lat_0")
    first = lax.axis_index("lat_1") == 0
    across = [(0, 1), (1, 0)]

    forward = []
    for m in range(peers):
        for z in range(rings):
            for x in range(sides):
                here = (m * rings + z) * sides + x
                if m % quarters < quarters - 1:
                    forward.append((here, here + bands))
                elif z < rings - 1:
                    forward.append((here, here - (quarters - 1) * bands + sides))
    backward = [(b, a) for a, b in forward]

    def halves(value, dim):
        low = lax.slice_in_dim(value, 0, levels_here, axis=dim)
        high = lax.slice_in_dim(value, levels_here, levels, axis=dim)
        return jnp.where(first, low, high), jnp.where(first, high, low)

    def in_order(mine, theirs, dim):
        return jnp.where(
            first, jnp.concatenate([mine, theirs], dim), jnp.concatenate([theirs, mine], dim)
        )

    weight_rows = pairs * coarse_rows
    coarse_total = bands * coarse_rows
    mine, theirs = halves(coarse_weights, 2)
    lat_rows = jnp.concatenate([lat_matrix[: row_count // 2], lat_matrix[row_count // 2 :]], axis=1)

    def by_pair_first(value):
        value = value.reshape(coarse_rows, pairs, coarse_lons)
        return jnp.transpose(value, (1, 0, 2))

    theirs = by_pair_first(theirs).reshape(weight_rows, coarse_lons)
    from_side = lax.ppermute(jnp.concatenate([theirs, lat_rows], axis=0), "lat_1", across)
    both = in_order(
        by_pair_first(mine), from_side[:weight_rows].reshape(pairs, coarse_rows, coarse_lons), 1
    ).reshape(sides * weight_rows, coarse_lons)
    both = jnp.concatenate([both, in_order(lat_rows, from_side[weight_rows:], 0)], axis=0)

    packed = jnp.concatenate(
        [observed_cell.astype(jnp.float32), observed_value, observed_weight], axis=0
    )
    kinds, _, _, block_count = packed.shape
    lanes = 2 * col_count
    packed = jnp.transpose(packed, (1, 2, 0, 3)).reshape(levels, row_count, kinds * block_count)
    packed = jnp.pad(packed, ((0, 0), (0, 0), (0, lanes - kinds * block_count)))
    winds = jnp.transpose(wind_field, (1, 0, 2)).reshape(1, row_count, lanes)
    parts = row_count // own_rows
    packed = packed.reshape(sides, levels_here, 1, parts, own_rows, lanes)
    winds = jnp.broadcast_to(
        winds.reshape(1, 1, 1, parts, own_rows, lanes), (1, levels_here, 1, parts, own_rows, lanes)
    )
    packed = jnp.transpose(jnp.concatenate([packed, winds], axis=0), (1, 2, 3, 0, 4, 5))
    packed = jnp.broadcast_to(
        packed, (levels_here, quarters // parts, parts, sides + 1, own_rows, lanes)
    )
    packed = swapped(packed.reshape(peers, sides + 1, own_rows, lanes), "mem", 0)

    side = lax.axis_index("lat_1")
    other_members = lax.dynamic_slice_in_dim(
        perturbations, (1 - side) * levels_here, levels_here, axis=1
    )
    other_members = lax.ppermute(other_members, "lat_1", across)
    up = [(i, (i + 1) % rings) for i in range(rings)]
    down = [(b, a) for a, b in up]
    blocks = {0: both}
    rising = falling = both
    for hop in range(1, rings // 2 + 1):
        rising = lax.ppermute(rising, "lat_0", up)
        if hop < rings - hop:
            falling = lax.ppermute(falling, "lat_0", down)
        if hop == 2:
            rising, falling, packed = lax.optimization_barrier((rising, falling, packed))
            passed = jnp.where(first, packed[:, 1:], jnp.stack([packed[:, 0], packed[:, 2]], axis=1))
            passed = lax.ppermute(passed, "lat_1", across)
        blocks[-hop % rings] = rising
        if hop < rings - hop:
            blocks[hop] = falling

    def lat_of(block):
        rows = block[sides * weight_rows :].reshape(sides, row_count // 2, coarse_lons)
        rows = jnp.concatenate([rows[..., :coarse_total], rows[..., coarse_total:]], 1)
        return rows.reshape(1, wide_count, coarse_total)

    columns = lat_of(both)[0].reshape(wide_count, rings, sides * coarse_rows)
    columns = lax.dynamic_slice_in_dim(
        jnp.concatenate([columns, columns], axis=1), ring, rings, axis=1
    ).reshape(wide_count, coarse_total)

    scalars = pl.BlockSpec(memory_space=pltpu.SMEM)
    whole = pl.BlockSpec(memory_space=pltpu.VMEM)
    roomy = pltpu.CompilerParams(vmem_limit_bytes=48 * 1024 * 1024)
    where_side = jnp.reshape(side, (1,)).astype(jnp.int32)
    partial_sum = pl.pallas_call(
        localize_kernel,
        out_shape=jax.ShapeDtypeStruct((peers, own_rows, lon_total), jnp.float32),
        in_specs=[scalars] + [whole] * (4 + rings),
        out_specs=whole,
        compiler_params=roomy,
    )(
        where_side,
        columns,
        lon_matrix,
        perturbations,
        other_members,
        *[blocks[d] for d in range(rings)],
    )
    partial_sum, packed, passed = lax.optimization_barrier((partial_sum, packed, passed))
    arrived = swapped(partial_sum, "mem", 0)

    is_own = (quarter // parts == side).astype(jnp.int32)
    local = pl.pallas_call(
        arrange_kernel,
        out_shape=jax.ShapeDtypeStruct(
            (own_rows, 2 * lon_total + kinds * peers * block_count), jnp.float32
        ),
        in_specs=[scalars, whole, whole],
        out_specs=whole,
        compiler_params=roomy,
    )(jnp.stack([side.astype(jnp.int32), is_own]), packed, passed)
    local, *tied = lax.optimization_barrier((local, *[blocks[d] for d in range(rings)]))
    lat_ring = jnp.concatenate([lat_of(block) for block in tied], axis=0)
    lat_all = lax.dynamic_slice_in_dim(
        jnp.concatenate([lat_ring, lat_ring], axis=0), rings - ring, rings, axis=0
    )
    repeats = pairs // rings
    lat_all = jnp.broadcast_to(lat_all[:, None], (rings, repeats, wide_count, coarse_total))
    lat_all = jnp.transpose(lat_all.reshape(rings * repeats * wide_count, coarse_total))
    before = lax.ppermute(local[-HALO:], ALL, forward)
    after = lax.ppermute(local[:HALO], ALL, backward)
    wide_rows = own_rows + 2 * HALO
    wide_wind, gains, values = pl.pallas_call(
        spread_kernel,
        out_shape=[
            jax.ShapeDtypeStruct((count, wide_rows, lon_total), jnp.float32)
            for count in (2, STEPS, STEPS)
        ],
        in_specs=[whole] * 3,
        out_specs=[whole] * 3,
        compiler_params=roomy,
    )(before, local, after)

    own = arrived.sum(axis=0) * member_scale

    before = lax.ppermute(own[-HALO:], ALL, forward)
    after = lax.ppermute(own[:HALO], ALL, backward)
    place = jnp.stack(
        [ring * wide_count + quarter * own_rows - HALO, jnp.int32(row_count * bands)]
    ).astype(jnp.int32)
    copies = pl.pallas_call(
        stencil_kernel,
        out_shape=jax.ShapeDtypeStruct((peers, own_rows * lon_total // 128 + 8, 128), jnp.float32),
        in_specs=[scalars] + [whole] * 6,
        out_specs=whole,
        compiler_params=roomy,
    )(place, own, before, after, wide_wind, gains, values)

    adjoint_all = swapped(copies, "mem", 0)
    projected, tiles = pl.pallas_call(
        project_kernel,
        out_shape=[
            jax.ShapeDtypeStruct((rings, repeats * wide_count + 16, coarse_lons), jnp.int16),
            jax.ShapeDtypeStruct((sides, levels_here, row_count, col_count), jnp.float32),
        ],
        in_specs=[scalars] + [whole] * 4,
        out_specs=[whole] * 2,
        compiler_params=roomy,
    )(where_side, adjoint_all, jnp.transpose(lon_matrix), perturbations, other_members)
    by_pair = swapped(projected, "lat_0", 0)
    full = pl.pallas_call(
        functools.partial(gather_kernel, (members_here * peers - 1) ** -0.5),
        out_shape=jax.ShapeDtypeStruct((bands, repeats, coarse_rows, coarse_lons), jnp.float32),
        in_specs=[whole] * 2,
        out_specs=whole,
        compiler_params=roomy,
    )(by_pair, lat_all)
    full = swapped(full, LAT, 0)
    full = full.reshape(
        members_here, rings // members_here, sides, pairs // rings, coarse_rows, coarse_lons
    )
    full = jnp.transpose(full, (4, 0, 2, 1, 3, 5)).reshape(coarse_weights.shape)
    gradient = full + coarse_weights.astype(jnp.float32)

    kept = jnp.where(first, tiles[0], tiles[1])
    sent = jnp.where(first, tiles[1], tiles[0])
    increment = in_order(kept, lax.ppermute(sent, "lat_1", across), 0)
    return (gradient, increment)


def solution(mesh):
    split = Mesh(mesh.devices.reshape(mesh.shape["mem"], 8, 2), ("mem", "lat_0", "lat_1"))
    placed = (
        P(LAT, "mem", None, None),
        P("mem", None, LAT, None),
        P(LAT, None),
        P(),
        P(None, LAT, "mem"),
        P(None, None, LAT, "mem"),
        P(None, None, LAT, "mem"),
        P(None, None, LAT, "mem"),
    )
    return jax.shard_map(
        body,
        mesh=split,
        in_specs=placed,
        out_specs=(P(LAT, "mem", None, None), P(None, LAT, "mem")),
        check_vma=False,
    )
```

```python
import functools

import jax
import jax.numpy as jnp
from jax import lax
from jax.experimental import pallas as pl
from jax.experimental.pallas import tpu as pltpu
from jax.sharding import Mesh
from jax.sharding import PartitionSpec as P

STEPS = 4
OBLK = 8
HALO = 8
LN2 = 0.6931471805599453
STEPS_16 = 32767.0
LAT = ("lat_0", "lat_1")
ALL = ("mem", "lat_0", "lat_1")

def swapped(value, axis, dim):
    return lax.all_to_all(value, axis, split_axis=dim, concat_axis=dim, tiled=True)


def two_terms(value):
    high = value.astype(jnp.bfloat16)
    low = (value - high.astype(jnp.float32)).astype(jnp.bfloat16)
    return jnp.concatenate([high, low], axis=0)


def dot(a, b):
    return jnp.dot(a, b, preferred_element_type=jnp.float32)


def dot_last(a, b):
    return lax.dot_general(a, b, (((1,), (1,)), ((), ())), preferred_element_type=jnp.float32)


def row_codes(value):
    largest = jnp.maximum(jnp.max(jnp.abs(value), axis=1, keepdims=True), 1e-30)
    return jnp.ceil(jnp.log(largest) * (256.0 / LN2)) + 1.0


def code_scale(codes):
    return jnp.exp(codes * (LN2 / 256.0))


def rounded(value, codes):
    return jnp.round(value * (STEPS_16 / code_scale(codes)))


def to_16(value):
    return value.astype(jnp.int32).astype(jnp.int16)


def from_16(value):
    return value.astype(jnp.int32).astype(jnp.float32)


def as_tiles(value):
    rows, cols = value.shape
    return jnp.concatenate(
        [
            value[t * 8 : (t + 1) * 8, at * 128 : (at + 1) * 128]
            for t in range(rows // 8)
            for at in range(cols // 128)
        ],
        axis=0,
    )


def from_tiles(value, row_tiles):
    lane_tiles = value.shape[0] // 8 // row_tiles
    rows = []
    for t in range(row_tiles):
        start = t * lane_tiles * 8
        strips = [value[start + at * 8 : start + (at + 1) * 8] for at in range(lane_tiles)]
        rows.append(jnp.concatenate(strips, axis=1))
    return jnp.concatenate(rows, axis=0)


def tile_scales(codes, lane_tiles):
    scales = code_scale(codes) * (1.0 / STEPS_16)
    parts = []
    for t in range(scales.shape[0] // 8):
        parts += [scales[t * 8 : (t + 1) * 8]] * lane_tiles
    return jnp.concatenate(parts, axis=0)


def load_members(side, own_hbm, other_hbm, own_ref, other_ref, sems):
    levels_here = other_hbm.shape[1]
    copies = []
    for level in range(levels_here):
        pair = (
            pltpu.make_async_copy(
                own_hbm.at[:, side * levels_here + level], own_ref.at[:, level], sems.at[2 * level]
            ),
            pltpu.make_async_copy(
                other_hbm.at[:, level], other_ref.at[:, level], sems.at[2 * level + 1]
            ),
        )
        for copy in pair:
            copy.start()
        copies.append(pair)
    return copies


def member_rows(side, own_ref, other_ref, member, level):
    own = own_ref[member, level].astype(jnp.float32)
    other = other_ref[member, level].astype(jnp.float32)
    low = jnp.where(side == 0, own, other)
    high = jnp.where(side == 0, other, own)
    return jnp.concatenate([low, high], axis=0)


def localize_kernel(side_ref, columns_ref, lon_hbm, own_hbm, other_hbm, *refs):
    block_refs = refs[:-6]
    out_hbm, lon_ref, own_ref, other_ref, out_ref, sems = refs[-6:]
    members, levels_here, row_count, lon_total = other_ref.shape
    tall = 2 * row_count
    side = side_ref[0]
    lon_copy = pltpu.make_async_copy(lon_hbm, lon_ref, sems.at[3 * levels_here])
    lon_copy.start()
    loads = load_members(side, own_hbm, other_hbm, own_ref, other_ref, sems)
    per_block = columns_ref.shape[1] // len(block_refs)
    columns = columns_ref[...]
    count = out_ref.shape[0] // levels_here
    piece_rows = tall // count
    data = piece_rows * lon_total // 128
    stores = []
    for level in range(levels_here):
        narrow = []
        for member in range(members):
            start = (member * levels_here + level) * per_block
            weights = jnp.concatenate([ref[start : start + per_block] for ref in block_refs], axis=0)
            narrow.append(dot(columns, weights))
        if level == 0:
            lon_copy.wait()
        localized = dot(two_terms(jnp.concatenate(narrow, axis=0)), lon_ref[...])
        for copy in loads[level]:
            copy.wait()
        total = None
        for member in range(members):
            at = member * tall
            term = localized[at : at + tall] + localized[at + members * tall : at + (members + 1) * tall]
            term = term * member_rows(side, own_ref, other_ref, member, level)
            total = term if total is None else total + term
        codes = row_codes(total)
        total = rounded(total, codes)
        for piece in range(count):
            part = slice(piece * piece_rows, (piece + 1) * piece_rows)
            out_ref[level * count + piece, :data] = to_16(as_tiles(total[part]))
            out_ref[level * count + piece, data:] = to_16(
                jnp.broadcast_to(codes[part], (piece_rows, 128))
            )
        part = pl.ds(level * count, count)
        store = pltpu.make_async_copy(
            out_ref.at[part], out_hbm.at[part], sems.at[2 * levels_here + level]
        )
        store.start()
        stores.append(store)
    for store in stores:
        store.wait()


def add_kernel(scale, message_ref, out_ref):
    sources, rows, _ = message_ref.shape
    own_rows, lon_total = out_ref.shape
    total = None
    for source in range(sources):
        value = from_16(message_ref[source, : rows - own_rows])
        codes = from_16(message_ref[source, rows - own_rows :])
        value = value * tile_scales(codes, lon_total // 128)
        total = value if total is None else total + value
    out_ref[...] = from_tiles(total, own_rows // 8) * scale


def project_kernel(side_ref, message_ref, lon_hbm, own_hbm, other_hbm, out_hbm, tile_ref, lon_ref, own_ref, other_ref, out_ref, sems):
    members, levels_here, row_count, lon_total = other_ref.shape
    rings, _, coarse_lons = out_ref.shape
    tall = 2 * row_count
    side = side_ref[0]
    lon_copy = pltpu.make_async_copy(lon_hbm, lon_ref, sems.at[2 * levels_here])
    lon_copy.start()
    loads = load_members(side, own_hbm, other_hbm, own_ref, other_ref, sems)
    quarters = message_ref.shape[0] // levels_here
    own_rows = tall // quarters
    lane_tiles = lon_total // 128
    data = own_rows * lane_tiles
    per_message = members * levels_here // rings
    row = lax.broadcasted_iota(jnp.int32, (tall, 128), 0)
    lane = lax.broadcasted_iota(jnp.int32, (tall, 128), 1)
    tails = [jnp.zeros((1, 128), jnp.float32) for _ in range(rings)]
    width = tile_ref.shape[3]
    for level in range(levels_here):
        pieces = []
        for q in range(quarters):
            value = from_16(message_ref[level * quarters + q, :data])
            codes = from_16(message_ref[level * quarters + q, data : data + own_rows])
            pieces.append(from_tiles(value * tile_scales(codes, lane_tiles), own_rows // 8))
            tail = from_16(message_ref[level * quarters + q, data + own_rows :])
            tile = tail[:8] * (code_scale(tail[8:]) * (1.0 / STEPS_16))
            band, start = q * own_rows // row_count, q * own_rows % row_count
            tile_ref[band, level, start : start + 8] = tile[:, :width]
            tile_ref[band, level, start + 8 : start + 16] = tile[:, width:]
        adjoint = jnp.concatenate(pieces, axis=0)
        for copy in loads[level]:
            copy.wait()
        product = [
            member_rows(side, own_ref, other_ref, member, level) * adjoint for member in range(members)
        ]
        if level == 0:
            lon_copy.wait()
        projected = dot_last(two_terms(jnp.concatenate(product, axis=0)), lon_ref[...])
        for member in range(members):
            at = member * tall
            value = projected[at : at + tall] + projected[at + members * tall : at + (members + 1) * tall]
            pair = member * levels_here + level
            ring, place = pair // per_message, pair % per_message
            codes = row_codes(value)
            out_ref[ring, place * tall : (place + 1) * tall] = to_16(rounded(value, codes))
            mark = jnp.where(lane == row + place * tall, codes, 0.0)
            tails[ring] = tails[ring] + jnp.sum(mark, axis=0, keepdims=True)
    stores = []
    for ring in range(rings):
        tail = to_16(jnp.broadcast_to(tails[ring], (16, 128)))
        start = per_message * tall
        out_ref[ring, start : start + 16] = jnp.concatenate([tail] * (coarse_lons // 128), axis=1)
    store = pltpu.make_async_copy(out_ref, out_hbm, sems.at[2 * levels_here + 1])
    store.start()
    store.wait()


def gather_kernel(scale, message_ref, lat_ref, out_ref):
    rings, rows, lons = message_ref.shape
    bands, places, coarse_rows, _ = out_ref.shape
    data = rows - 16
    coarse = bands * coarse_rows
    high, low, scales = [], [], []
    for ring in range(rings):
        value = from_16(message_ref[ring, :data])
        upper = jnp.floor(value * (1.0 / 256.0)) * 256.0
        high.append(upper.astype(jnp.bfloat16))
        low.append((value - upper).astype(jnp.bfloat16))
        codes = from_16(message_ref[ring, data:])[:1, :data]
        scales.append(code_scale(codes) * (scale / STEPS_16))
    high = jnp.concatenate(high, axis=0)
    low = jnp.concatenate(low, axis=0)
    lat = lat_ref[...].astype(jnp.float32) * jnp.concatenate(scales, axis=1)
    place = lax.broadcasted_iota(jnp.int32, lat.shape, 1) % data // (data // places)
    lat = jnp.concatenate([jnp.where(place == p, lat, 0.0) for p in range(places)], axis=0)
    terms = two_terms(lat)
    total = dot(terms, high)
    total = total[: places * coarse] + (total[places * coarse :] + dot(terms[: places * coarse], low))
    for band in range(bands):
        for p in range(places):
            at = p * coarse + band * coarse_rows
            out_ref[band, p] = total[at : at + coarse_rows]


def arrange_kernel(side_ref, own_ref, other_ref, out_ref):
    peers, _, row_count, lanes = own_ref.shape
    side = side_ref[0]
    is_own = side_ref[1] == 1
    lane = lax.broadcasted_iota(jnp.int32, (row_count, lanes), 1)
    width = lanes // 2
    pick = lambda peer, which, mine: jnp.where(is_own, own_ref[peer, mine], other_ref[peer, which])
    winds = [pick(peer, 1, 2) for peer in range(peers)]
    seen = [pick(peer, 0, side) for peer in range(peers)]
    lon_total = peers * width
    for at in range(peers // 2):
        even, odd = winds[2 * at], winds[2 * at + 1]
        spot = slice(at * lanes, (at + 1) * lanes)
        out_ref[:, spot] = jnp.where(lane < width, even, pltpu.roll(odd, width, 1))
        spot = slice(lon_total + at * lanes, lon_total + (at + 1) * lanes)
        out_ref[:, spot] = jnp.where(lane < width, pltpu.roll(even, width, 1), odd)
    blocks = lanes // peers
    kinds = (out_ref.shape[1] - 2 * lon_total) // lanes
    owner = lane // blocks
    for kind in range(kinds):
        total = jnp.zeros((row_count, lanes), jnp.float32)
        for peer in range(peers):
            shift = (peer - kind) * blocks % lanes
            value = seen[peer] if shift == 0 else pltpu.roll(seen[peer], shift, 1)
            total = jnp.where(owner == peer, value, total)
        spot = slice(2 * lon_total + kind * lanes, 2 * lon_total + (kind + 1) * lanes)
        out_ref[:, spot] = total


def spread_kernel(before_ref, local_ref, after_ref, wind_ref, gain_ref, value_ref):
    _, rows, cols = wind_ref.shape
    lanes = cols // OBLK
    local = jnp.concatenate([before_ref[...], local_ref[...], after_ref[...]], axis=0)
    wind_ref[0] = local[:, :cols]
    wind_ref[1] = local[:, cols : 2 * cols]
    sights = [local[:, 2 * cols + k * lanes : 2 * cols + (k + 1) * lanes] for k in range(3 * STEPS)]
    cells = jnp.concatenate(sights[:STEPS], axis=0).astype(jnp.bfloat16)
    others = jnp.concatenate(sights[STEPS:], axis=0)
    high = others.astype(jnp.bfloat16)
    rest = others - high.astype(jnp.float32)
    middle = rest.astype(jnp.bfloat16)
    low = (rest - middle.astype(jnp.float32)).astype(jnp.bfloat16)
    block = lax.broadcasted_iota(jnp.int32, (lanes, cols), 0)
    spread = (lax.broadcasted_iota(jnp.int32, (lanes, cols), 1) // OBLK == block).astype(jnp.bfloat16)
    cells = dot(cells, spread)
    wide = dot(high, spread) + (dot(middle, spread) + dot(low, spread))
    offset = lax.broadcasted_iota(jnp.int32, (rows, cols), 1) % OBLK
    offset = offset.astype(jnp.float32)
    for step in range(STEPS):
        value_ref[step] = wide[step * rows : (step + 1) * rows]
        hit = jnp.abs(cells[step * rows : (step + 1) * rows] - offset) < 0.5
        weight = wide[(STEPS + step) * rows : (STEPS + step + 1) * rows]
        gain_ref[step] = jnp.where(hit, weight, 0.0)


def stencil_kernel(place_ref, own_ref, before_ref, after_ref, wind_ref, gain_ref, value_ref, out_hbm, adjoint_ref, piece_ref, sems):
    rows, cols = wind_ref.shape[1:]
    first_row = place_ref[0]
    last_row = place_ref[1]
    state = jnp.concatenate([before_ref[...], own_ref[...], after_ref[...]], axis=0)
    row = lax.broadcasted_iota(jnp.int32, (rows, cols), 0) + first_row
    col = lax.broadcasted_iota(jnp.int32, (rows, cols), 1)
    inside = ((row >= 0) & (row < last_row)).astype(jnp.float32)
    not_first = (col > 0).astype(jnp.float32)
    not_last = (col < cols - 1).astype(jnp.float32)
    lon_wind = 0.5 * wind_ref[0]
    lat_wind = 0.5 * wind_ref[1]

    def north(x):
        return pltpu.roll(x, rows - 1, 0)

    def south(x):
        return pltpu.roll(x, 1, 0)

    def east(x):
        return pltpu.roll(x, cols - 1, 1)

    def west(x):
        return pltpu.roll(x, 1, 1)

    from_north = (0.2 - lat_wind) * inside
    from_south = (0.2 + lat_wind) * inside
    from_east = (0.2 - lon_wind) * inside * not_last
    from_west = (0.2 + lon_wind) * inside * not_first
    centre = 0.2 * inside
    forcings = []
    for step in range(STEPS):
        state = (
            centre * state
            + from_north * north(state)
            + from_south * south(state)
            + from_east * east(state)
            + from_west * west(state)
        )
        forcings.append(gain_ref[step] * (state - value_ref[step]))
    to_south = 0.2 + lat_wind
    to_north = 0.2 - lat_wind
    to_west = (0.2 + lon_wind) * not_first
    to_east = (0.2 - lon_wind) * not_last
    adjoint = None
    for step in reversed(range(STEPS)):
        pushed = forcings[step] if adjoint is None else adjoint + forcings[step]
        adjoint = inside * (
            0.2 * pushed
            + north(to_south * pushed)
            + south(to_north * pushed)
            + east(to_west * pushed)
            + west(to_east * pushed)
        )
    adjoint = adjoint[HALO : rows - HALO]
    own_rows = rows - 2 * HALO
    data = own_rows * cols // 128
    codes = row_codes(adjoint)
    adjoint_ref[:data] = to_16(as_tiles(rounded(adjoint, codes)))
    adjoint_ref[data:] = to_16(jnp.broadcast_to(codes, (own_rows, 128)))
    count = out_hbm.shape[0]
    copies = [
        pltpu.make_async_copy(
            adjoint_ref, out_hbm.at[copy, pl.ds(0, data + own_rows)], sems.at[copy]
        )
        for copy in range(count)
    ]
    for copy in copies:
        copy.start()
    width = cols // count
    lane = lax.broadcasted_iota(jnp.int32, (8, 128), 1)
    own = own_ref[...]
    codes = row_codes(own)
    own = rounded(own, codes)
    codes = jnp.where(lane < width, codes[:8], codes[8:])
    for copy in range(count):
        strip = slice(copy * width // 128 * 128, copy * width // 128 * 128 + 128)
        top, bottom = own[0:8, strip], own[8:16, strip]
        if copy % 2 == 0:
            piece = jnp.where(lane < width, top, pltpu.roll(bottom, width, 1))
        else:
            piece = jnp.where(lane < width, pltpu.roll(top, width, 1), bottom)
        piece_ref[copy] = to_16(jnp.concatenate([piece, codes], axis=0))
    last = pltpu.make_async_copy(
        piece_ref, out_hbm.at[:, pl.ds(data + own_rows, 16)], sems.at[count]
    )
    last.start()
    for copy in copies:
        copy.wait()
    last.wait()


def body(
    coarse_weights,
    perturbations,
    lat_matrix,
    lon_matrix,
    wind_field,
    observed_cell,
    observed_value,
    observed_weight,
):
    members_here, levels, row_count, lon_total = perturbations.shape
    coarse_rows, _, _, coarse_lons = coarse_weights.shape
    col_count = wind_field.shape[2]
    peers = lax.axis_size("mem")
    rings = lax.axis_size("lat_0")
    sides = lax.axis_size("lat_1")
    bands = rings * sides
    levels_here = levels // sides
    wide_count = row_count * sides
    pairs = members_here * levels_here
    quarters = peers // levels_here
    own_rows = wide_count // quarters
    quarter = lax.axis_index("mem") % quarters
    ring = lax.axis_index("lat_0")
    first = lax.axis_index("lat_1") == 0
    across = [(0, 1), (1, 0)]

    forward = []
    for m in range(peers):
        for z in range(rings):
            for x in range(sides):
                here = (m * rings + z) * sides + x
                if m % quarters < quarters - 1:
                    forward.append((here, here + bands))
                elif z < rings - 1:
                    forward.append((here, here - (quarters - 1) * bands + sides))
    backward = [(b, a) for a, b in forward]

    def halves(value, dim):
        low = lax.slice_in_dim(value, 0, levels_here, axis=dim)
        high = lax.slice_in_dim(value, levels_here, levels, axis=dim)
        return jnp.where(first, low, high), jnp.where(first, high, low)

    def in_order(mine, theirs, dim):
        return jnp.where(
            first, jnp.concatenate([mine, theirs], dim), jnp.concatenate([theirs, mine], dim)
        )

    weight_rows = pairs * coarse_rows
    coarse_total = bands * coarse_rows
    mine, theirs = halves(coarse_weights, 2)
    lat_rows = jnp.concatenate([lat_matrix[: row_count // 2], lat_matrix[row_count // 2 :]], axis=1)

    def by_pair_first(value):
        value = value.reshape(coarse_rows, pairs, coarse_lons)
        return jnp.transpose(value, (1, 0, 2))

    theirs = by_pair_first(theirs).reshape(weight_rows, coarse_lons)
    from_side = lax.ppermute(jnp.concatenate([theirs, lat_rows], axis=0), "lat_1", across)
    both = in_order(
        by_pair_first(mine), from_side[:weight_rows].reshape(pairs, coarse_rows, coarse_lons), 1
    ).reshape(sides * weight_rows, coarse_lons)
    both = jnp.concatenate([both, in_order(lat_rows, from_side[weight_rows:], 0)], axis=0)

    packed = jnp.concatenate(
        [observed_cell.astype(jnp.float32), observed_value, observed_weight], axis=0
    )
    kinds, _, _, block_count = packed.shape
    lanes = 2 * col_count
    packed = jnp.transpose(packed, (1, 2, 0, 3)).reshape(levels, row_count, kinds * block_count)
    packed = jnp.pad(packed, ((0, 0), (0, 0), (0, lanes - kinds * block_count)))
    winds = jnp.transpose(wind_field, (1, 0, 2)).reshape(1, row_count, lanes)
    parts = row_count // own_rows
    packed = packed.reshape(sides, levels_here, 1, parts, own_rows, lanes)
    winds = jnp.broadcast_to(
        winds.reshape(1, 1, 1, parts, own_rows, lanes), (1, levels_here, 1, parts, own_rows, lanes)
    )
    packed = jnp.transpose(jnp.concatenate([packed, winds], axis=0), (1, 2, 3, 0, 4, 5))
    packed = jnp.broadcast_to(
        packed, (levels_here, quarters // parts, parts, sides + 1, own_rows, lanes)
    )
    packed = swapped(packed.reshape(peers, sides + 1, own_rows, lanes), "mem", 0)

    side = lax.axis_index("lat_1")
    other_members = lax.dynamic_slice_in_dim(
        perturbations, (1 - side) * levels_here, levels_here, axis=1
    )
    other_members = lax.ppermute(other_members, "lat_1", across)
    up = [(i, (i + 1) % rings) for i in range(rings)]
    down = [(b, a) for a, b in up]
    blocks = {0: both}
    rising = falling = both
    for hop in range(1, rings // 2 + 1):
        rising = lax.ppermute(rising, "lat_0", up)
        if hop < rings - hop:
            falling = lax.ppermute(falling, "lat_0", down)
        if hop == 2:
            rising, falling, packed = lax.optimization_barrier((rising, falling, packed))
            passed = jnp.where(first, packed[:, 1:], jnp.stack([packed[:, 0], packed[:, 2]], axis=1))
            passed = lax.ppermute(passed, "lat_1", across)
        if hop == 3:
            rising, falling, other_members = lax.optimization_barrier(
                (rising, falling, other_members)
            )
        blocks[-hop % rings] = rising
        if hop < rings - hop:
            blocks[hop] = falling

    def lat_of(block):
        rows = block[sides * weight_rows :].reshape(sides, row_count // 2, coarse_lons)
        rows = jnp.concatenate([rows[..., :coarse_total], rows[..., coarse_total:]], 1)
        return rows.reshape(1, wide_count, coarse_total)

    columns = lat_of(both)[0].reshape(wide_count, rings, sides * coarse_rows)
    columns = lax.dynamic_slice_in_dim(
        jnp.concatenate([columns, columns], axis=1), ring, rings, axis=1
    ).reshape(wide_count, coarse_total)

    scalars = pl.BlockSpec(memory_space=pltpu.SMEM)
    whole = pl.BlockSpec(memory_space=pltpu.VMEM)
    roomy = pltpu.CompilerParams(vmem_limit_bytes=48 * 1024 * 1024)
    where_side = jnp.reshape(side, (1,)).astype(jnp.int32)
    anywhere = pl.BlockSpec(memory_space=pl.ANY)
    half_members = pltpu.VMEM((members_here, levels_here, row_count, lon_total), jnp.bfloat16)
    whole_lon = pltpu.VMEM(lon_matrix.shape, jnp.bfloat16)
    piece_rows = own_rows * lon_total // 128 + own_rows
    partial_sum = pl.pallas_call(
        localize_kernel,
        out_shape=jax.ShapeDtypeStruct((peers, piece_rows, 128), jnp.int16),
        in_specs=[scalars, whole] + [anywhere] * 3 + [whole] * rings,
        out_specs=anywhere,
        scratch_shapes=[
            whole_lon,
            half_members,
            half_members,
            pltpu.VMEM((peers, piece_rows, 128), jnp.int16),
            pltpu.SemaphoreType.DMA((3 * levels_here + 1,)),
        ],
        compiler_params=roomy,
    )(
        where_side,
        columns,
        lon_matrix,
        perturbations,
        other_members,
        *[blocks[d] for d in range(rings)],
    )
    partial_sum, packed, passed = lax.optimization_barrier((partial_sum, packed, passed))
    arrived = swapped(partial_sum, "mem", 0)

    is_own = (quarter // parts == side).astype(jnp.int32)
    local = pl.pallas_call(
        arrange_kernel,
        out_shape=jax.ShapeDtypeStruct(
            (own_rows, 2 * lon_total + kinds * peers * block_count), jnp.float32
        ),
        in_specs=[scalars, whole, whole],
        out_specs=whole,
        compiler_params=roomy,
    )(jnp.stack([side.astype(jnp.int32), is_own]), packed, passed)
    local, *tied = lax.optimization_barrier((local, *[blocks[d] for d in range(rings)]))
    lat_ring = jnp.concatenate([lat_of(block) for block in tied], axis=0)
    lat_all = lax.dynamic_slice_in_dim(
        jnp.concatenate([lat_ring, lat_ring], axis=0), rings - ring, rings, axis=0
    )
    repeats = pairs // rings
    lat_all = jnp.broadcast_to(lat_all[:, None], (rings, repeats, wide_count, coarse_total))
    lat_all = jnp.transpose(lat_all.reshape(rings * repeats * wide_count, coarse_total))
    before = lax.ppermute(local[-HALO:], ALL, forward)
    after = lax.ppermute(local[:HALO], ALL, backward)
    wide_rows = own_rows + 2 * HALO
    wide_wind, gains, values = pl.pallas_call(
        spread_kernel,
        out_shape=[
            jax.ShapeDtypeStruct((count, wide_rows, lon_total), jnp.float32)
            for count in (2, STEPS, STEPS)
        ],
        in_specs=[whole] * 3,
        out_specs=[whole] * 3,
        compiler_params=roomy,
    )(before, local, after)

    scale = (members_here * peers - 1) ** -0.5
    own = pl.pallas_call(
        functools.partial(add_kernel, scale),
        out_shape=jax.ShapeDtypeStruct((own_rows, lon_total), jnp.float32),
        in_specs=[whole],
        out_specs=whole,
        compiler_params=roomy,
    )(arrived)

    before = lax.ppermute(own[-HALO:], ALL, forward)
    after = lax.ppermute(own[:HALO], ALL, backward)
    place = jnp.stack(
        [ring * wide_count + quarter * own_rows - HALO, jnp.int32(row_count * bands)]
    ).astype(jnp.int32)
    copies = pl.pallas_call(
        stencil_kernel,
        out_shape=jax.ShapeDtypeStruct((peers, piece_rows + 16, 128), jnp.int16),
        in_specs=[scalars] + [whole] * 6,
        out_specs=anywhere,
        scratch_shapes=[
            pltpu.VMEM((piece_rows, 128), jnp.int16),
            pltpu.VMEM((peers, 16, 128), jnp.int16),
            pltpu.SemaphoreType.DMA((peers + 1,)),
        ],
        compiler_params=roomy,
    )(place, own, before, after, wide_wind, gains, values)

    adjoint_all = swapped(copies, "mem", 0)
    projected, tiles = pl.pallas_call(
        project_kernel,
        out_shape=[
            jax.ShapeDtypeStruct((rings, repeats * wide_count + 16, coarse_lons), jnp.int16),
            jax.ShapeDtypeStruct((sides, levels_here, row_count, col_count), jnp.float32),
        ],
        in_specs=[scalars, whole] + [anywhere] * 3,
        out_specs=[anywhere, whole],
        scratch_shapes=[
            whole_lon,
            half_members,
            half_members,
            pltpu.VMEM((rings, repeats * wide_count + 16, coarse_lons), jnp.int16),
            pltpu.SemaphoreType.DMA((2 * levels_here + 2,)),
        ],
        compiler_params=roomy,
    )(where_side, adjoint_all, lon_matrix, perturbations, other_members)
    by_pair = swapped(projected, "lat_0", 0)
    full = pl.pallas_call(
        functools.partial(gather_kernel, scale),
        out_shape=jax.ShapeDtypeStruct((bands, repeats, coarse_rows, coarse_lons), jnp.float32),
        in_specs=[whole] * 2,
        out_specs=whole,
        compiler_params=roomy,
    )(by_pair, lat_all)
    full = swapped(full, LAT, 0)
    full = full.reshape(
        members_here, rings // members_here, sides, pairs // rings, coarse_rows, coarse_lons
    )
    full = jnp.transpose(full, (4, 0, 2, 1, 3, 5)).reshape(coarse_weights.shape)
    gradient = full + coarse_weights.astype(jnp.float32)

    kept = jnp.where(first, tiles[0], tiles[1])
    sent = jnp.where(first, tiles[1], tiles[0])
    increment = in_order(kept, lax.ppermute(sent, "lat_1", across), 0)
    return (gradient, increment)


def solution(mesh):
    split = Mesh(mesh.devices.reshape(mesh.shape["mem"], 8, 2), ("mem", "lat_0", "lat_1"))
    placed = (
        P(LAT, "mem", None, None),
        P("mem", None, LAT, None),
        P(LAT, None),
        P(),
        P(None, LAT, "mem"),
        P(None, None, LAT, "mem"),
        P(None, None, LAT, "mem"),
        P(None, None, LAT, "mem"),
    )
    return jax.shard_map(
        body,
        mesh=split,
        in_specs=placed,
        out_specs=(P(LAT, "mem", None, None), P(None, LAT, "mem")),
        check_vma=False,
    )
```

```python
import functools

import jax
import jax.numpy as jnp
from jax import lax
from jax.experimental import pallas as pl
from jax.experimental.pallas import tpu as pltpu
from jax.sharding import Mesh
from jax.sharding import PartitionSpec as P

STEPS = 4
OBLK = 8
HALO = 8
LN2 = 0.6931471805599453
STEPS_16 = 32767.0
LAT = ("lat_0", "lat_1")
ALL = ("mem", "lat_0", "lat_1")

def swapped(value, axis, dim):
    return lax.all_to_all(value, axis, split_axis=dim, concat_axis=dim, tiled=True)


def two_terms(value):
    high = value.astype(jnp.bfloat16)
    low = (value - high.astype(jnp.float32)).astype(jnp.bfloat16)
    return jnp.concatenate([high, low], axis=0)


def dot(a, b):
    return jnp.dot(a, b, preferred_element_type=jnp.float32)


def dot_last(a, b):
    return lax.dot_general(a, b, (((1,), (1,)), ((), ())), preferred_element_type=jnp.float32)


def row_codes(value):
    largest = jnp.maximum(jnp.max(jnp.abs(value), axis=1, keepdims=True), 1e-30)
    return jnp.ceil(jnp.log(largest) * (256.0 / LN2)) + 1.0


def code_scale(codes):
    return jnp.exp(codes * (LN2 / 256.0))


def rounded(value, codes):
    return jnp.round(value * (STEPS_16 / code_scale(codes)))


def to_16(value):
    return value.astype(jnp.int32).astype(jnp.int16)


def from_16(value):
    return value.astype(jnp.int32).astype(jnp.float32)


def as_tiles(value):
    rows, cols = value.shape
    return jnp.concatenate(
        [
            value[t * 8 : (t + 1) * 8, at * 128 : (at + 1) * 128]
            for t in range(rows // 8)
            for at in range(cols // 128)
        ],
        axis=0,
    )


def from_tiles(value, row_tiles):
    lane_tiles = value.shape[0] // 8 // row_tiles
    rows = []
    for t in range(row_tiles):
        start = t * lane_tiles * 8
        strips = [value[start + at * 8 : start + (at + 1) * 8] for at in range(lane_tiles)]
        rows.append(jnp.concatenate(strips, axis=1))
    return jnp.concatenate(rows, axis=0)


def tile_scales(codes, lane_tiles):
    scales = code_scale(codes) * (1.0 / STEPS_16)
    parts = []
    for t in range(scales.shape[0] // 8):
        parts += [scales[t * 8 : (t + 1) * 8]] * lane_tiles
    return jnp.concatenate(parts, axis=0)


def member_rows(side, own_ref, other_ref, member, level):
    levels_here = other_ref.shape[1]
    own = own_ref[member, side * levels_here + level].astype(jnp.float32)
    other = other_ref[member, level].astype(jnp.float32)
    low = jnp.where(side == 0, own, other)
    high = jnp.where(side == 0, other, own)
    return jnp.concatenate([low, high], axis=0)


def localize_kernel(place_ref, lon_ref, own_ref, other_ref, *refs):
    block_refs, sum_ref = refs[:-1], refs[-1]
    members, levels_here, row_count, lon_total = other_ref.shape
    tall = 2 * row_count
    side = place_ref[0]
    pairs = members * levels_here
    lat_start = block_refs[0].shape[0] - row_count
    per_block = lat_start // pairs
    coarse_total = per_block * len(block_refs)
    lat = block_refs[0][lat_start:].astype(jnp.float32)
    half = row_count // 2
    columns = jnp.concatenate(
        [
            lat[band * half : (band + 1) * half, part * coarse_total : (part + 1) * coarse_total]
            for band in range(2)
            for part in range(2)
        ],
        axis=0,
    )
    turn = (len(block_refs) - place_ref[1]) * per_block % coarse_total
    columns = pltpu.roll(columns, turn, 1).astype(jnp.bfloat16)
    lon = lon_ref[...]
    for level in range(levels_here):
        narrow = []
        for member in range(members):
            start = (member * levels_here + level) * per_block
            weights = jnp.concatenate([ref[start : start + per_block] for ref in block_refs], axis=0)
            narrow.append(dot(columns, weights))
        localized = dot(two_terms(jnp.concatenate(narrow, axis=0)), lon)
        total = None
        for member in range(members):
            at = member * tall
            term = localized[at : at + tall] + localized[at + members * tall : at + (members + 1) * tall]
            term = term * member_rows(side, own_ref, other_ref, member, level)
            total = term if total is None else total + term
        count = sum_ref.shape[0] // levels_here
        piece_rows = tall // count
        data = piece_rows * lon_total // 128
        codes = row_codes(total)
        total = rounded(total, codes)
        for piece in range(count):
            part = slice(piece * piece_rows, (piece + 1) * piece_rows)
            sum_ref[level * count + piece, :data] = to_16(as_tiles(total[part]))
            sum_ref[level * count + piece, data:] = to_16(
                jnp.broadcast_to(codes[part], (piece_rows, 128))
            )


def add_kernel(scale, message_ref, out_ref):
    sources, rows, _ = message_ref.shape
    own_rows, lon_total = out_ref.shape
    total = None
    for source in range(sources):
        value = from_16(message_ref[source, : rows - own_rows])
        codes = from_16(message_ref[source, rows - own_rows :])
        value = value * tile_scales(codes, lon_total // 128)
        total = value if total is None else total + value
    out_ref[...] = from_tiles(total, own_rows // 8) * scale


def project_kernel(side_ref, adjoint_ref, lon_ref, own_ref, other_ref, out_ref, tile_ref):
    members, levels_here, row_count, lon_total = other_ref.shape
    rings, _, coarse_lons = out_ref.shape
    tall = 2 * row_count
    side = side_ref[0]
    lon = lon_ref[...]
    quarters = adjoint_ref.shape[0] // levels_here
    row_tiles = tall // quarters // 8
    lane_tiles = lon_total // 128
    per_message = members * levels_here // rings
    row = lax.broadcasted_iota(jnp.int32, (tall, 128), 0)
    lane = lax.broadcasted_iota(jnp.int32, (tall, 128), 1)
    tails = [jnp.zeros((1, 128), jnp.float32) for _ in range(rings)]
    for level in range(levels_here):
        strips = []
        for at in range(lane_tiles):
            strips.append(
                jnp.concatenate(
                    [
                        adjoint_ref[
                            level * quarters + q, (t * lane_tiles + at) * 8 : (t * lane_tiles + at + 1) * 8
                        ]
                        for q in range(quarters)
                        for t in range(row_tiles)
                    ],
                    axis=0,
                )
            )
        adjoint = jnp.concatenate(strips, axis=1)
        product = [
            member_rows(side, own_ref, other_ref, member, level) * adjoint for member in range(members)
        ]
        projected = dot_last(two_terms(jnp.concatenate(product, axis=0)), lon)
        for member in range(members):
            at = member * tall
            value = projected[at : at + tall] + projected[at + members * tall : at + (members + 1) * tall]
            pair = member * levels_here + level
            ring, place = pair // per_message, pair % per_message
            codes = row_codes(value)
            whole = jnp.round(value * (STEPS_16 / code_scale(codes))).astype(jnp.int32)
            out_ref[ring, place * tall : (place + 1) * tall] = whole.astype(jnp.int16)
            mark = jnp.where(lane == row + place * tall, codes, 0.0)
            tails[ring] = tails[ring] + jnp.sum(mark, axis=0, keepdims=True)
        for q in range(quarters):
            piece = adjoint_ref[level * quarters + q, row_tiles * lane_tiles * 8 :]
            band, start = q * row_tiles * 8 // row_count, q * row_tiles * 8 % row_count
            width = tile_ref.shape[3]
            tile_ref[band, level, start : start + 8] = piece[:, :width]
            tile_ref[band, level, start + 8 : start + 16] = piece[:, width:]
    data = per_message * tall
    for ring in range(rings):
        tail = jnp.broadcast_to(tails[ring], (16, 128)).astype(jnp.int32).astype(jnp.int16)
        out_ref[ring, data : data + 16] = jnp.concatenate([tail] * (coarse_lons // 128), axis=1)


def gather_kernel(scale, message_ref, lat_ref, out_ref):
    rings, rows, lons = message_ref.shape
    bands, places, coarse_rows, _ = out_ref.shape
    data = rows - 16
    coarse = bands * coarse_rows
    high, low, scales = [], [], []
    for ring in range(rings):
        value = message_ref[ring, :data].astype(jnp.int32).astype(jnp.float32)
        upper = jnp.floor(value * (1.0 / 256.0)) * 256.0
        high.append(upper.astype(jnp.bfloat16))
        low.append((value - upper).astype(jnp.bfloat16))
        codes = message_ref[ring, data:].astype(jnp.int32).astype(jnp.float32)[:1, :data]
        scales.append(code_scale(codes) * (scale / STEPS_16))
    high = jnp.concatenate(high, axis=0)
    low = jnp.concatenate(low, axis=0)
    lat = lat_ref[...].astype(jnp.float32) * jnp.concatenate(scales, axis=1)
    place = lax.broadcasted_iota(jnp.int32, lat.shape, 1) % data // (data // places)
    lat = jnp.concatenate([jnp.where(place == p, lat, 0.0) for p in range(places)], axis=0)
    terms = two_terms(lat)
    total = dot(terms, high)
    total = total[: places * coarse] + (total[places * coarse :] + dot(terms[: places * coarse], low))
    for band in range(bands):
        for p in range(places):
            at = p * coarse + band * coarse_rows
            out_ref[band, p] = total[at : at + coarse_rows]


def pack_kernel(cell_ref, value_ref, weight_ref, wind_ref, out_ref):
    steps, levels, blocks, row_count = cell_ref.shape
    peers, kinds, own_rows, lanes = out_ref.shape
    levels_here = levels // (kinds - 1)
    parts = row_count // own_rows
    filler = jnp.zeros((lanes - 3 * steps * blocks, row_count), jnp.float32)
    winds = jnp.concatenate([wind_ref[0], wind_ref[1]], axis=1)
    for level in range(levels):
        seen = [cell_ref[t, level].astype(jnp.float32) for t in range(steps)]
        seen += [value_ref[t, level] for t in range(steps)]
        seen += [weight_ref[t, level] for t in range(steps)]
        rows = jnp.transpose(jnp.concatenate(seen + [filler], axis=0))
        start, kind = level % levels_here * (peers // levels_here), level // levels_here
        for peer in range(peers // levels_here):
            at = peer % parts * own_rows
            out_ref[start + peer, kind] = rows[at : at + own_rows]
            if kind == 0:
                out_ref[start + peer, kinds - 1] = winds[at : at + own_rows]


def arrange_kernel(side_ref, own_ref, other_ref, out_ref):
    peers, _, row_count, lanes = own_ref.shape
    side = side_ref[0]
    is_own = side_ref[2] == 1
    lane = lax.broadcasted_iota(jnp.int32, (row_count, lanes), 1)
    width = lanes // 2
    pick = lambda peer, which, mine: jnp.where(is_own, own_ref[peer, mine], other_ref[peer, which])
    winds = [pick(peer, 1, 2) for peer in range(peers)]
    seen = [pick(peer, 0, side) for peer in range(peers)]
    lon_total = peers * width
    for at in range(peers // 2):
        even, odd = winds[2 * at], winds[2 * at + 1]
        spot = slice(at * lanes, (at + 1) * lanes)
        out_ref[:, spot] = jnp.where(lane < width, even, pltpu.roll(odd, width, 1))
        spot = slice(lon_total + at * lanes, lon_total + (at + 1) * lanes)
        out_ref[:, spot] = jnp.where(lane < width, pltpu.roll(even, width, 1), odd)
    blocks = lanes // peers
    kinds = (out_ref.shape[1] - 2 * lon_total) // lanes
    owner = lane // blocks
    for kind in range(kinds):
        total = jnp.zeros((row_count, lanes), jnp.float32)
        for peer in range(peers):
            shift = (peer - kind) * blocks % lanes
            value = seen[peer] if shift == 0 else pltpu.roll(seen[peer], shift, 1)
            total = jnp.where(owner == peer, value, total)
        spot = slice(2 * lon_total + kind * lanes, 2 * lon_total + (kind + 1) * lanes)
        out_ref[:, spot] = total


def spread_kernel(before_ref, local_ref, after_ref, wind_ref, gain_ref, value_ref):
    _, rows, cols = wind_ref.shape
    lanes = cols // OBLK
    local = jnp.concatenate([before_ref[...], local_ref[...], after_ref[...]], axis=0)
    wind_ref[0] = local[:, :cols]
    wind_ref[1] = local[:, cols : 2 * cols]
    sights = [local[:, 2 * cols + k * lanes : 2 * cols + (k + 1) * lanes] for k in range(3 * STEPS)]
    cells = jnp.concatenate(sights[:STEPS], axis=0).astype(jnp.bfloat16)
    others = jnp.concatenate(sights[STEPS:], axis=0)
    high = others.astype(jnp.bfloat16)
    rest = others - high.astype(jnp.float32)
    middle = rest.astype(jnp.bfloat16)
    low = (rest - middle.astype(jnp.float32)).astype(jnp.bfloat16)
    block = lax.broadcasted_iota(jnp.int32, (lanes, cols), 0)
    spread = (lax.broadcasted_iota(jnp.int32, (lanes, cols), 1) // OBLK == block).astype(jnp.bfloat16)
    cells = dot(cells, spread)
    wide = dot(high, spread) + (dot(middle, spread) + dot(low, spread))
    offset = lax.broadcasted_iota(jnp.int32, (rows, cols), 1) % OBLK
    offset = offset.astype(jnp.float32)
    for step in range(STEPS):
        value_ref[step] = wide[step * rows : (step + 1) * rows]
        hit = jnp.abs(cells[step * rows : (step + 1) * rows] - offset) < 0.5
        weight = wide[(STEPS + step) * rows : (STEPS + step + 1) * rows]
        gain_ref[step] = jnp.where(hit, weight, 0.0)


def stencil_kernel(place_ref, own_ref, before_ref, after_ref, wind_ref, gain_ref, value_ref, adjoint_ref):
    rows, cols = wind_ref.shape[1:]
    first_row = place_ref[3]
    last_row = place_ref[4]
    state = jnp.concatenate([before_ref[...], own_ref[...], after_ref[...]], axis=0)
    row = lax.broadcasted_iota(jnp.int32, (rows, cols), 0) + first_row
    col = lax.broadcasted_iota(jnp.int32, (rows, cols), 1)
    inside = ((row >= 0) & (row < last_row)).astype(jnp.float32)
    not_first = (col > 0).astype(jnp.float32)
    not_last = (col < cols - 1).astype(jnp.float32)
    lon_wind = 0.5 * wind_ref[0]
    lat_wind = 0.5 * wind_ref[1]

    def north(x):
        return pltpu.roll(x, rows - 1, 0)

    def south(x):
        return pltpu.roll(x, 1, 0)

    def east(x):
        return pltpu.roll(x, cols - 1, 1)

    def west(x):
        return pltpu.roll(x, 1, 1)

    from_north = (0.2 - lat_wind) * inside
    from_south = (0.2 + lat_wind) * inside
    from_east = (0.2 - lon_wind) * inside * not_last
    from_west = (0.2 + lon_wind) * inside * not_first
    centre = 0.2 * inside
    forcings = []
    for step in range(STEPS):
        state = (
            centre * state
            + from_north * north(state)
            + from_south * south(state)
            + from_east * east(state)
            + from_west * west(state)
        )
        forcings.append(gain_ref[step] * (state - value_ref[step]))
    to_south = 0.2 + lat_wind
    to_north = 0.2 - lat_wind
    to_west = (0.2 + lon_wind) * not_first
    to_east = (0.2 - lon_wind) * not_last
    adjoint = None
    for step in reversed(range(STEPS)):
        pushed = forcings[step] if adjoint is None else adjoint + forcings[step]
        adjoint = inside * (
            0.2 * pushed
            + north(to_south * pushed)
            + south(to_north * pushed)
            + east(to_west * pushed)
            + west(to_east * pushed)
        )
    adjoint = adjoint[HALO : rows - HALO]
    row_tiles, lane_tiles = (rows - 2 * HALO) // 8, cols // 128
    packed = jnp.concatenate(
        [
            adjoint[t * 8 : (t + 1) * 8, at * 128 : (at + 1) * 128]
            for t in range(row_tiles)
            for at in range(lane_tiles)
        ],
        axis=0,
    )
    count = adjoint_ref.shape[0]
    width = cols // count
    lane = lax.broadcasted_iota(jnp.int32, (8, 128), 1)
    for copy in range(count):
        adjoint_ref[copy, : row_tiles * lane_tiles * 8] = packed
        strip = slice(copy * width // 128 * 128, copy * width // 128 * 128 + 128)
        top, bottom = own_ref[0:8, strip], own_ref[8:16, strip]
        if copy % 2 == 0:
            piece = jnp.where(lane < width, top, pltpu.roll(bottom, width, 1))
        else:
            piece = jnp.where(lane < width, pltpu.roll(top, width, 1), bottom)
        adjoint_ref[copy, row_tiles * lane_tiles * 8 :] = piece


def body(
    coarse_weights,
    perturbations,
    lat_matrix,
    lon_matrix,
    wind_field,
    observed_cell,
    observed_value,
    observed_weight,
):
    members_here, levels, row_count, lon_total = perturbations.shape
    coarse_rows, _, _, coarse_lons = coarse_weights.shape
    col_count = wind_field.shape[2]
    peers = lax.axis_size("mem")
    rings = lax.axis_size("lat_0")
    sides = lax.axis_size("lat_1")
    bands = rings * sides
    levels_here = levels // sides
    wide_count = row_count * sides
    pairs = members_here * levels_here
    quarters = peers // levels_here
    own_rows = wide_count // quarters
    quarter = lax.axis_index("mem") % quarters
    ring = lax.axis_index("lat_0")
    first = lax.axis_index("lat_1") == 0
    across = [(0, 1), (1, 0)]

    forward = []
    for m in range(peers):
        for z in range(rings):
            for x in range(sides):
                here = (m * rings + z) * sides + x
                if m % quarters < quarters - 1:
                    forward.append((here, here + bands))
                elif z < rings - 1:
                    forward.append((here, here - (quarters - 1) * bands + sides))
    backward = [(b, a) for a, b in forward]

    def halves(value, dim):
        low = lax.slice_in_dim(value, 0, levels_here, axis=dim)
        high = lax.slice_in_dim(value, levels_here, levels, axis=dim)
        return jnp.where(first, low, high), jnp.where(first, high, low)

    def in_order(mine, theirs, dim):
        return jnp.where(
            first, jnp.concatenate([mine, theirs], dim), jnp.concatenate([theirs, mine], dim)
        )

    weight_rows = pairs * coarse_rows
    coarse_total = bands * coarse_rows
    mine, theirs = halves(coarse_weights, 2)
    lat_rows = jnp.concatenate([lat_matrix[: row_count // 2], lat_matrix[row_count // 2 :]], axis=1)

    def by_pair_first(value):
        value = value.reshape(coarse_rows, pairs, coarse_lons)
        return jnp.transpose(value, (1, 0, 2))

    theirs = by_pair_first(theirs).reshape(weight_rows, coarse_lons)
    from_side = lax.ppermute(jnp.concatenate([theirs, lat_rows], axis=0), "lat_1", across)
    both = in_order(
        by_pair_first(mine), from_side[:weight_rows].reshape(pairs, coarse_rows, coarse_lons), 1
    ).reshape(sides * weight_rows, coarse_lons)
    both = jnp.concatenate([both, in_order(lat_rows, from_side[weight_rows:], 0)], axis=0)

    kinds, block_count = 3 * STEPS, observed_cell.shape[3]
    lanes = 2 * col_count
    parts = row_count // own_rows
    whole = pl.BlockSpec(memory_space=pltpu.VMEM)
    roomy = pltpu.CompilerParams(vmem_limit_bytes=24 * 1024 * 1024)
    packed = pl.pallas_call(
        pack_kernel,
        out_shape=jax.ShapeDtypeStruct((peers, sides + 1, own_rows, lanes), jnp.float32),
        in_specs=[whole] * 4,
        out_specs=whole,
        compiler_params=roomy,
    )(
        *[jnp.swapaxes(seen, 2, 3) for seen in (observed_cell, observed_value, observed_weight)],
        wind_field,
    )
    _, packed = lax.optimization_barrier((from_side, packed))
    packed = swapped(packed, "mem", 0)

    side = lax.axis_index("lat_1")
    other_members = lax.dynamic_slice_in_dim(
        perturbations, (1 - side) * levels_here, levels_here, axis=1
    )
    other_members = lax.ppermute(other_members, "lat_1", across)
    up = [(i, (i + 1) % rings) for i in range(rings)]
    down = [(b, a) for a, b in up]
    blocks = {0: both}
    rising = falling = both
    for hop in range(1, rings // 2 + 1):
        rising = lax.ppermute(rising, "lat_0", up)
        if hop < rings - hop:
            falling = lax.ppermute(falling, "lat_0", down)
        if hop == 2:
            rising, falling, packed = lax.optimization_barrier((rising, falling, packed))
            passed = jnp.where(first, packed[:, 1:], jnp.stack([packed[:, 0], packed[:, 2]], axis=1))
            passed = lax.ppermute(passed, "lat_1", across)
        blocks[-hop % rings] = rising
        if hop < rings - hop:
            blocks[hop] = falling

    def lat_of(block):
        rows = block[sides * weight_rows :].reshape(sides, row_count // 2, coarse_lons)
        rows = jnp.concatenate([rows[..., :coarse_total], rows[..., coarse_total:]], 1)
        return rows.reshape(1, wide_count, coarse_total)


    scalars = pl.BlockSpec(memory_space=pltpu.SMEM)
    is_own = (quarter // parts == side).astype(jnp.int32)
    place = jnp.stack(
        [
            side,
            ring,
            is_own,
            ring * wide_count + quarter * own_rows - HALO,
            jnp.int32(row_count * bands),
        ]
    ).astype(jnp.int32)
    piece_rows = own_rows * lon_total // 128 + own_rows
    partial_sum = pl.pallas_call(
        localize_kernel,
        out_shape=jax.ShapeDtypeStruct((peers, piece_rows, 128), jnp.int16),
        in_specs=[scalars] + [whole] * (3 + rings),
        out_specs=whole,
        compiler_params=roomy,
    )(
        place,
        lon_matrix,
        perturbations,
        other_members,
        *[blocks[d] for d in range(rings)],
    )
    partial_sum, packed, passed = lax.optimization_barrier((partial_sum, packed, passed))
    arrived = swapped(partial_sum, "mem", 0)

    local = pl.pallas_call(
        arrange_kernel,
        out_shape=jax.ShapeDtypeStruct(
            (own_rows, 2 * lon_total + kinds * peers * block_count), jnp.float32
        ),
        in_specs=[scalars, whole, whole],
        out_specs=whole,
        compiler_params=roomy,
    )(place, packed, passed)
    local, *tied = lax.optimization_barrier((local, *[blocks[d] for d in range(rings)]))
    lat_ring = jnp.concatenate([lat_of(block) for block in tied], axis=0)
    lat_all = lax.dynamic_slice_in_dim(
        jnp.concatenate([lat_ring, lat_ring], axis=0), rings - ring, rings, axis=0
    )
    repeats = pairs // rings
    lat_all = jnp.broadcast_to(lat_all[:, None], (rings, repeats, wide_count, coarse_total))
    lat_all = jnp.transpose(lat_all.reshape(rings * repeats * wide_count, coarse_total))
    before = lax.ppermute(local[-HALO:], ALL, forward)
    after = lax.ppermute(local[:HALO], ALL, backward)
    wide_rows = own_rows + 2 * HALO
    wide_wind, gains, values = pl.pallas_call(
        spread_kernel,
        out_shape=[
            jax.ShapeDtypeStruct((count, wide_rows, lon_total), jnp.float32)
            for count in (2, STEPS, STEPS)
        ],
        in_specs=[whole] * 3,
        out_specs=[whole] * 3,
        compiler_params=roomy,
    )(before, local, after)

    scale = (members_here * peers - 1) ** -0.5
    own = pl.pallas_call(
        functools.partial(add_kernel, scale),
        out_shape=jax.ShapeDtypeStruct((own_rows, lon_total), jnp.float32),
        in_specs=[whole],
        out_specs=whole,
        compiler_params=roomy,
    )(arrived)

    before = lax.ppermute(own[-HALO:], ALL, forward)
    after = lax.ppermute(own[:HALO], ALL, backward)
    copies = pl.pallas_call(
        stencil_kernel,
        out_shape=jax.ShapeDtypeStruct((peers, own_rows * lon_total // 128 + 8, 128), jnp.float32),
        in_specs=[scalars] + [whole] * 6,
        out_specs=whole,
        compiler_params=roomy,
    )(place, own, before, after, wide_wind, gains, values)

    adjoint_all = swapped(copies, "mem", 0)
    projected, tiles = pl.pallas_call(
        project_kernel,
        out_shape=[
            jax.ShapeDtypeStruct((rings, repeats * wide_count + 16, coarse_lons), jnp.int16),
            jax.ShapeDtypeStruct((sides, levels_here, row_count, col_count), jnp.float32),
        ],
        in_specs=[scalars] + [whole] * 4,
        out_specs=[whole] * 2,
        compiler_params=roomy,
    )(place, adjoint_all, lon_matrix, perturbations, other_members)
    by_pair = swapped(projected, "lat_0", 0)
    full = pl.pallas_call(
        functools.partial(gather_kernel, scale),
        out_shape=jax.ShapeDtypeStruct((bands, repeats, coarse_rows, coarse_lons), jnp.float32),
        in_specs=[whole] * 2,
        out_specs=whole,
        compiler_params=roomy,
    )(by_pair, lat_all)
    full = swapped(full, LAT, 0)
    full = full.reshape(
        members_here, rings // members_here, sides, pairs // rings, coarse_rows, coarse_lons
    )
    full = jnp.transpose(full, (4, 0, 2, 1, 3, 5)).reshape(coarse_weights.shape)
    gradient = full + coarse_weights.astype(jnp.float32)

    kept = jnp.where(first, tiles[0], tiles[1])
    sent = jnp.where(first, tiles[1], tiles[0])
    increment = in_order(kept, lax.ppermute(sent, "lat_1", across), 0)
    return (gradient, increment)


def solution(mesh):
    split = Mesh(mesh.devices.reshape(mesh.shape["mem"], 8, 2), ("mem", "lat_0", "lat_1"))
    placed = (
        P(LAT, "mem", None, None),
        P("mem", None, LAT, None),
        P(LAT, None),
        P(),
        P(None, LAT, "mem"),
        P(None, None, LAT, "mem"),
        P(None, None, LAT, "mem"),
        P(None, None, LAT, "mem"),
    )
    return jax.shard_map(
        body,
        mesh=split,
        in_specs=placed,
        out_specs=(P(LAT, "mem", None, None), P(None, LAT, "mem")),
        check_vma=False,
    )
```

```python
import functools

import jax
import jax.numpy as jnp
from jax import lax
from jax.experimental import pallas as pl
from jax.experimental.pallas import tpu as pltpu
from jax.sharding import Mesh
from jax.sharding import PartitionSpec as P

STEPS = 4
OBLK = 8
HALO = 8
LN2 = 0.6931471805599453
STEPS_16 = 32767.0
LAT = ("lat_0", "lat_1")
ALL = ("mem", "lat_0", "lat_1")

def swapped(value, axis, dim):
    return lax.all_to_all(value, axis, split_axis=dim, concat_axis=dim, tiled=True)


def two_terms(value):
    high = value.astype(jnp.bfloat16)
    low = (value - high.astype(jnp.float32)).astype(jnp.bfloat16)
    return jnp.concatenate([high, low], axis=0)


def dot(a, b):
    return jnp.dot(a, b, preferred_element_type=jnp.float32)


def row_codes(value):
    largest = jnp.maximum(jnp.max(jnp.abs(value), axis=1, keepdims=True), 1e-30)
    return jnp.ceil(jnp.log(largest) * (256.0 / LN2)) + 1.0


def code_scale(codes):
    return jnp.exp(codes * (LN2 / 256.0))


def rounded(value, codes):
    return jnp.round(value * (STEPS_16 / code_scale(codes)))


def to_16(value):
    return value.astype(jnp.int32).astype(jnp.int16)


def from_16(value):
    return value.astype(jnp.int32).astype(jnp.float32)


def as_tiles(value):
    rows, cols = value.shape
    return jnp.concatenate(
        [
            value[t * 8 : (t + 1) * 8, at * 128 : (at + 1) * 128]
            for t in range(rows // 8)
            for at in range(cols // 128)
        ],
        axis=0,
    )


def from_tiles(value, row_tiles):
    lane_tiles = value.shape[0] // 8 // row_tiles
    rows = []
    for t in range(row_tiles):
        start = t * lane_tiles * 8
        strips = [value[start + at * 8 : start + (at + 1) * 8] for at in range(lane_tiles)]
        rows.append(jnp.concatenate(strips, axis=1))
    return jnp.concatenate(rows, axis=0)


def tile_scales(codes, lane_tiles):
    scales = code_scale(codes) * (1.0 / STEPS_16)
    parts = []
    for t in range(scales.shape[0] // 8):
        parts += [scales[t * 8 : (t + 1) * 8]] * lane_tiles
    return jnp.concatenate(parts, axis=0)


def member_rows(side, own_ref, other_ref, member, level):
    levels_here = other_ref.shape[1]
    own = own_ref[member, side * levels_here + level].astype(jnp.float32)
    other = other_ref[member, level].astype(jnp.float32)
    low = jnp.where(side == 0, own, other)
    high = jnp.where(side == 0, other, own)
    return jnp.concatenate([low, high], axis=0)


def localize_kernel(side_ref, columns_ref, lon_ref, own_ref, other_ref, *refs):
    block_refs, sum_ref = refs[:-1], refs[-1]
    members, levels_here, row_count, lon_total = other_ref.shape
    tall = 2 * row_count
    side = side_ref[0]
    per_block = columns_ref.shape[1] // len(block_refs)
    columns = columns_ref[...]
    lon = lon_ref[...]
    for level in range(levels_here):
        narrow = []
        for member in range(members):
            start = (member * levels_here + level) * per_block
            weights = jnp.concatenate([ref[start : start + per_block] for ref in block_refs], axis=0)
            narrow.append(dot(columns, weights))
        localized = dot(two_terms(jnp.concatenate(narrow, axis=0)), lon)
        total = None
        for member in range(members):
            at = member * tall
            term = localized[at : at + tall] + localized[at + members * tall : at + (members + 1) * tall]
            term = term * member_rows(side, own_ref, other_ref, member, level)
            total = term if total is None else total + term
        count = sum_ref.shape[0] // levels_here
        piece_rows = tall // count
        data = piece_rows * lon_total // 128
        codes = row_codes(total)
        total = rounded(total, codes)
        for piece in range(count):
            part = slice(piece * piece_rows, (piece + 1) * piece_rows)
            sum_ref[level * count + piece, :data] = to_16(as_tiles(total[part]))
            sum_ref[level * count + piece, data:] = to_16(
                jnp.broadcast_to(codes[part], (piece_rows, 128))
            )


def add_kernel(scale, message_ref, out_ref):
    sources, rows, _ = message_ref.shape
    own_rows, lon_total = out_ref.shape
    total = None
    for source in range(sources):
        value = from_16(message_ref[source, : rows - own_rows])
        codes = from_16(message_ref[source, rows - own_rows :])
        value = value * tile_scales(codes, lon_total // 128)
        total = value if total is None else total + value
    out_ref[...] = from_tiles(total, own_rows // 8) * scale


def project_kernel(side_ref, adjoint_ref, lon_ref, own_ref, other_ref, out_ref, tile_ref):
    members, levels_here, row_count, lon_total = other_ref.shape
    rings, _, coarse_lons = out_ref.shape
    tall = 2 * row_count
    side = side_ref[0]
    lon = lon_ref[...]
    quarters = adjoint_ref.shape[0] // levels_here
    row_tiles = tall // quarters // 8
    lane_tiles = lon_total // 128
    per_message = members * levels_here // rings
    row = lax.broadcasted_iota(jnp.int32, (tall, 128), 0)
    lane = lax.broadcasted_iota(jnp.int32, (tall, 128), 1)
    tails = [jnp.zeros((1, 128), jnp.float32) for _ in range(rings)]
    for level in range(levels_here):
        strips = []
        for at in range(lane_tiles):
            strips.append(
                jnp.concatenate(
                    [
                        adjoint_ref[
                            level * quarters + q, (t * lane_tiles + at) * 8 : (t * lane_tiles + at + 1) * 8
                        ]
                        for q in range(quarters)
                        for t in range(row_tiles)
                    ],
                    axis=0,
                )
            )
        adjoint = jnp.concatenate(strips, axis=1)
        product = [
            member_rows(side, own_ref, other_ref, member, level) * adjoint for member in range(members)
        ]
        projected = dot(two_terms(jnp.concatenate(product, axis=0)), lon)
        for member in range(members):
            at = member * tall
            value = projected[at : at + tall] + projected[at + members * tall : at + (members + 1) * tall]
            pair = member * levels_here + level
            ring, place = pair // per_message, pair % per_message
            codes = row_codes(value)
            whole = jnp.round(value * (STEPS_16 / code_scale(codes))).astype(jnp.int32)
            out_ref[ring, place * tall : (place + 1) * tall] = whole.astype(jnp.int16)
            mark = jnp.where(lane == row + place * tall, codes, 0.0)
            tails[ring] = tails[ring] + jnp.sum(mark, axis=0, keepdims=True)
        for q in range(quarters):
            piece = adjoint_ref[level * quarters + q, row_tiles * lane_tiles * 8 :]
            band, start = q * row_tiles * 8 // row_count, q * row_tiles * 8 % row_count
            width = tile_ref.shape[3]
            tile_ref[band, level, start : start + 8] = piece[:, :width]
            tile_ref[band, level, start + 8 : start + 16] = piece[:, width:]
    data = per_message * tall
    for ring in range(rings):
        tail = jnp.broadcast_to(tails[ring], (16, 128)).astype(jnp.int32).astype(jnp.int16)
        out_ref[ring, data : data + 16] = jnp.concatenate([tail] * (coarse_lons // 128), axis=1)


def gather_kernel(scale, message_ref, lat_ref, out_ref):
    rings, rows, lons = message_ref.shape
    bands, places, coarse_rows, _ = out_ref.shape
    data = rows - 16
    coarse = bands * coarse_rows
    high, low, scales = [], [], []
    for ring in range(rings):
        value = message_ref[ring, :data].astype(jnp.int32).astype(jnp.float32)
        upper = jnp.floor(value * (1.0 / 256.0)) * 256.0
        high.append(upper.astype(jnp.bfloat16))
        low.append((value - upper).astype(jnp.bfloat16))
        codes = message_ref[ring, data:].astype(jnp.int32).astype(jnp.float32)[:1, :data]
        scales.append(code_scale(codes) * (scale / STEPS_16))
    high = jnp.concatenate(high, axis=0)
    low = jnp.concatenate(low, axis=0)
    lat = lat_ref[...].astype(jnp.float32) * jnp.concatenate(scales, axis=1)
    place = lax.broadcasted_iota(jnp.int32, lat.shape, 1) % data // (data // places)
    lat = jnp.concatenate([jnp.where(place == p, lat, 0.0) for p in range(places)], axis=0)
    terms = two_terms(lat)
    total = dot(terms, high)
    total = total[: places * coarse] + (total[places * coarse :] + dot(terms[: places * coarse], low))
    for band in range(bands):
        for p in range(places):
            at = p * coarse + band * coarse_rows
            out_ref[band, p] = total[at : at + coarse_rows]


def arrange_kernel(side_ref, own_ref, other_ref, out_ref):
    peers, _, row_count, lanes = own_ref.shape
    side = side_ref[0]
    is_own = side_ref[1] == 1
    lane = lax.broadcasted_iota(jnp.int32, (row_count, lanes), 1)
    width = lanes // 2
    pick = lambda peer, which, mine: jnp.where(is_own, own_ref[peer, mine], other_ref[peer, which])
    winds = [pick(peer, 1, 2) for peer in range(peers)]
    seen = [pick(peer, 0, side) for peer in range(peers)]
    lon_total = peers * width
    for at in range(peers // 2):
        even, odd = winds[2 * at], winds[2 * at + 1]
        spot = slice(at * lanes, (at + 1) * lanes)
        out_ref[:, spot] = jnp.where(lane < width, even, pltpu.roll(odd, width, 1))
        spot = slice(lon_total + at * lanes, lon_total + (at + 1) * lanes)
        out_ref[:, spot] = jnp.where(lane < width, pltpu.roll(even, width, 1), odd)
    blocks = lanes // peers
    kinds = (out_ref.shape[1] - 2 * lon_total) // lanes
    owner = lane // blocks
    for kind in range(kinds):
        total = jnp.zeros((row_count, lanes), jnp.float32)
        for peer in range(peers):
            shift = (peer - kind) * blocks % lanes
            value = seen[peer] if shift == 0 else pltpu.roll(seen[peer], shift, 1)
            total = jnp.where(owner == peer, value, total)
        spot = slice(2 * lon_total + kind * lanes, 2 * lon_total + (kind + 1) * lanes)
        out_ref[:, spot] = total


def spread_kernel(before_ref, local_ref, after_ref, wind_ref, gain_ref, value_ref):
    _, rows, cols = wind_ref.shape
    lanes = cols // OBLK
    local = jnp.concatenate([before_ref[...], local_ref[...], after_ref[...]], axis=0)
    wind_ref[0] = local[:, :cols]
    wind_ref[1] = local[:, cols : 2 * cols]
    sights = [local[:, 2 * cols + k * lanes : 2 * cols + (k + 1) * lanes] for k in range(3 * STEPS)]
    cells = jnp.concatenate(sights[:STEPS], axis=0).astype(jnp.bfloat16)
    others = jnp.concatenate(sights[STEPS:], axis=0)
    high = others.astype(jnp.bfloat16)
    rest = others - high.astype(jnp.float32)
    middle = rest.astype(jnp.bfloat16)
    low = (rest - middle.astype(jnp.float32)).astype(jnp.bfloat16)
    block = lax.broadcasted_iota(jnp.int32, (lanes, cols), 0)
    spread = (lax.broadcasted_iota(jnp.int32, (lanes, cols), 1) // OBLK == block).astype(jnp.bfloat16)
    cells = dot(cells, spread)
    wide = dot(high, spread) + (dot(middle, spread) + dot(low, spread))
    offset = lax.broadcasted_iota(jnp.int32, (rows, cols), 1) % OBLK
    offset = offset.astype(jnp.float32)
    for step in range(STEPS):
        value_ref[step] = wide[step * rows : (step + 1) * rows]
        hit = jnp.abs(cells[step * rows : (step + 1) * rows] - offset) < 0.5
        weight = wide[(STEPS + step) * rows : (STEPS + step + 1) * rows]
        gain_ref[step] = jnp.where(hit, weight, 0.0)


def stencil_kernel(place_ref, own_ref, before_ref, after_ref, wind_ref, gain_ref, value_ref, adjoint_ref):
    rows, cols = wind_ref.shape[1:]
    first_row = place_ref[0]
    last_row = place_ref[1]
    state = jnp.concatenate([before_ref[...], own_ref[...], after_ref[...]], axis=0)
    row = lax.broadcasted_iota(jnp.int32, (rows, cols), 0) + first_row
    col = lax.broadcasted_iota(jnp.int32, (rows, cols), 1)
    inside = ((row >= 0) & (row < last_row)).astype(jnp.float32)
    not_first = (col > 0).astype(jnp.float32)
    not_last = (col < cols - 1).astype(jnp.float32)
    lon_wind = 0.5 * wind_ref[0]
    lat_wind = 0.5 * wind_ref[1]

    def north(x):
        return pltpu.roll(x, rows - 1, 0)

    def south(x):
        return pltpu.roll(x, 1, 0)

    def east(x):
        return pltpu.roll(x, cols - 1, 1)

    def west(x):
        return pltpu.roll(x, 1, 1)

    from_north = (0.2 - lat_wind) * inside
    from_south = (0.2 + lat_wind) * inside
    from_east = (0.2 - lon_wind) * inside * not_last
    from_west = (0.2 + lon_wind) * inside * not_first
    centre = 0.2 * inside
    forcings = []
    for step in range(STEPS):
        state = (
            centre * state
            + from_north * north(state)
            + from_south * south(state)
            + from_east * east(state)
            + from_west * west(state)
        )
        forcings.append(gain_ref[step] * (state - value_ref[step]))
    to_south = 0.2 + lat_wind
    to_north = 0.2 - lat_wind
    to_west = (0.2 + lon_wind) * not_first
    to_east = (0.2 - lon_wind) * not_last
    adjoint = None
    for step in reversed(range(STEPS)):
        pushed = forcings[step] if adjoint is None else adjoint + forcings[step]
        adjoint = inside * (
            0.2 * pushed
            + north(to_south * pushed)
            + south(to_north * pushed)
            + east(to_west * pushed)
            + west(to_east * pushed)
        )
    adjoint = adjoint[HALO : rows - HALO]
    row_tiles, lane_tiles = (rows - 2 * HALO) // 8, cols // 128
    packed = jnp.concatenate(
        [
            adjoint[t * 8 : (t + 1) * 8, at * 128 : (at + 1) * 128]
            for t in range(row_tiles)
            for at in range(lane_tiles)
        ],
        axis=0,
    )
    count = adjoint_ref.shape[0]
    width = cols // count
    lane = lax.broadcasted_iota(jnp.int32, (8, 128), 1)
    for copy in range(count):
        adjoint_ref[copy, : row_tiles * lane_tiles * 8] = packed
        strip = slice(copy * width // 128 * 128, copy * width // 128 * 128 + 128)
        top, bottom = own_ref[0:8, strip], own_ref[8:16, strip]
        if copy % 2 == 0:
            piece = jnp.where(lane < width, top, pltpu.roll(bottom, width, 1))
        else:
            piece = jnp.where(lane < width, pltpu.roll(top, width, 1), bottom)
        adjoint_ref[copy, row_tiles * lane_tiles * 8 :] = piece


def body(
    coarse_weights,
    perturbations,
    lat_matrix,
    lon_matrix,
    wind_field,
    observed_cell,
    observed_value,
    observed_weight,
):
    members_here, levels, row_count, lon_total = perturbations.shape
    coarse_rows, _, _, coarse_lons = coarse_weights.shape
    col_count = wind_field.shape[2]
    peers = lax.axis_size("mem")
    rings = lax.axis_size("lat_0")
    sides = lax.axis_size("lat_1")
    bands = rings * sides
    levels_here = levels // sides
    wide_count = row_count * sides
    pairs = members_here * levels_here
    quarters = peers // levels_here
    own_rows = wide_count // quarters
    quarter = lax.axis_index("mem") % quarters
    ring = lax.axis_index("lat_0")
    first = lax.axis_index("lat_1") == 0
    across = [(0, 1), (1, 0)]

    forward = []
    for m in range(peers):
        for z in range(rings):
            for x in range(sides):
                here = (m * rings + z) * sides + x
                if m % quarters < quarters - 1:
                    forward.append((here, here + bands))
                elif z < rings - 1:
                    forward.append((here, here - (quarters - 1) * bands + sides))
    backward = [(b, a) for a, b in forward]

    def halves(value, dim):
        low = lax.slice_in_dim(value, 0, levels_here, axis=dim)
        high = lax.slice_in_dim(value, levels_here, levels, axis=dim)
        return jnp.where(first, low, high), jnp.where(first, high, low)

    def in_order(mine, theirs, dim):
        return jnp.where(
            first, jnp.concatenate([mine, theirs], dim), jnp.concatenate([theirs, mine], dim)
        )

    weight_rows = pairs * coarse_rows
    coarse_total = bands * coarse_rows
    mine, theirs = halves(coarse_weights, 2)
    lat_rows = jnp.concatenate([lat_matrix[: row_count // 2], lat_matrix[row_count // 2 :]], axis=1)

    def by_pair_first(value):
        value = value.reshape(coarse_rows, pairs, coarse_lons)
        return jnp.transpose(value, (1, 0, 2))

    theirs = by_pair_first(theirs).reshape(weight_rows, coarse_lons)
    from_side = lax.ppermute(jnp.concatenate([theirs, lat_rows], axis=0), "lat_1", across)
    both = in_order(
        by_pair_first(mine), from_side[:weight_rows].reshape(pairs, coarse_rows, coarse_lons), 1
    ).reshape(sides * weight_rows, coarse_lons)
    both = jnp.concatenate([both, in_order(lat_rows, from_side[weight_rows:], 0)], axis=0)

    packed = jnp.concatenate(
        [observed_cell.astype(jnp.float32), observed_value, observed_weight], axis=0
    )
    kinds, _, _, block_count = packed.shape
    lanes = 2 * col_count
    packed = jnp.transpose(packed, (1, 2, 0, 3)).reshape(levels, row_count, kinds * block_count)
    packed = jnp.pad(packed, ((0, 0), (0, 0), (0, lanes - kinds * block_count)))
    winds = jnp.transpose(wind_field, (1, 0, 2)).reshape(1, row_count, lanes)
    parts = row_count // own_rows
    packed = packed.reshape(sides, levels_here, 1, parts, own_rows, lanes)
    winds = jnp.broadcast_to(
        winds.reshape(1, 1, 1, parts, own_rows, lanes), (1, levels_here, 1, parts, own_rows, lanes)
    )
    packed = jnp.transpose(jnp.concatenate([packed, winds], axis=0), (1, 2, 3, 0, 4, 5))
    packed = jnp.broadcast_to(
        packed, (levels_here, quarters // parts, parts, sides + 1, own_rows, lanes)
    )
    packed = swapped(packed.reshape(peers, sides + 1, own_rows, lanes), "mem", 0)

    side = lax.axis_index("lat_1")
    other_members = lax.dynamic_slice_in_dim(
        perturbations, (1 - side) * levels_here, levels_here, axis=1
    )
    other_members = lax.ppermute(other_members, "lat_1", across)
    up = [(i, (i + 1) % rings) for i in range(rings)]
    down = [(b, a) for a, b in up]
    blocks = {0: both}
    rising = falling = both
    for hop in range(1, rings // 2 + 1):
        rising = lax.ppermute(rising, "lat_0", up)
        if hop < rings - hop:
            falling = lax.ppermute(falling, "lat_0", down)
        if hop == 2:
            rising, falling, packed = lax.optimization_barrier((rising, falling, packed))
            passed = jnp.where(first, packed[:, 1:], jnp.stack([packed[:, 0], packed[:, 2]], axis=1))
            passed = lax.ppermute(passed, "lat_1", across)
        blocks[-hop % rings] = rising
        if hop < rings - hop:
            blocks[hop] = falling

    def lat_of(block):
        rows = block[sides * weight_rows :].reshape(sides, row_count // 2, coarse_lons)
        rows = jnp.concatenate([rows[..., :coarse_total], rows[..., coarse_total:]], 1)
        return rows.reshape(1, wide_count, coarse_total)

    columns = lat_of(both)[0].reshape(wide_count, rings, sides * coarse_rows)
    columns = lax.dynamic_slice_in_dim(
        jnp.concatenate([columns, columns], axis=1), ring, rings, axis=1
    ).reshape(wide_count, coarse_total)

    scalars = pl.BlockSpec(memory_space=pltpu.SMEM)
    whole = pl.BlockSpec(memory_space=pltpu.VMEM)
    roomy = pltpu.CompilerParams(vmem_limit_bytes=48 * 1024 * 1024)
    where_side = jnp.reshape(side, (1,)).astype(jnp.int32)
    piece_rows = own_rows * lon_total // 128 + own_rows
    partial_sum = pl.pallas_call(
        localize_kernel,
        out_shape=jax.ShapeDtypeStruct((peers, piece_rows, 128), jnp.int16),
        in_specs=[scalars] + [whole] * (4 + rings),
        out_specs=whole,
        compiler_params=roomy,
    )(
        where_side,
        columns,
        lon_matrix,
        perturbations,
        other_members,
        *[blocks[d] for d in range(rings)],
    )
    partial_sum, packed, passed = lax.optimization_barrier((partial_sum, packed, passed))
    arrived = swapped(partial_sum, "mem", 0)

    is_own = (quarter // parts == side).astype(jnp.int32)
    local = pl.pallas_call(
        arrange_kernel,
        out_shape=jax.ShapeDtypeStruct(
            (own_rows, 2 * lon_total + kinds * peers * block_count), jnp.float32
        ),
        in_specs=[scalars, whole, whole],
        out_specs=whole,
        compiler_params=roomy,
    )(jnp.stack([side.astype(jnp.int32), is_own]), packed, passed)
    local, *tied = lax.optimization_barrier((local, *[blocks[d] for d in range(rings)]))
    lat_ring = jnp.concatenate([lat_of(block) for block in tied], axis=0)
    lat_all = lax.dynamic_slice_in_dim(
        jnp.concatenate([lat_ring, lat_ring], axis=0), rings - ring, rings, axis=0
    )
    repeats = pairs // rings
    lat_all = jnp.broadcast_to(lat_all[:, None], (rings, repeats, wide_count, coarse_total))
    lat_all = jnp.transpose(lat_all.reshape(rings * repeats * wide_count, coarse_total))
    before = lax.ppermute(local[-HALO:], ALL, forward)
    after = lax.ppermute(local[:HALO], ALL, backward)
    wide_rows = own_rows + 2 * HALO
    wide_wind, gains, values = pl.pallas_call(
        spread_kernel,
        out_shape=[
            jax.ShapeDtypeStruct((count, wide_rows, lon_total), jnp.float32)
            for count in (2, STEPS, STEPS)
        ],
        in_specs=[whole] * 3,
        out_specs=[whole] * 3,
        compiler_params=roomy,
    )(before, local, after)

    scale = (members_here * peers - 1) ** -0.5
    own = pl.pallas_call(
        functools.partial(add_kernel, scale),
        out_shape=jax.ShapeDtypeStruct((own_rows, lon_total), jnp.float32),
        in_specs=[whole],
        out_specs=whole,
        compiler_params=roomy,
    )(arrived)

    before = lax.ppermute(own[-HALO:], ALL, forward)
    after = lax.ppermute(own[:HALO], ALL, backward)
    place = jnp.stack(
        [ring * wide_count + quarter * own_rows - HALO, jnp.int32(row_count * bands)]
    ).astype(jnp.int32)
    copies = pl.pallas_call(
        stencil_kernel,
        out_shape=jax.ShapeDtypeStruct((peers, own_rows * lon_total // 128 + 8, 128), jnp.float32),
        in_specs=[scalars] + [whole] * 6,
        out_specs=whole,
        compiler_params=roomy,
    )(place, own, before, after, wide_wind, gains, values)

    adjoint_all = swapped(copies, "mem", 0)
    projected, tiles = pl.pallas_call(
        project_kernel,
        out_shape=[
            jax.ShapeDtypeStruct((rings, repeats * wide_count + 16, coarse_lons), jnp.int16),
            jax.ShapeDtypeStruct((sides, levels_here, row_count, col_count), jnp.float32),
        ],
        in_specs=[scalars] + [whole] * 4,
        out_specs=[whole] * 2,
        compiler_params=roomy,
    )(where_side, adjoint_all, jnp.transpose(lon_matrix), perturbations, other_members)
    by_pair = swapped(projected, "lat_0", 0)
    full = pl.pallas_call(
        functools.partial(gather_kernel, scale),
        out_shape=jax.ShapeDtypeStruct((bands, repeats, coarse_rows, coarse_lons), jnp.float32),
        in_specs=[whole] * 2,
        out_specs=whole,
        compiler_params=roomy,
    )(by_pair, lat_all)
    full = swapped(full, LAT, 0)
    full = full.reshape(
        members_here, rings // members_here, sides, pairs // rings, coarse_rows, coarse_lons
    )
    full = jnp.transpose(full, (4, 0, 2, 1, 3, 5)).reshape(coarse_weights.shape)
    gradient = full + coarse_weights.astype(jnp.float32)

    kept = jnp.where(first, tiles[0], tiles[1])
    sent = jnp.where(first, tiles[1], tiles[0])
    increment = in_order(kept, lax.ppermute(sent, "lat_1", across), 0)
    return (gradient, increment)


def solution(mesh):
    split = Mesh(mesh.devices.reshape(mesh.shape["mem"], 8, 2), ("mem", "lat_0", "lat_1"))
    placed = (
        P(LAT, "mem", None, None),
        P("mem", None, LAT, None),
        P(LAT, None),
        P(),
        P(None, LAT, "mem"),
        P(None, None, LAT, "mem"),
        P(None, None, LAT, "mem"),
        P(None, None, LAT, "mem"),
    )
    return jax.shard_map(
        body,
        mesh=split,
        in_specs=placed,
        out_specs=(P(LAT, "mem", None, None), P(None, LAT, "mem")),
        check_vma=False,
    )
```

```python
import functools

import jax
import jax.numpy as jnp
from jax import lax
from jax.experimental import pallas as pl
from jax.experimental.pallas import tpu as pltpu
from jax.sharding import Mesh
from jax.sharding import PartitionSpec as P

STEPS = 4
OBLK = 8
HALO = 8
LN2 = 0.6931471805599453
STEPS_16 = 32767.0
LAT = ("lat_0", "lat_1")
ALL = ("mem", "lat_0", "lat_1")

def swapped(value, axis, dim):
    return lax.all_to_all(value, axis, split_axis=dim, concat_axis=dim, tiled=True)


def two_terms(value):
    high = value.astype(jnp.bfloat16)
    low = (value - high.astype(jnp.float32)).astype(jnp.bfloat16)
    return jnp.concatenate([high, low], axis=0)


def dot(a, b):
    return jnp.dot(a, b, preferred_element_type=jnp.float32)


def row_codes(value):
    largest = jnp.maximum(jnp.max(jnp.abs(value), axis=1, keepdims=True), 1e-30)
    return jnp.ceil(jnp.log(largest) * (256.0 / LN2)) + 1.0


def code_scale(codes):
    return jnp.exp(codes * (LN2 / 256.0))


def rounded(value, codes):
    return jnp.round(value * (STEPS_16 / code_scale(codes)))


def to_16(value):
    return value.astype(jnp.int32).astype(jnp.int16)


def from_16(value):
    return value.astype(jnp.int32).astype(jnp.float32)


def as_tiles(value):
    rows, cols = value.shape
    return jnp.concatenate(
        [
            value[t * 8 : (t + 1) * 8, at * 128 : (at + 1) * 128]
            for t in range(rows // 8)
            for at in range(cols // 128)
        ],
        axis=0,
    )


def from_tiles(value, row_tiles):
    lane_tiles = value.shape[0] // 8 // row_tiles
    rows = []
    for t in range(row_tiles):
        start = t * lane_tiles * 8
        strips = [value[start + at * 8 : start + (at + 1) * 8] for at in range(lane_tiles)]
        rows.append(jnp.concatenate(strips, axis=1))
    return jnp.concatenate(rows, axis=0)


def tile_scales(codes, lane_tiles):
    scales = code_scale(codes) * (1.0 / STEPS_16)
    parts = []
    for t in range(scales.shape[0] // 8):
        parts += [scales[t * 8 : (t + 1) * 8]] * lane_tiles
    return jnp.concatenate(parts, axis=0)


def member_rows(side, own_ref, other_ref, member, level):
    levels_here = other_ref.shape[1]
    own = own_ref[member, side * levels_here + level].astype(jnp.float32)
    other = other_ref[member, level].astype(jnp.float32)
    low = jnp.where(side == 0, own, other)
    high = jnp.where(side == 0, other, own)
    return jnp.concatenate([low, high], axis=0)


def localize_kernel(side_ref, columns_ref, lon_ref, own_ref, other_ref, *refs):
    block_refs, sum_ref, lat_ref = refs[:-2], refs[-2], refs[-1]
    members, levels_here, row_count, lon_total = other_ref.shape
    tall = 2 * row_count
    side = side_ref[0]
    per_block = columns_ref.shape[1] // len(block_refs)
    columns = columns_ref[...]
    lon = lon_ref[...]
    for level in range(levels_here):
        narrow = []
        for member in range(members):
            start = (member * levels_here + level) * per_block
            weights = jnp.concatenate([ref[start : start + per_block] for ref in block_refs], axis=0)
            narrow.append(dot(columns, weights))
        localized = dot(two_terms(jnp.concatenate(narrow, axis=0)), lon)
        total = None
        for member in range(members):
            at = member * tall
            term = localized[at : at + tall] + localized[at + members * tall : at + (members + 1) * tall]
            term = term * member_rows(side, own_ref, other_ref, member, level)
            total = term if total is None else total + term
        count = sum_ref.shape[0] // levels_here
        piece_rows = tall // count
        data = piece_rows * lon_total // 128
        codes = row_codes(total)
        total = rounded(total, codes)
        for piece in range(count):
            part = slice(piece * piece_rows, (piece + 1) * piece_rows)
            sum_ref[level * count + piece, :data] = to_16(as_tiles(total[part]))
            sum_ref[level * count + piece, data:] = to_16(
                jnp.broadcast_to(codes[part], (piece_rows, 128))
            )
    half = row_count // 2
    for at, ref in enumerate(block_refs):
        lat = ref[ref.shape[0] - row_count :]
        for part in range(4):
            rows = lat[part // 2 * half : (part // 2 + 1) * half]
            lat_ref[at, part * half : (part + 1) * half] = rows[
                :, part % 2 * lat_ref.shape[2] : (part % 2 + 1) * lat_ref.shape[2]
            ]


def add_kernel(scale, message_ref, out_ref):
    sources, rows, _ = message_ref.shape
    own_rows, lon_total = out_ref.shape
    total = None
    for source in range(sources):
        value = from_16(message_ref[source, : rows - own_rows])
        codes = from_16(message_ref[source, rows - own_rows :])
        value = value * tile_scales(codes, lon_total // 128)
        total = value if total is None else total + value
    out_ref[...] = from_tiles(total, own_rows // 8) * scale


def project_kernel(side_ref, adjoint_ref, lon_ref, own_ref, other_ref, out_ref, tile_ref):
    members, levels_here, row_count, lon_total = other_ref.shape
    rings, _, coarse_lons = out_ref.shape
    tall = 2 * row_count
    side = side_ref[0]
    lon = lon_ref[...]
    quarters = adjoint_ref.shape[0] // levels_here
    row_tiles = tall // quarters // 8
    lane_tiles = lon_total // 128
    per_message = members * levels_here // rings
    row = lax.broadcasted_iota(jnp.int32, (tall, 128), 0)
    lane = lax.broadcasted_iota(jnp.int32, (tall, 128), 1)
    tails = [jnp.zeros((1, 128), jnp.float32) for _ in range(rings)]
    for level in range(levels_here):
        strips = []
        for at in range(lane_tiles):
            strips.append(
                jnp.concatenate(
                    [
                        adjoint_ref[
                            level * quarters + q, (t * lane_tiles + at) * 8 : (t * lane_tiles + at + 1) * 8
                        ]
                        for q in range(quarters)
                        for t in range(row_tiles)
                    ],
                    axis=0,
                )
            )
        adjoint = jnp.concatenate(strips, axis=1)
        product = [
            member_rows(side, own_ref, other_ref, member, level) * adjoint for member in range(members)
        ]
        projected = dot(two_terms(jnp.concatenate(product, axis=0)), lon)
        for member in range(members):
            at = member * tall
            value = projected[at : at + tall] + projected[at + members * tall : at + (members + 1) * tall]
            pair = member * levels_here + level
            ring, place = pair // per_message, pair % per_message
            codes = row_codes(value)
            whole = jnp.round(value * (STEPS_16 / code_scale(codes))).astype(jnp.int32)
            out_ref[ring, place * tall : (place + 1) * tall] = whole.astype(jnp.int16)
            mark = jnp.where(lane == row + place * tall, codes, 0.0)
            tails[ring] = tails[ring] + jnp.sum(mark, axis=0, keepdims=True)
        for q in range(quarters):
            piece = adjoint_ref[level * quarters + q, row_tiles * lane_tiles * 8 :]
            band, start = q * row_tiles * 8 // row_count, q * row_tiles * 8 % row_count
            width = tile_ref.shape[3]
            tile_ref[band, level, start : start + 8] = piece[:, :width]
            tile_ref[band, level, start + 8 : start + 16] = piece[:, width:]
    data = per_message * tall
    for ring in range(rings):
        tail = jnp.broadcast_to(tails[ring], (16, 128)).astype(jnp.int32).astype(jnp.int16)
        out_ref[ring, data : data + 16] = jnp.concatenate([tail] * (coarse_lons // 128), axis=1)


def gather_kernel(scale, message_ref, lat_ref, out_ref):
    rings, rows, lons = message_ref.shape
    bands, places, coarse_rows, _ = out_ref.shape
    data = rows - 16
    coarse = bands * coarse_rows
    high, low, scales = [], [], []
    for ring in range(rings):
        value = message_ref[ring, :data].astype(jnp.int32).astype(jnp.float32)
        upper = jnp.floor(value * (1.0 / 256.0)) * 256.0
        high.append(upper.astype(jnp.bfloat16))
        low.append((value - upper).astype(jnp.bfloat16))
        codes = message_ref[ring, data:].astype(jnp.int32).astype(jnp.float32)[:1, :data]
        scales.append(code_scale(codes) * (scale / STEPS_16))
    high = jnp.concatenate(high, axis=0)
    low = jnp.concatenate(low, axis=0)
    lat = lat_ref[...].astype(jnp.float32) * jnp.concatenate(scales, axis=1)
    place = lax.broadcasted_iota(jnp.int32, lat.shape, 1) % data // (data // places)
    lat = jnp.concatenate([jnp.where(place == p, lat, 0.0) for p in range(places)], axis=0)
    terms = two_terms(lat)
    total = dot(terms, high)
    total = total[: places * coarse] + (total[places * coarse :] + dot(terms[: places * coarse], low))
    for band in range(bands):
        for p in range(places):
            at = p * coarse + band * coarse_rows
            out_ref[band, p] = total[at : at + coarse_rows]


def arrange_kernel(side_ref, own_ref, other_ref, out_ref):
    peers, _, row_count, lanes = own_ref.shape
    side = side_ref[0]
    is_own = side_ref[1] == 1
    lane = lax.broadcasted_iota(jnp.int32, (row_count, lanes), 1)
    width = lanes // 2
    pick = lambda peer, which, mine: jnp.where(is_own, own_ref[peer, mine], other_ref[peer, which])
    winds = [pick(peer, 1, 2) for peer in range(peers)]
    seen = [pick(peer, 0, side) for peer in range(peers)]
    lon_total = peers * width
    for at in range(peers // 2):
        even, odd = winds[2 * at], winds[2 * at + 1]
        spot = slice(at * lanes, (at + 1) * lanes)
        out_ref[:, spot] = jnp.where(lane < width, even, pltpu.roll(odd, width, 1))
        spot = slice(lon_total + at * lanes, lon_total + (at + 1) * lanes)
        out_ref[:, spot] = jnp.where(lane < width, pltpu.roll(even, width, 1), odd)
    blocks = lanes // peers
    kinds = (out_ref.shape[1] - 2 * lon_total) // lanes
    owner = lane // blocks
    for kind in range(kinds):
        total = jnp.zeros((row_count, lanes), jnp.float32)
        for peer in range(peers):
            shift = (peer - kind) * blocks % lanes
            value = seen[peer] if shift == 0 else pltpu.roll(seen[peer], shift, 1)
            total = jnp.where(owner == peer, value, total)
        spot = slice(2 * lon_total + kind * lanes, 2 * lon_total + (kind + 1) * lanes)
        out_ref[:, spot] = total


def spread_kernel(before_ref, local_ref, after_ref, wind_ref, gain_ref, value_ref):
    _, rows, cols = wind_ref.shape
    lanes = cols // OBLK
    local = jnp.concatenate([before_ref[...], local_ref[...], after_ref[...]], axis=0)
    wind_ref[0] = local[:, :cols]
    wind_ref[1] = local[:, cols : 2 * cols]
    sights = [local[:, 2 * cols + k * lanes : 2 * cols + (k + 1) * lanes] for k in range(3 * STEPS)]
    cells = jnp.concatenate(sights[:STEPS], axis=0).astype(jnp.bfloat16)
    others = jnp.concatenate(sights[STEPS:], axis=0)
    high = others.astype(jnp.bfloat16)
    rest = others - high.astype(jnp.float32)
    middle = rest.astype(jnp.bfloat16)
    low = (rest - middle.astype(jnp.float32)).astype(jnp.bfloat16)
    block = lax.broadcasted_iota(jnp.int32, (lanes, cols), 0)
    spread = (lax.broadcasted_iota(jnp.int32, (lanes, cols), 1) // OBLK == block).astype(jnp.bfloat16)
    cells = dot(cells, spread)
    wide = dot(high, spread) + (dot(middle, spread) + dot(low, spread))
    offset = lax.broadcasted_iota(jnp.int32, (rows, cols), 1) % OBLK
    offset = offset.astype(jnp.float32)
    for step in range(STEPS):
        value_ref[step] = wide[step * rows : (step + 1) * rows]
        hit = jnp.abs(cells[step * rows : (step + 1) * rows] - offset) < 0.5
        weight = wide[(STEPS + step) * rows : (STEPS + step + 1) * rows]
        gain_ref[step] = jnp.where(hit, weight, 0.0)


def stencil_kernel(place_ref, own_ref, before_ref, after_ref, wind_ref, gain_ref, value_ref, adjoint_ref):
    rows, cols = wind_ref.shape[1:]
    first_row = place_ref[0]
    last_row = place_ref[1]
    state = jnp.concatenate([before_ref[...], own_ref[...], after_ref[...]], axis=0)
    row = lax.broadcasted_iota(jnp.int32, (rows, cols), 0) + first_row
    col = lax.broadcasted_iota(jnp.int32, (rows, cols), 1)
    inside = ((row >= 0) & (row < last_row)).astype(jnp.float32)
    not_first = (col > 0).astype(jnp.float32)
    not_last = (col < cols - 1).astype(jnp.float32)
    lon_wind = 0.5 * wind_ref[0]
    lat_wind = 0.5 * wind_ref[1]

    def north(x):
        return pltpu.roll(x, rows - 1, 0)

    def south(x):
        return pltpu.roll(x, 1, 0)

    def east(x):
        return pltpu.roll(x, cols - 1, 1)

    def west(x):
        return pltpu.roll(x, 1, 1)

    from_north = (0.2 - lat_wind) * inside
    from_south = (0.2 + lat_wind) * inside
    from_east = (0.2 - lon_wind) * inside * not_last
    from_west = (0.2 + lon_wind) * inside * not_first
    centre = 0.2 * inside
    forcings = []
    for step in range(STEPS):
        state = (
            centre * state
            + from_north * north(state)
            + from_south * south(state)
            + from_east * east(state)
            + from_west * west(state)
        )
        forcings.append(gain_ref[step] * (state - value_ref[step]))
    to_south = 0.2 + lat_wind
    to_north = 0.2 - lat_wind
    to_west = (0.2 + lon_wind) * not_first
    to_east = (0.2 - lon_wind) * not_last
    adjoint = None
    for step in reversed(range(STEPS)):
        pushed = forcings[step] if adjoint is None else adjoint + forcings[step]
        adjoint = inside * (
            0.2 * pushed
            + north(to_south * pushed)
            + south(to_north * pushed)
            + east(to_west * pushed)
            + west(to_east * pushed)
        )
    adjoint = adjoint[HALO : rows - HALO]
    row_tiles, lane_tiles = (rows - 2 * HALO) // 8, cols // 128
    packed = jnp.concatenate(
        [
            adjoint[t * 8 : (t + 1) * 8, at * 128 : (at + 1) * 128]
            for t in range(row_tiles)
            for at in range(lane_tiles)
        ],
        axis=0,
    )
    count = adjoint_ref.shape[0]
    width = cols // count
    lane = lax.broadcasted_iota(jnp.int32, (8, 128), 1)
    for copy in range(count):
        adjoint_ref[copy, : row_tiles * lane_tiles * 8] = packed
        strip = slice(copy * width // 128 * 128, copy * width // 128 * 128 + 128)
        top, bottom = own_ref[0:8, strip], own_ref[8:16, strip]
        if copy % 2 == 0:
            piece = jnp.where(lane < width, top, pltpu.roll(bottom, width, 1))
        else:
            piece = jnp.where(lane < width, pltpu.roll(top, width, 1), bottom)
        adjoint_ref[copy, row_tiles * lane_tiles * 8 :] = piece


def body(
    coarse_weights,
    perturbations,
    lat_matrix,
    lon_matrix,
    wind_field,
    observed_cell,
    observed_value,
    observed_weight,
):
    members_here, levels, row_count, lon_total = perturbations.shape
    coarse_rows, _, _, coarse_lons = coarse_weights.shape
    col_count = wind_field.shape[2]
    peers = lax.axis_size("mem")
    rings = lax.axis_size("lat_0")
    sides = lax.axis_size("lat_1")
    bands = rings * sides
    levels_here = levels // sides
    wide_count = row_count * sides
    pairs = members_here * levels_here
    quarters = peers // levels_here
    own_rows = wide_count // quarters
    quarter = lax.axis_index("mem") % quarters
    ring = lax.axis_index("lat_0")
    first = lax.axis_index("lat_1") == 0
    across = [(0, 1), (1, 0)]

    forward = []
    for m in range(peers):
        for z in range(rings):
            for x in range(sides):
                here = (m * rings + z) * sides + x
                if m % quarters < quarters - 1:
                    forward.append((here, here + bands))
                elif z < rings - 1:
                    forward.append((here, here - (quarters - 1) * bands + sides))
    backward = [(b, a) for a, b in forward]

    def halves(value, dim):
        low = lax.slice_in_dim(value, 0, levels_here, axis=dim)
        high = lax.slice_in_dim(value, levels_here, levels, axis=dim)
        return jnp.where(first, low, high), jnp.where(first, high, low)

    def in_order(mine, theirs, dim):
        return jnp.where(
            first, jnp.concatenate([mine, theirs], dim), jnp.concatenate([theirs, mine], dim)
        )

    weight_rows = pairs * coarse_rows
    coarse_total = bands * coarse_rows
    mine, theirs = halves(coarse_weights, 2)
    lat_rows = jnp.concatenate([lat_matrix[: row_count // 2], lat_matrix[row_count // 2 :]], axis=1)

    def by_pair_first(value):
        value = value.reshape(coarse_rows, pairs, coarse_lons)
        return jnp.transpose(value, (1, 0, 2))

    theirs = by_pair_first(theirs).reshape(weight_rows, coarse_lons)
    from_side = lax.ppermute(jnp.concatenate([theirs, lat_rows], axis=0), "lat_1", across)
    both = in_order(
        by_pair_first(mine), from_side[:weight_rows].reshape(pairs, coarse_rows, coarse_lons), 1
    ).reshape(sides * weight_rows, coarse_lons)
    both = jnp.concatenate([both, in_order(lat_rows, from_side[weight_rows:], 0)], axis=0)

    packed = jnp.concatenate(
        [observed_cell.astype(jnp.float32), observed_value, observed_weight], axis=0
    )
    kinds, _, _, block_count = packed.shape
    lanes = 2 * col_count
    packed = jnp.transpose(packed, (1, 2, 0, 3)).reshape(levels, row_count, kinds * block_count)
    packed = jnp.pad(packed, ((0, 0), (0, 0), (0, lanes - kinds * block_count)))
    winds = jnp.transpose(wind_field, (1, 0, 2)).reshape(1, row_count, lanes)
    parts = row_count // own_rows
    packed = packed.reshape(sides, levels_here, 1, parts, own_rows, lanes)
    winds = jnp.broadcast_to(
        winds.reshape(1, 1, 1, parts, own_rows, lanes), (1, levels_here, 1, parts, own_rows, lanes)
    )
    packed = jnp.transpose(jnp.concatenate([packed, winds], axis=0), (1, 2, 3, 0, 4, 5))
    packed = jnp.broadcast_to(
        packed, (levels_here, quarters // parts, parts, sides + 1, own_rows, lanes)
    )
    packed = swapped(packed.reshape(peers, sides + 1, own_rows, lanes), "mem", 0)

    side = lax.axis_index("lat_1")
    other_members = lax.dynamic_slice_in_dim(
        perturbations, (1 - side) * levels_here, levels_here, axis=1
    )
    other_members = lax.ppermute(other_members, "lat_1", across)
    up = [(i, (i + 1) % rings) for i in range(rings)]
    down = [(b, a) for a, b in up]
    blocks = {0: both}
    rising = falling = both
    for hop in range(1, rings // 2 + 1):
        rising = lax.ppermute(rising, "lat_0", up)
        if hop < rings - hop:
            falling = lax.ppermute(falling, "lat_0", down)
        if hop == 2:
            rising, falling, packed = lax.optimization_barrier((rising, falling, packed))
            passed = jnp.where(first, packed[:, 1:], jnp.stack([packed[:, 0], packed[:, 2]], axis=1))
            passed = lax.ppermute(passed, "lat_1", across)
        blocks[-hop % rings] = rising
        if hop < rings - hop:
            blocks[hop] = falling

    def lat_of(block):
        rows = block[sides * weight_rows :].reshape(sides, row_count // 2, coarse_lons)
        rows = jnp.concatenate([rows[..., :coarse_total], rows[..., coarse_total:]], 1)
        return rows.reshape(1, wide_count, coarse_total)

    columns = lat_of(both)[0].reshape(wide_count, rings, sides * coarse_rows)
    columns = lax.dynamic_slice_in_dim(
        jnp.concatenate([columns, columns], axis=1), ring, rings, axis=1
    ).reshape(wide_count, coarse_total)

    scalars = pl.BlockSpec(memory_space=pltpu.SMEM)
    whole = pl.BlockSpec(memory_space=pltpu.VMEM)
    roomy = pltpu.CompilerParams(vmem_limit_bytes=48 * 1024 * 1024)
    where_side = jnp.reshape(side, (1,)).astype(jnp.int32)
    piece_rows = own_rows * lon_total // 128 + own_rows
    partial_sum, lat_ring = pl.pallas_call(
        localize_kernel,
        out_shape=[
            jax.ShapeDtypeStruct((peers, piece_rows, 128), jnp.int16),
            jax.ShapeDtypeStruct((rings, wide_count, coarse_total), jnp.bfloat16),
        ],
        in_specs=[scalars] + [whole] * (4 + rings),
        out_specs=[whole] * 2,
        compiler_params=roomy,
    )(
        where_side,
        columns,
        lon_matrix,
        perturbations,
        other_members,
        *[blocks[d] for d in range(rings)],
    )
    partial_sum, packed, passed = lax.optimization_barrier((partial_sum, packed, passed))
    arrived = swapped(partial_sum, "mem", 0)

    is_own = (quarter // parts == side).astype(jnp.int32)
    local = pl.pallas_call(
        arrange_kernel,
        out_shape=jax.ShapeDtypeStruct(
            (own_rows, 2 * lon_total + kinds * peers * block_count), jnp.float32
        ),
        in_specs=[scalars, whole, whole],
        out_specs=whole,
        compiler_params=roomy,
    )(jnp.stack([side.astype(jnp.int32), is_own]), packed, passed)
    before = lax.ppermute(local[-HALO:], ALL, forward)
    after = lax.ppermute(local[:HALO], ALL, backward)
    wide_rows = own_rows + 2 * HALO
    wide_wind, gains, values = pl.pallas_call(
        spread_kernel,
        out_shape=[
            jax.ShapeDtypeStruct((count, wide_rows, lon_total), jnp.float32)
            for count in (2, STEPS, STEPS)
        ],
        in_specs=[whole] * 3,
        out_specs=[whole] * 3,
        compiler_params=roomy,
    )(before, local, after)

    scale = (members_here * peers - 1) ** -0.5
    own = pl.pallas_call(
        functools.partial(add_kernel, scale),
        out_shape=jax.ShapeDtypeStruct((own_rows, lon_total), jnp.float32),
        in_specs=[whole],
        out_specs=whole,
        compiler_params=roomy,
    )(arrived)

    before = lax.ppermute(own[-HALO:], ALL, forward)
    after = lax.ppermute(own[:HALO], ALL, backward)
    place = jnp.stack(
        [ring * wide_count + quarter * own_rows - HALO, jnp.int32(row_count * bands)]
    ).astype(jnp.int32)
    copies = pl.pallas_call(
        stencil_kernel,
        out_shape=jax.ShapeDtypeStruct((peers, own_rows * lon_total // 128 + 8, 128), jnp.float32),
        in_specs=[scalars] + [whole] * 6,
        out_specs=whole,
        compiler_params=roomy,
    )(place, own, before, after, wide_wind, gains, values)

    adjoint_all = swapped(copies, "mem", 0)
    repeats = pairs // rings
    projected, tiles = pl.pallas_call(
        project_kernel,
        out_shape=[
            jax.ShapeDtypeStruct((rings, repeats * wide_count + 16, coarse_lons), jnp.int16),
            jax.ShapeDtypeStruct((sides, levels_here, row_count, col_count), jnp.float32),
        ],
        in_specs=[scalars] + [whole] * 4,
        out_specs=[whole] * 2,
        compiler_params=roomy,
    )(where_side, adjoint_all, jnp.transpose(lon_matrix), perturbations, other_members)
    _, lat_ring = lax.optimization_barrier((projected, lat_ring))
    lat_all = lax.dynamic_slice_in_dim(
        jnp.concatenate([lat_ring, lat_ring], axis=0), rings - ring, rings, axis=0
    )
    lat_all = jnp.broadcast_to(lat_all[:, None], (rings, repeats, wide_count, coarse_total))
    lat_all = jnp.transpose(lat_all.reshape(rings * repeats * wide_count, coarse_total))
    by_pair = swapped(projected, "lat_0", 0)
    full = pl.pallas_call(
        functools.partial(gather_kernel, scale),
        out_shape=jax.ShapeDtypeStruct((bands, repeats, coarse_rows, coarse_lons), jnp.float32),
        in_specs=[whole] * 2,
        out_specs=whole,
        compiler_params=roomy,
    )(by_pair, lat_all)
    full = swapped(full, LAT, 0)
    full = full.reshape(
        members_here, rings // members_here, sides, pairs // rings, coarse_rows, coarse_lons
    )
    full = jnp.transpose(full, (4, 0, 2, 1, 3, 5)).reshape(coarse_weights.shape)
    gradient = full + coarse_weights.astype(jnp.float32)

    kept = jnp.where(first, tiles[0], tiles[1])
    sent = jnp.where(first, tiles[1], tiles[0])
    increment = in_order(kept, lax.ppermute(sent, "lat_1", across), 0)
    return (gradient, increment)


def solution(mesh):
    split = Mesh(mesh.devices.reshape(mesh.shape["mem"], 8, 2), ("mem", "lat_0", "lat_1"))
    placed = (
        P(LAT, "mem", None, None),
        P("mem", None, LAT, None),
        P(LAT, None),
        P(),
        P(None, LAT, "mem"),
        P(None, None, LAT, "mem"),
        P(None, None, LAT, "mem"),
        P(None, None, LAT, "mem"),
    )
    return jax.shard_map(
        body,
        mesh=split,
        in_specs=placed,
        out_specs=(P(LAT, "mem", None, None), P(None, LAT, "mem")),
        check_vma=False,
    )
```

```python
import functools

import jax
import jax.numpy as jnp
from jax import lax
from jax.experimental import pallas as pl
from jax.experimental.pallas import tpu as pltpu
from jax.sharding import Mesh
from jax.sharding import PartitionSpec as P

STEPS = 4
OBLK = 8
HALO = 8
LN2 = 0.6931471805599453
STEPS_16 = 32767.0
LAT = ("lat_0", "lat_1")
ALL = ("mem", "lat_0", "lat_1")

def swapped(value, axis, dim):
    return lax.all_to_all(value, axis, split_axis=dim, concat_axis=dim, tiled=True)


def two_terms(value):
    high = value.astype(jnp.bfloat16)
    low = (value - high.astype(jnp.float32)).astype(jnp.bfloat16)
    return jnp.concatenate([high, low], axis=0)


def dot(a, b):
    return jnp.dot(a, b, preferred_element_type=jnp.float32)


def row_codes(value):
    largest = jnp.maximum(jnp.max(jnp.abs(value), axis=1, keepdims=True), 1e-30)
    return jnp.ceil(jnp.log(largest) * (256.0 / LN2)) + 1.0


def code_scale(codes):
    return jnp.exp(codes * (LN2 / 256.0))


def rounded(value, codes):
    return jnp.round(value * (STEPS_16 / code_scale(codes)))


def to_16(value):
    return value.astype(jnp.int32).astype(jnp.int16)


def from_16(value):
    return value.astype(jnp.int32).astype(jnp.float32)


def as_tiles(value):
    rows, cols = value.shape
    return jnp.concatenate(
        [
            value[t * 8 : (t + 1) * 8, at * 128 : (at + 1) * 128]
            for t in range(rows // 8)
            for at in range(cols // 128)
        ],
        axis=0,
    )


def from_tiles(value, row_tiles):
    lane_tiles = value.shape[0] // 8 // row_tiles
    rows = []
    for t in range(row_tiles):
        start = t * lane_tiles * 8
        strips = [value[start + at * 8 : start + (at + 1) * 8] for at in range(lane_tiles)]
        rows.append(jnp.concatenate(strips, axis=1))
    return jnp.concatenate(rows, axis=0)


def tile_scales(codes, lane_tiles):
    scales = code_scale(codes) * (1.0 / STEPS_16)
    parts = []
    for t in range(scales.shape[0] // 8):
        parts += [scales[t * 8 : (t + 1) * 8]] * lane_tiles
    return jnp.concatenate(parts, axis=0)


def member_rows(side, own_ref, other_ref, member, level):
    levels_here = other_ref.shape[1]
    own = own_ref[member, side * levels_here + level].astype(jnp.float32)
    other = other_ref[member, level].astype(jnp.float32)
    low = jnp.where(side == 0, own, other)
    high = jnp.where(side == 0, other, own)
    return jnp.concatenate([low, high], axis=0)


def localize_kernel(side_ref, columns_ref, lon_ref, own_ref, other_ref, *refs):
    block_refs, sum_ref, lat_ref = refs[:-2], refs[-2], refs[-1]
    members, levels_here, row_count, lon_total = other_ref.shape
    tall = 2 * row_count
    side = side_ref[0]
    per_block = columns_ref.shape[1] // len(block_refs)
    columns = columns_ref[...]
    lon = lon_ref[...]
    for level in range(levels_here):
        narrow = []
        for member in range(members):
            start = (member * levels_here + level) * per_block
            weights = jnp.concatenate([ref[start : start + per_block] for ref in block_refs], axis=0)
            narrow.append(dot(columns, weights))
        localized = dot(two_terms(jnp.concatenate(narrow, axis=0)), lon)
        total = None
        for member in range(members):
            at = member * tall
            term = localized[at : at + tall] + localized[at + members * tall : at + (members + 1) * tall]
            term = term * member_rows(side, own_ref, other_ref, member, level)
            total = term if total is None else total + term
        count = sum_ref.shape[0] // levels_here
        piece_rows = tall // count
        data = piece_rows * lon_total // 128
        codes = row_codes(total)
        total = rounded(total, codes)
        for piece in range(count):
            part = slice(piece * piece_rows, (piece + 1) * piece_rows)
            sum_ref[level * count + piece, :data] = to_16(as_tiles(total[part]))
            sum_ref[level * count + piece, data:] = to_16(
                jnp.broadcast_to(codes[part], (piece_rows, 128))
            )
    half = row_count // 2
    for at, ref in enumerate(block_refs):
        lat = ref[ref.shape[0] - row_count :]
        for part in range(4):
            rows = lat[part // 2 * half : (part // 2 + 1) * half]
            lat_ref[at, part * half : (part + 1) * half] = rows[
                :, part % 2 * lat_ref.shape[2] : (part % 2 + 1) * lat_ref.shape[2]
            ]


def add_kernel(scale, message_ref, out_ref):
    sources, rows, _ = message_ref.shape
    own_rows, lon_total = out_ref.shape
    total = None
    for source in range(sources):
        value = from_16(message_ref[source, : rows - own_rows])
        codes = from_16(message_ref[source, rows - own_rows :])
        value = value * tile_scales(codes, lon_total // 128)
        total = value if total is None else total + value
    out_ref[...] = from_tiles(total, own_rows // 8) * scale


def project_kernel(side_ref, message_ref, lon_ref, own_ref, other_ref, out_ref, tile_ref):
    members, levels_here, row_count, lon_total = other_ref.shape
    rings, _, coarse_lons = out_ref.shape
    tall = 2 * row_count
    side = side_ref[0]
    lon = lon_ref[...]
    quarters = message_ref.shape[0] // levels_here
    own_rows = tall // quarters
    lane_tiles = lon_total // 128
    data = own_rows * lane_tiles
    width = tile_ref.shape[3]
    per_message = members * levels_here // rings
    row = lax.broadcasted_iota(jnp.int32, (tall, 128), 0)
    lane = lax.broadcasted_iota(jnp.int32, (tall, 128), 1)
    tails = [jnp.zeros((1, 128), jnp.float32) for _ in range(rings)]
    for level in range(levels_here):
        pieces = []
        for q in range(quarters):
            value = from_16(message_ref[level * quarters + q, :data])
            codes = from_16(message_ref[level * quarters + q, data : data + own_rows])
            pieces.append(from_tiles(value * tile_scales(codes, lane_tiles), own_rows // 8))
            tail = from_16(message_ref[level * quarters + q, data + own_rows :])
            tile = tail[:8] * (code_scale(tail[8:]) * (1.0 / STEPS_16))
            band, start = q * own_rows // row_count, q * own_rows % row_count
            tile_ref[band, level, start : start + 8] = tile[:, :width]
            tile_ref[band, level, start + 8 : start + 16] = tile[:, width:]
        adjoint = jnp.concatenate(pieces, axis=0)
        product = [
            member_rows(side, own_ref, other_ref, member, level) * adjoint for member in range(members)
        ]
        projected = dot(two_terms(jnp.concatenate(product, axis=0)), lon)
        for member in range(members):
            at = member * tall
            value = projected[at : at + tall] + projected[at + members * tall : at + (members + 1) * tall]
            pair = member * levels_here + level
            ring, place = pair // per_message, pair % per_message
            codes = row_codes(value)
            whole = jnp.round(value * (STEPS_16 / code_scale(codes))).astype(jnp.int32)
            out_ref[ring, place * tall : (place + 1) * tall] = whole.astype(jnp.int16)
            mark = jnp.where(lane == row + place * tall, codes, 0.0)
            tails[ring] = tails[ring] + jnp.sum(mark, axis=0, keepdims=True)
    end = per_message * tall
    for ring in range(rings):
        tail = jnp.broadcast_to(tails[ring], (16, 128)).astype(jnp.int32).astype(jnp.int16)
        out_ref[ring, end : end + 16] = jnp.concatenate([tail] * (coarse_lons // 128), axis=1)


def gather_kernel(scale, message_ref, lat_ref, out_ref):
    rings, rows, lons = message_ref.shape
    bands, places, coarse_rows, _ = out_ref.shape
    data = rows - 16
    coarse = bands * coarse_rows
    high, low, scales = [], [], []
    for ring in range(rings):
        value = message_ref[ring, :data].astype(jnp.int32).astype(jnp.float32)
        upper = jnp.floor(value * (1.0 / 256.0)) * 256.0
        high.append(upper.astype(jnp.bfloat16))
        low.append((value - upper).astype(jnp.bfloat16))
        codes = message_ref[ring, data:].astype(jnp.int32).astype(jnp.float32)[:1, :data]
        scales.append(code_scale(codes) * (scale / STEPS_16))
    high = jnp.concatenate(high, axis=0)
    low = jnp.concatenate(low, axis=0)
    lat = lat_ref[...].astype(jnp.float32) * jnp.concatenate(scales, axis=1)
    place = lax.broadcasted_iota(jnp.int32, lat.shape, 1) % data // (data // places)
    lat = jnp.concatenate([jnp.where(place == p, lat, 0.0) for p in range(places)], axis=0)
    terms = two_terms(lat)
    total = dot(terms, high)
    total = total[: places * coarse] + (total[places * coarse :] + dot(terms[: places * coarse], low))
    for band in range(bands):
        for p in range(places):
            at = p * coarse + band * coarse_rows
            out_ref[band, p] = total[at : at + coarse_rows]


def arrange_kernel(side_ref, own_ref, other_ref, out_ref):
    peers, _, row_count, lanes = own_ref.shape
    side = side_ref[0]
    is_own = side_ref[1] == 1
    lane = lax.broadcasted_iota(jnp.int32, (row_count, lanes), 1)
    width = lanes // 2
    pick = lambda peer, which, mine: jnp.where(is_own, own_ref[peer, mine], other_ref[peer, which])
    winds = [pick(peer, 1, 2) for peer in range(peers)]
    seen = [pick(peer, 0, side) for peer in range(peers)]
    lon_total = peers * width
    for at in range(peers // 2):
        even, odd = winds[2 * at], winds[2 * at + 1]
        spot = slice(at * lanes, (at + 1) * lanes)
        out_ref[:, spot] = jnp.where(lane < width, even, pltpu.roll(odd, width, 1))
        spot = slice(lon_total + at * lanes, lon_total + (at + 1) * lanes)
        out_ref[:, spot] = jnp.where(lane < width, pltpu.roll(even, width, 1), odd)
    blocks = lanes // peers
    kinds = (out_ref.shape[1] - 2 * lon_total) // lanes
    owner = lane // blocks
    for kind in range(kinds):
        total = jnp.zeros((row_count, lanes), jnp.float32)
        for peer in range(peers):
            shift = (peer - kind) * blocks % lanes
            value = seen[peer] if shift == 0 else pltpu.roll(seen[peer], shift, 1)
            total = jnp.where(owner == peer, value, total)
        spot = slice(2 * lon_total + kind * lanes, 2 * lon_total + (kind + 1) * lanes)
        out_ref[:, spot] = total


def spread_kernel(before_ref, local_ref, after_ref, wind_ref, gain_ref, value_ref):
    _, rows, cols = wind_ref.shape
    lanes = cols // OBLK
    local = jnp.concatenate([before_ref[...], local_ref[...], after_ref[...]], axis=0)
    wind_ref[0] = local[:, :cols]
    wind_ref[1] = local[:, cols : 2 * cols]
    sights = [local[:, 2 * cols + k * lanes : 2 * cols + (k + 1) * lanes] for k in range(3 * STEPS)]
    cells = jnp.concatenate(sights[:STEPS], axis=0).astype(jnp.bfloat16)
    others = jnp.concatenate(sights[STEPS:], axis=0)
    high = others.astype(jnp.bfloat16)
    rest = others - high.astype(jnp.float32)
    middle = rest.astype(jnp.bfloat16)
    low = (rest - middle.astype(jnp.float32)).astype(jnp.bfloat16)
    block = lax.broadcasted_iota(jnp.int32, (lanes, cols), 0)
    spread = (lax.broadcasted_iota(jnp.int32, (lanes, cols), 1) // OBLK == block).astype(jnp.bfloat16)
    cells = dot(cells, spread)
    wide = dot(high, spread) + (dot(middle, spread) + dot(low, spread))
    offset = lax.broadcasted_iota(jnp.int32, (rows, cols), 1) % OBLK
    offset = offset.astype(jnp.float32)
    for step in range(STEPS):
        value_ref[step] = wide[step * rows : (step + 1) * rows]
        hit = jnp.abs(cells[step * rows : (step + 1) * rows] - offset) < 0.5
        weight = wide[(STEPS + step) * rows : (STEPS + step + 1) * rows]
        gain_ref[step] = jnp.where(hit, weight, 0.0)


def stencil_kernel(place_ref, own_ref, before_ref, after_ref, wind_ref, gain_ref, value_ref, out_hbm, adjoint_ref, piece_ref, sems):
    rows, cols = wind_ref.shape[1:]
    first_row = place_ref[0]
    last_row = place_ref[1]
    state = jnp.concatenate([before_ref[...], own_ref[...], after_ref[...]], axis=0)
    row = lax.broadcasted_iota(jnp.int32, (rows, cols), 0) + first_row
    col = lax.broadcasted_iota(jnp.int32, (rows, cols), 1)
    inside = ((row >= 0) & (row < last_row)).astype(jnp.float32)
    not_first = (col > 0).astype(jnp.float32)
    not_last = (col < cols - 1).astype(jnp.float32)
    lon_wind = 0.5 * wind_ref[0]
    lat_wind = 0.5 * wind_ref[1]

    def north(x):
        return pltpu.roll(x, rows - 1, 0)

    def south(x):
        return pltpu.roll(x, 1, 0)

    def east(x):
        return pltpu.roll(x, cols - 1, 1)

    def west(x):
        return pltpu.roll(x, 1, 1)

    from_north = (0.2 - lat_wind) * inside
    from_south = (0.2 + lat_wind) * inside
    from_east = (0.2 - lon_wind) * inside * not_last
    from_west = (0.2 + lon_wind) * inside * not_first
    centre = 0.2 * inside
    forcings = []
    for step in range(STEPS):
        state = (
            centre * state
            + from_north * north(state)
            + from_south * south(state)
            + from_east * east(state)
            + from_west * west(state)
        )
        forcings.append(gain_ref[step] * (state - value_ref[step]))
    to_south = 0.2 + lat_wind
    to_north = 0.2 - lat_wind
    to_west = (0.2 + lon_wind) * not_first
    to_east = (0.2 - lon_wind) * not_last
    adjoint = None
    for step in reversed(range(STEPS)):
        pushed = forcings[step] if adjoint is None else adjoint + forcings[step]
        adjoint = inside * (
            0.2 * pushed
            + north(to_south * pushed)
            + south(to_north * pushed)
            + east(to_west * pushed)
            + west(to_east * pushed)
        )
    adjoint = adjoint[HALO : rows - HALO]
    own_rows = rows - 2 * HALO
    data = own_rows * cols // 128
    codes = row_codes(adjoint)
    adjoint_ref[:data] = to_16(as_tiles(rounded(adjoint, codes)))
    adjoint_ref[data:] = to_16(jnp.broadcast_to(codes, (own_rows, 128)))
    count = out_hbm.shape[0]
    copies = [
        pltpu.make_async_copy(
            adjoint_ref, out_hbm.at[copy, pl.ds(0, data + own_rows)], sems.at[copy]
        )
        for copy in range(count)
    ]
    for copy in copies:
        copy.start()
    width = cols // count
    lane = lax.broadcasted_iota(jnp.int32, (8, 128), 1)
    own = own_ref[...]
    codes = row_codes(own)
    own = rounded(own, codes)
    codes = jnp.where(lane < width, codes[:8], codes[8:])
    for copy in range(count):
        strip = slice(copy * width // 128 * 128, copy * width // 128 * 128 + 128)
        top, bottom = own[0:8, strip], own[8:16, strip]
        if copy % 2 == 0:
            piece = jnp.where(lane < width, top, pltpu.roll(bottom, width, 1))
        else:
            piece = jnp.where(lane < width, pltpu.roll(top, width, 1), bottom)
        piece_ref[copy] = to_16(jnp.concatenate([piece, codes], axis=0))
    last = pltpu.make_async_copy(
        piece_ref, out_hbm.at[:, pl.ds(data + own_rows, 16)], sems.at[count]
    )
    last.start()
    for copy in copies:
        copy.wait()
    last.wait()


def body(
    coarse_weights,
    perturbations,
    lat_matrix,
    lon_matrix,
    wind_field,
    observed_cell,
    observed_value,
    observed_weight,
):
    members_here, levels, row_count, lon_total = perturbations.shape
    coarse_rows, _, _, coarse_lons = coarse_weights.shape
    col_count = wind_field.shape[2]
    peers = lax.axis_size("mem")
    rings = lax.axis_size("lat_0")
    sides = lax.axis_size("lat_1")
    bands = rings * sides
    levels_here = levels // sides
    wide_count = row_count * sides
    pairs = members_here * levels_here
    quarters = peers // levels_here
    own_rows = wide_count // quarters
    quarter = lax.axis_index("mem") % quarters
    ring = lax.axis_index("lat_0")
    first = lax.axis_index("lat_1") == 0
    across = [(0, 1), (1, 0)]

    forward = []
    for m in range(peers):
        for z in range(rings):
            for x in range(sides):
                here = (m * rings + z) * sides + x
                if m % quarters < quarters - 1:
                    forward.append((here, here + bands))
                elif z < rings - 1:
                    forward.append((here, here - (quarters - 1) * bands + sides))
    backward = [(b, a) for a, b in forward]

    def halves(value, dim):
        low = lax.slice_in_dim(value, 0, levels_here, axis=dim)
        high = lax.slice_in_dim(value, levels_here, levels, axis=dim)
        return jnp.where(first, low, high), jnp.where(first, high, low)

    def in_order(mine, theirs, dim):
        return jnp.where(
            first, jnp.concatenate([mine, theirs], dim), jnp.concatenate([theirs, mine], dim)
        )

    weight_rows = pairs * coarse_rows
    coarse_total = bands * coarse_rows
    mine, theirs = halves(coarse_weights, 2)
    lat_rows = jnp.concatenate([lat_matrix[: row_count // 2], lat_matrix[row_count // 2 :]], axis=1)

    def by_pair_first(value):
        value = value.reshape(coarse_rows, pairs, coarse_lons)
        return jnp.transpose(value, (1, 0, 2))

    theirs = by_pair_first(theirs).reshape(weight_rows, coarse_lons)
    from_side = lax.ppermute(jnp.concatenate([theirs, lat_rows], axis=0), "lat_1", across)
    both = in_order(
        by_pair_first(mine), from_side[:weight_rows].reshape(pairs, coarse_rows, coarse_lons), 1
    ).reshape(sides * weight_rows, coarse_lons)
    both = jnp.concatenate([both, in_order(lat_rows, from_side[weight_rows:], 0)], axis=0)

    packed = jnp.concatenate(
        [observed_cell.astype(jnp.float32), observed_value, observed_weight], axis=0
    )
    kinds, _, _, block_count = packed.shape
    lanes = 2 * col_count
    packed = jnp.transpose(packed, (1, 2, 0, 3)).reshape(levels, row_count, kinds * block_count)
    packed = jnp.pad(packed, ((0, 0), (0, 0), (0, lanes - kinds * block_count)))
    winds = jnp.transpose(wind_field, (1, 0, 2)).reshape(1, row_count, lanes)
    parts = row_count // own_rows
    packed = packed.reshape(sides, levels_here, 1, parts, own_rows, lanes)
    winds = jnp.broadcast_to(
        winds.reshape(1, 1, 1, parts, own_rows, lanes), (1, levels_here, 1, parts, own_rows, lanes)
    )
    packed = jnp.transpose(jnp.concatenate([packed, winds], axis=0), (1, 2, 3, 0, 4, 5))
    packed = jnp.broadcast_to(
        packed, (levels_here, quarters // parts, parts, sides + 1, own_rows, lanes)
    )
    packed = swapped(packed.reshape(peers, sides + 1, own_rows, lanes), "mem", 0)

    side = lax.axis_index("lat_1")
    other_members = lax.dynamic_slice_in_dim(
        perturbations, (1 - side) * levels_here, levels_here, axis=1
    )
    other_members = lax.ppermute(other_members, "lat_1", across)
    up = [(i, (i + 1) % rings) for i in range(rings)]
    down = [(b, a) for a, b in up]
    blocks = {0: both}
    rising = falling = both
    for hop in range(1, rings // 2 + 1):
        rising = lax.ppermute(rising, "lat_0", up)
        if hop < rings - hop:
            falling = lax.ppermute(falling, "lat_0", down)
        if hop == 2:
            rising, falling, packed = lax.optimization_barrier((rising, falling, packed))
            passed = jnp.where(first, packed[:, 1:], jnp.stack([packed[:, 0], packed[:, 2]], axis=1))
            passed = lax.ppermute(passed, "lat_1", across)
        blocks[-hop % rings] = rising
        if hop < rings - hop:
            blocks[hop] = falling

    def lat_of(block):
        rows = block[sides * weight_rows :].reshape(sides, row_count // 2, coarse_lons)
        rows = jnp.concatenate([rows[..., :coarse_total], rows[..., coarse_total:]], 1)
        return rows.reshape(1, wide_count, coarse_total)

    columns = lat_of(both)[0].reshape(wide_count, rings, sides * coarse_rows)
    columns = lax.dynamic_slice_in_dim(
        jnp.concatenate([columns, columns], axis=1), ring, rings, axis=1
    ).reshape(wide_count, coarse_total)

    scalars = pl.BlockSpec(memory_space=pltpu.SMEM)
    whole = pl.BlockSpec(memory_space=pltpu.VMEM)
    roomy = pltpu.CompilerParams(vmem_limit_bytes=48 * 1024 * 1024)
    where_side = jnp.reshape(side, (1,)).astype(jnp.int32)
    anywhere = pl.BlockSpec(memory_space=pl.ANY)
    piece_rows = own_rows * lon_total // 128 + own_rows
    partial_sum, lat_ring = pl.pallas_call(
        localize_kernel,
        out_shape=[
            jax.ShapeDtypeStruct((peers, piece_rows, 128), jnp.int16),
            jax.ShapeDtypeStruct((rings, wide_count, coarse_total), jnp.bfloat16),
        ],
        in_specs=[scalars] + [whole] * (4 + rings),
        out_specs=[whole] * 2,
        compiler_params=roomy,
    )(
        where_side,
        columns,
        lon_matrix,
        perturbations,
        other_members,
        *[blocks[d] for d in range(rings)],
    )
    partial_sum, packed, passed = lax.optimization_barrier((partial_sum, packed, passed))
    arrived = swapped(partial_sum, "mem", 0)

    is_own = (quarter // parts == side).astype(jnp.int32)
    local = pl.pallas_call(
        arrange_kernel,
        out_shape=jax.ShapeDtypeStruct(
            (own_rows, 2 * lon_total + kinds * peers * block_count), jnp.float32
        ),
        in_specs=[scalars, whole, whole],
        out_specs=whole,
        compiler_params=roomy,
    )(jnp.stack([side.astype(jnp.int32), is_own]), packed, passed)
    before = lax.ppermute(local[-HALO:], ALL, forward)
    after = lax.ppermute(local[:HALO], ALL, backward)
    wide_rows = own_rows + 2 * HALO
    wide_wind, gains, values = pl.pallas_call(
        spread_kernel,
        out_shape=[
            jax.ShapeDtypeStruct((count, wide_rows, lon_total), jnp.float32)
            for count in (2, STEPS, STEPS)
        ],
        in_specs=[whole] * 3,
        out_specs=[whole] * 3,
        compiler_params=roomy,
    )(before, local, after)

    scale = (members_here * peers - 1) ** -0.5
    own = pl.pallas_call(
        functools.partial(add_kernel, scale),
        out_shape=jax.ShapeDtypeStruct((own_rows, lon_total), jnp.float32),
        in_specs=[whole],
        out_specs=whole,
        compiler_params=roomy,
    )(arrived)

    before = lax.ppermute(own[-HALO:], ALL, forward)
    after = lax.ppermute(own[:HALO], ALL, backward)
    place = jnp.stack(
        [ring * wide_count + quarter * own_rows - HALO, jnp.int32(row_count * bands)]
    ).astype(jnp.int32)
    copies = pl.pallas_call(
        stencil_kernel,
        out_shape=jax.ShapeDtypeStruct((peers, piece_rows + 16, 128), jnp.int16),
        in_specs=[scalars] + [whole] * 6,
        out_specs=anywhere,
        scratch_shapes=[
            pltpu.VMEM((piece_rows, 128), jnp.int16),
            pltpu.VMEM((peers, 16, 128), jnp.int16),
            pltpu.SemaphoreType.DMA((peers + 1,)),
        ],
        compiler_params=roomy,
    )(place, own, before, after, wide_wind, gains, values)

    adjoint_all = swapped(copies, "mem", 0)
    repeats = pairs // rings
    projected, tiles = pl.pallas_call(
        project_kernel,
        out_shape=[
            jax.ShapeDtypeStruct((rings, repeats * wide_count + 16, coarse_lons), jnp.int16),
            jax.ShapeDtypeStruct((sides, levels_here, row_count, col_count), jnp.float32),
        ],
        in_specs=[scalars] + [whole] * 4,
        out_specs=[whole] * 2,
        compiler_params=roomy,
    )(where_side, adjoint_all, jnp.transpose(lon_matrix), perturbations, other_members)
    _, lat_ring = lax.optimization_barrier((projected, lat_ring))
    lat_all = lax.dynamic_slice_in_dim(
        jnp.concatenate([lat_ring, lat_ring], axis=0), rings - ring, rings, axis=0
    )
    lat_all = jnp.broadcast_to(lat_all[:, None], (rings, repeats, wide_count, coarse_total))
    lat_all = jnp.transpose(lat_all.reshape(rings * repeats * wide_count, coarse_total))
    by_pair = swapped(projected, "lat_0", 0)
    full = pl.pallas_call(
        functools.partial(gather_kernel, scale),
        out_shape=jax.ShapeDtypeStruct((bands, repeats, coarse_rows, coarse_lons), jnp.float32),
        in_specs=[whole] * 2,
        out_specs=whole,
        compiler_params=roomy,
    )(by_pair, lat_all)
    full = swapped(full, LAT, 0)
    full = full.reshape(
        members_here, rings // members_here, sides, pairs // rings, coarse_rows, coarse_lons
    )
    full = jnp.transpose(full, (4, 0, 2, 1, 3, 5)).reshape(coarse_weights.shape)
    gradient = full + coarse_weights.astype(jnp.float32)

    kept = jnp.where(first, tiles[0], tiles[1])
    sent = jnp.where(first, tiles[1], tiles[0])
    increment = in_order(kept, lax.ppermute(sent, "lat_1", across), 0)
    return (gradient, increment)


def solution(mesh):
    split = Mesh(mesh.devices.reshape(mesh.shape["mem"], 8, 2), ("mem", "lat_0", "lat_1"))
    placed = (
        P(LAT, "mem", None, None),
        P("mem", None, LAT, None),
        P(LAT, None),
        P(),
        P(None, LAT, "mem"),
        P(None, None, LAT, "mem"),
        P(None, None, LAT, "mem"),
        P(None, None, LAT, "mem"),
    )
    return jax.shard_map(
        body,
        mesh=split,
        in_specs=placed,
        out_specs=(P(LAT, "mem", None, None), P(None, LAT, "mem")),
        check_vma=False,
    )
```

```python
import functools

import jax
import jax.numpy as jnp
from jax import lax
from jax.experimental import pallas as pl
from jax.experimental.pallas import tpu as pltpu
from jax.sharding import Mesh
from jax.sharding import PartitionSpec as P

STEPS = 4
OBLK = 8
HALO = 8
LN2 = 0.6931471805599453
STEPS_16 = 32767.0
LAT = ("lat_0", "lat_1")
ALL = ("mem", "lat_0", "lat_1")

def swapped(value, axis, dim):
    return lax.all_to_all(value, axis, split_axis=dim, concat_axis=dim, tiled=True)


def two_terms(value):
    high = value.astype(jnp.bfloat16)
    low = (value - high.astype(jnp.float32)).astype(jnp.bfloat16)
    return jnp.concatenate([high, low], axis=0)


def dot(a, b):
    return jnp.dot(a, b, preferred_element_type=jnp.float32)


def row_codes(value):
    largest = jnp.maximum(jnp.max(jnp.abs(value), axis=1, keepdims=True), 1e-30)
    return jnp.ceil(jnp.log(largest) * (256.0 / LN2)) + 1.0


def code_scale(codes):
    return jnp.exp(codes * (LN2 / 256.0))


def rounded(value, codes):
    return jnp.round(value * (STEPS_16 / code_scale(codes)))


def to_16(value):
    return value.astype(jnp.int32).astype(jnp.int16)


def from_16(value):
    return value.astype(jnp.int32).astype(jnp.float32)


def as_tiles(value):
    rows, cols = value.shape
    return jnp.concatenate(
        [
            value[t * 8 : (t + 1) * 8, at * 128 : (at + 1) * 128]
            for t in range(rows // 8)
            for at in range(cols // 128)
        ],
        axis=0,
    )


def from_tiles(value, row_tiles):
    lane_tiles = value.shape[0] // 8 // row_tiles
    rows = []
    for t in range(row_tiles):
        start = t * lane_tiles * 8
        strips = [value[start + at * 8 : start + (at + 1) * 8] for at in range(lane_tiles)]
        rows.append(jnp.concatenate(strips, axis=1))
    return jnp.concatenate(rows, axis=0)


def tile_scales(codes, lane_tiles):
    scales = code_scale(codes) * (1.0 / STEPS_16)
    parts = []
    for t in range(scales.shape[0] // 8):
        parts += [scales[t * 8 : (t + 1) * 8]] * lane_tiles
    return jnp.concatenate(parts, axis=0)


def member_rows(side, own_ref, other_ref, member, level):
    levels_here = other_ref.shape[1]
    own = own_ref[member, side * levels_here + level].astype(jnp.float32)
    other = other_ref[member, level].astype(jnp.float32)
    low = jnp.where(side == 0, own, other)
    high = jnp.where(side == 0, other, own)
    return jnp.concatenate([low, high], axis=0)


def localize_kernel(side_ref, columns_ref, lon_ref, own_ref, other_ref, *refs):
    block_refs, sum_ref, lat_ref = refs[:-2], refs[-2], refs[-1]
    members, levels_here, row_count, lon_total = other_ref.shape
    tall = 2 * row_count
    side = side_ref[0]
    per_block = columns_ref.shape[1] // len(block_refs)
    columns = columns_ref[...]
    lon = lon_ref[...]
    for level in range(levels_here):
        narrow = []
        for member in range(members):
            start = (member * levels_here + level) * per_block
            weights = jnp.concatenate([ref[start : start + per_block] for ref in block_refs], axis=0)
            narrow.append(dot(columns, weights))
        localized = dot(two_terms(jnp.concatenate(narrow, axis=0)), lon)
        total = None
        for member in range(members):
            at = member * tall
            term = localized[at : at + tall] + localized[at + members * tall : at + (members + 1) * tall]
            term = term * member_rows(side, own_ref, other_ref, member, level)
            total = term if total is None else total + term
        count = sum_ref.shape[0] // levels_here
        piece_rows = tall // count
        data = piece_rows * lon_total // 128
        codes = row_codes(total)
        total = rounded(total, codes)
        for piece in range(count):
            part = slice(piece * piece_rows, (piece + 1) * piece_rows)
            sum_ref[level * count + piece, :data] = to_16(as_tiles(total[part]))
            sum_ref[level * count + piece, data:] = to_16(
                jnp.broadcast_to(codes[part], (piece_rows, 128))
            )
    half = row_count // 2
    for at, ref in enumerate(block_refs):
        lat = ref[ref.shape[0] - row_count :]
        for part in range(4):
            rows = lat[part // 2 * half : (part // 2 + 1) * half]
            lat_ref[at, part * half : (part + 1) * half] = rows[
                :, part % 2 * lat_ref.shape[2] : (part % 2 + 1) * lat_ref.shape[2]
            ]


def add_kernel(scale, message_ref, out_ref):
    sources, rows, _ = message_ref.shape
    own_rows, lon_total = out_ref.shape
    total = None
    for source in range(sources):
        value = from_16(message_ref[source, : rows - own_rows])
        codes = from_16(message_ref[source, rows - own_rows :])
        value = value * tile_scales(codes, lon_total // 128)
        total = value if total is None else total + value
    out_ref[...] = from_tiles(total, own_rows // 8) * scale


def project_kernel(side_ref, message_ref, lon_ref, own_ref, other_ref, out_ref, tile_ref):
    members, levels_here, row_count, lon_total = other_ref.shape
    rings, _, coarse_lons = out_ref.shape
    tall = 2 * row_count
    side = side_ref[0]
    lon = lon_ref[...]
    quarters = message_ref.shape[0] // levels_here
    own_rows = tall // quarters
    lane_tiles = lon_total // 128
    data = own_rows * lane_tiles
    width = tile_ref.shape[3]
    per_message = members * levels_here // rings
    row = lax.broadcasted_iota(jnp.int32, (tall, 128), 0)
    lane = lax.broadcasted_iota(jnp.int32, (tall, 128), 1)
    tails = [jnp.zeros((1, 128), jnp.float32) for _ in range(rings)]
    for level in range(levels_here):
        pieces = []
        for q in range(quarters):
            value = from_16(message_ref[level * quarters + q, :data])
            codes = from_16(message_ref[level * quarters + q, data : data + own_rows])
            pieces.append(from_tiles(value * tile_scales(codes, lane_tiles), own_rows // 8))
            tail = from_16(message_ref[level * quarters + q, data + own_rows :])
            tile = tail[:8] * (code_scale(tail[8:]) * (1.0 / STEPS_16))
            band, start = q * own_rows // row_count, q * own_rows % row_count
            tile_ref[band, level, start : start + 8] = tile[:, :width]
            tile_ref[band, level, start + 8 : start + 16] = tile[:, width:]
        adjoint = jnp.concatenate(pieces, axis=0)
        product = [
            member_rows(side, own_ref, other_ref, member, level) * adjoint for member in range(members)
        ]
        projected = dot(two_terms(jnp.concatenate(product, axis=0)), lon)
        for member in range(members):
            at = member * tall
            value = projected[at : at + tall] + projected[at + members * tall : at + (members + 1) * tall]
            pair = member * levels_here + level
            ring, place = pair // per_message, pair % per_message
            codes = row_codes(value)
            whole = jnp.round(value * (STEPS_16 / code_scale(codes))).astype(jnp.int32)
            out_ref[ring, place * tall : (place + 1) * tall] = whole.astype(jnp.int16)
            mark = jnp.where(lane == row + place * tall, codes, 0.0)
            tails[ring] = tails[ring] + jnp.sum(mark, axis=0, keepdims=True)
    end = per_message * tall
    for ring in range(rings):
        tail = jnp.broadcast_to(tails[ring], (16, 128)).astype(jnp.int32).astype(jnp.int16)
        out_ref[ring, end : end + 16] = jnp.concatenate([tail] * (coarse_lons // 128), axis=1)


def gather_kernel(scale, message_ref, lat_ref, out_ref):
    rings, rows, lons = message_ref.shape
    bands, places, coarse_rows, _ = out_ref.shape
    data = rows - 16
    coarse = bands * coarse_rows
    high, low, scales = [], [], []
    for ring in range(rings):
        value = message_ref[ring, :data].astype(jnp.int32).astype(jnp.float32)
        upper = jnp.floor(value * (1.0 / 256.0)) * 256.0
        high.append(upper.astype(jnp.bfloat16))
        low.append((value - upper).astype(jnp.bfloat16))
        codes = message_ref[ring, data:].astype(jnp.int32).astype(jnp.float32)[:1, :data]
        scales.append(code_scale(codes) * (scale / STEPS_16))
    high = jnp.concatenate(high, axis=0)
    low = jnp.concatenate(low, axis=0)
    lat = lat_ref[...].astype(jnp.float32) * jnp.concatenate(scales, axis=1)
    place = lax.broadcasted_iota(jnp.int32, lat.shape, 1) % data // (data // places)
    lat = jnp.concatenate([jnp.where(place == p, lat, 0.0) for p in range(places)], axis=0)
    terms = two_terms(lat)
    total = dot(terms, high)
    total = total[: places * coarse] + (total[places * coarse :] + dot(terms[: places * coarse], low))
    for band in range(bands):
        for p in range(places):
            at = p * coarse + band * coarse_rows
            out_ref[band, p] = total[at : at + coarse_rows]


def arrange_kernel(side_ref, own_ref, other_ref, out_ref):
    peers, _, row_count, lanes = own_ref.shape
    side = side_ref[0]
    is_own = side_ref[1] == 1
    lane = lax.broadcasted_iota(jnp.int32, (row_count, lanes), 1)
    width = lanes // 2
    pick = lambda peer, which, mine: jnp.where(is_own, own_ref[peer, mine], other_ref[peer, which])
    winds = [pick(peer, 1, 2) for peer in range(peers)]
    seen = [pick(peer, 0, side) for peer in range(peers)]
    lon_total = peers * width
    for at in range(peers // 2):
        even, odd = winds[2 * at], winds[2 * at + 1]
        spot = slice(at * lanes, (at + 1) * lanes)
        out_ref[:, spot] = jnp.where(lane < width, even, pltpu.roll(odd, width, 1))
        spot = slice(lon_total + at * lanes, lon_total + (at + 1) * lanes)
        out_ref[:, spot] = jnp.where(lane < width, pltpu.roll(even, width, 1), odd)
    blocks = lanes // peers
    kinds = (out_ref.shape[1] - 2 * lon_total) // lanes
    owner = lane // blocks
    for kind in range(kinds):
        total = jnp.zeros((row_count, lanes), jnp.float32)
        for peer in range(peers):
            shift = (peer - kind) * blocks % lanes
            value = seen[peer] if shift == 0 else pltpu.roll(seen[peer], shift, 1)
            total = jnp.where(owner == peer, value, total)
        spot = slice(2 * lon_total + kind * lanes, 2 * lon_total + (kind + 1) * lanes)
        out_ref[:, spot] = total


def spread_kernel(before_ref, local_ref, after_ref, wind_ref, gain_ref, value_ref):
    _, rows, cols = wind_ref.shape
    lanes = cols // OBLK
    local = jnp.concatenate([before_ref[...], local_ref[...], after_ref[...]], axis=0)
    wind_ref[0] = local[:, :cols]
    wind_ref[1] = local[:, cols : 2 * cols]
    sights = [local[:, 2 * cols + k * lanes : 2 * cols + (k + 1) * lanes] for k in range(3 * STEPS)]
    cells = jnp.concatenate(sights[:STEPS], axis=0).astype(jnp.bfloat16)
    others = jnp.concatenate(sights[STEPS:], axis=0)
    high = others.astype(jnp.bfloat16)
    rest = others - high.astype(jnp.float32)
    middle = rest.astype(jnp.bfloat16)
    low = (rest - middle.astype(jnp.float32)).astype(jnp.bfloat16)
    block = lax.broadcasted_iota(jnp.int32, (lanes, cols), 0)
    spread = (lax.broadcasted_iota(jnp.int32, (lanes, cols), 1) // OBLK == block).astype(jnp.bfloat16)
    cells = dot(cells, spread)
    wide = dot(high, spread) + (dot(middle, spread) + dot(low, spread))
    offset = lax.broadcasted_iota(jnp.int32, (rows, cols), 1) % OBLK
    offset = offset.astype(jnp.float32)
    for step in range(STEPS):
        value_ref[step] = wide[step * rows : (step + 1) * rows]
        hit = jnp.abs(cells[step * rows : (step + 1) * rows] - offset) < 0.5
        weight = wide[(STEPS + step) * rows : (STEPS + step + 1) * rows]
        gain_ref[step] = jnp.where(hit, weight, 0.0)


def stencil_kernel(place_ref, own_ref, before_ref, after_ref, wind_ref, gain_ref, value_ref, out_hbm, adjoint_ref, piece_ref, sems):
    rows, cols = wind_ref.shape[1:]
    first_row = place_ref[0]
    last_row = place_ref[1]
    state = jnp.concatenate([before_ref[...], own_ref[...], after_ref[...]], axis=0)
    row = lax.broadcasted_iota(jnp.int32, (rows, cols), 0) + first_row
    col = lax.broadcasted_iota(jnp.int32, (rows, cols), 1)
    inside = ((row >= 0) & (row < last_row)).astype(jnp.float32)
    not_first = (col > 0).astype(jnp.float32)
    not_last = (col < cols - 1).astype(jnp.float32)
    lon_wind = 0.5 * wind_ref[0]
    lat_wind = 0.5 * wind_ref[1]

    def north(x):
        return pltpu.roll(x, rows - 1, 0)

    def south(x):
        return pltpu.roll(x, 1, 0)

    def east(x):
        return pltpu.roll(x, cols - 1, 1)

    def west(x):
        return pltpu.roll(x, 1, 1)

    from_north = (0.2 - lat_wind) * inside
    from_south = (0.2 + lat_wind) * inside
    from_east = (0.2 - lon_wind) * inside * not_last
    from_west = (0.2 + lon_wind) * inside * not_first
    centre = 0.2 * inside
    forcings = []
    for step in range(STEPS):
        state = (
            centre * state
            + from_north * north(state)
            + from_south * south(state)
            + from_east * east(state)
            + from_west * west(state)
        )
        forcings.append(gain_ref[step] * (state - value_ref[step]))
    to_south = 0.2 + lat_wind
    to_north = 0.2 - lat_wind
    to_west = (0.2 + lon_wind) * not_first
    to_east = (0.2 - lon_wind) * not_last
    adjoint = None
    for step in reversed(range(STEPS)):
        pushed = forcings[step] if adjoint is None else adjoint + forcings[step]
        adjoint = inside * (
            0.2 * pushed
            + north(to_south * pushed)
            + south(to_north * pushed)
            + east(to_west * pushed)
            + west(to_east * pushed)
        )
    adjoint = adjoint[HALO : rows - HALO]
    own_rows = rows - 2 * HALO
    data = own_rows * cols // 128
    codes = row_codes(adjoint)
    adjoint_ref[:data] = to_16(as_tiles(rounded(adjoint, codes)))
    adjoint_ref[data:] = to_16(jnp.broadcast_to(codes, (own_rows, 128)))
    count = out_hbm.shape[0]
    copies = [
        pltpu.make_async_copy(
            adjoint_ref, out_hbm.at[copy, pl.ds(0, data + own_rows)], sems.at[copy]
        )
        for copy in range(count)
    ]
    for copy in copies:
        copy.start()
    width = cols // count
    lane = lax.broadcasted_iota(jnp.int32, (8, 128), 1)
    own = own_ref[...]
    codes = row_codes(own)
    own = rounded(own, codes)
    codes = jnp.where(lane < width, codes[:8], codes[8:])
    for copy in range(count):
        strip = slice(copy * width // 128 * 128, copy * width // 128 * 128 + 128)
        top, bottom = own[0:8, strip], own[8:16, strip]
        if copy % 2 == 0:
            piece = jnp.where(lane < width, top, pltpu.roll(bottom, width, 1))
        else:
            piece = jnp.where(lane < width, pltpu.roll(top, width, 1), bottom)
        piece_ref[copy] = to_16(jnp.concatenate([piece, codes], axis=0))
    last = pltpu.make_async_copy(
        piece_ref, out_hbm.at[:, pl.ds(data + own_rows, 16)], sems.at[count]
    )
    last.start()
    for copy in copies:
        copy.wait()
    last.wait()


def body(
    coarse_weights,
    perturbations,
    lat_matrix,
    lon_matrix,
    wind_field,
    observed_cell,
    observed_value,
    observed_weight,
):
    members_here, levels, row_count, lon_total = perturbations.shape
    coarse_rows, _, _, coarse_lons = coarse_weights.shape
    col_count = wind_field.shape[2]
    peers = lax.axis_size("mem")
    rings = lax.axis_size("lat_0")
    sides = lax.axis_size("lat_1")
    bands = rings * sides
    levels_here = levels // sides
    wide_count = row_count * sides
    pairs = members_here * levels_here
    quarters = peers // levels_here
    own_rows = wide_count // quarters
    quarter = lax.axis_index("mem") % quarters
    ring = lax.axis_index("lat_0")
    first = lax.axis_index("lat_1") == 0
    across = [(0, 1), (1, 0)]

    forward = []
    for m in range(peers):
        for z in range(rings):
            for x in range(sides):
                here = (m * rings + z) * sides + x
                if m % quarters < quarters - 1:
                    forward.append((here, here + bands))
                elif z < rings - 1:
                    forward.append((here, here - (quarters - 1) * bands + sides))
    backward = [(b, a) for a, b in forward]

    def halves(value, dim):
        low = lax.slice_in_dim(value, 0, levels_here, axis=dim)
        high = lax.slice_in_dim(value, levels_here, levels, axis=dim)
        return jnp.where(first, low, high), jnp.where(first, high, low)

    def in_order(mine, theirs, dim):
        return jnp.where(
            first, jnp.concatenate([mine, theirs], dim), jnp.concatenate([theirs, mine], dim)
        )

    weight_rows = pairs * coarse_rows
    coarse_total = bands * coarse_rows
    mine, theirs = halves(coarse_weights, 2)
    lat_rows = jnp.concatenate([lat_matrix[: row_count // 2], lat_matrix[row_count // 2 :]], axis=1)

    def by_pair_first(value):
        value = value.reshape(coarse_rows, pairs, coarse_lons)
        return jnp.transpose(value, (1, 0, 2))

    theirs = by_pair_first(theirs).reshape(weight_rows, coarse_lons)
    from_side = lax.ppermute(jnp.concatenate([theirs, lat_rows], axis=0), "lat_1", across)
    both = in_order(
        by_pair_first(mine), from_side[:weight_rows].reshape(pairs, coarse_rows, coarse_lons), 1
    ).reshape(sides * weight_rows, coarse_lons)
    both = jnp.concatenate([both, in_order(lat_rows, from_side[weight_rows:], 0)], axis=0)

    packed = jnp.concatenate(
        [observed_cell.astype(jnp.float32), observed_value, observed_weight], axis=0
    )
    kinds, _, _, block_count = packed.shape
    lanes = 2 * col_count
    packed = jnp.transpose(packed, (1, 2, 0, 3)).reshape(levels, row_count, kinds * block_count)
    packed = jnp.pad(packed, ((0, 0), (0, 0), (0, lanes - kinds * block_count)))
    winds = jnp.transpose(wind_field, (1, 0, 2)).reshape(1, row_count, lanes)
    parts = row_count // own_rows
    packed = packed.reshape(sides, levels_here, 1, parts, own_rows, lanes)
    winds = jnp.broadcast_to(
        winds.reshape(1, 1, 1, parts, own_rows, lanes), (1, levels_here, 1, parts, own_rows, lanes)
    )
    packed = jnp.transpose(jnp.concatenate([packed, winds], axis=0), (1, 2, 3, 0, 4, 5))
    packed = jnp.broadcast_to(
        packed, (levels_here, quarters // parts, parts, sides + 1, own_rows, lanes)
    )
    packed = swapped(packed.reshape(peers, sides + 1, own_rows, lanes), "mem", 0)

    side = lax.axis_index("lat_1")
    other_members = lax.dynamic_slice_in_dim(
        perturbations, (1 - side) * levels_here, levels_here, axis=1
    )
    other_members = lax.ppermute(other_members, "lat_1", across)
    up = [(i, (i + 1) % rings) for i in range(rings)]
    down = [(b, a) for a, b in up]
    blocks = {0: both}
    rising = falling = both
    for hop in range(1, rings // 2 + 1):
        rising = lax.ppermute(rising, "lat_0", up)
        if hop < rings - hop:
            falling = lax.ppermute(falling, "lat_0", down)
        if hop == 2:
            rising, falling, packed = lax.optimization_barrier((rising, falling, packed))
            passed = jnp.where(first, packed[:, 1:], jnp.stack([packed[:, 0], packed[:, 2]], axis=1))
            passed = lax.ppermute(passed, "lat_1", across)
        blocks[-hop % rings] = rising
        if hop < rings - hop:
            blocks[hop] = falling

    def lat_of(block):
        rows = block[sides * weight_rows :].reshape(sides, row_count // 2, coarse_lons)
        rows = jnp.concatenate([rows[..., :coarse_total], rows[..., coarse_total:]], 1)
        return rows.reshape(1, wide_count, coarse_total)

    columns = lat_of(both)[0].reshape(wide_count, rings, sides * coarse_rows)
    columns = lax.dynamic_slice_in_dim(
        jnp.concatenate([columns, columns], axis=1), ring, rings, axis=1
    ).reshape(wide_count, coarse_total)

    scalars = pl.BlockSpec(memory_space=pltpu.SMEM)
    whole = pl.BlockSpec(memory_space=pltpu.VMEM)
    roomy = pltpu.CompilerParams(vmem_limit_bytes=48 * 1024 * 1024)
    where_side = jnp.reshape(side, (1,)).astype(jnp.int32)
    is_own = (quarter // parts == side).astype(jnp.int32)
    local = pl.pallas_call(
        arrange_kernel,
        out_shape=jax.ShapeDtypeStruct(
            (own_rows, 2 * lon_total + kinds * peers * block_count), jnp.float32
        ),
        in_specs=[scalars, whole, whole],
        out_specs=whole,
        compiler_params=roomy,
    )(jnp.stack([side.astype(jnp.int32), is_own]), packed, passed)
    seen_before = lax.ppermute(local[-HALO:], ALL, forward)
    seen_after = lax.ppermute(local[:HALO], ALL, backward)
    seen_before, seen_after, other_members = lax.optimization_barrier(
        (seen_before, seen_after, other_members)
    )
    anywhere = pl.BlockSpec(memory_space=pl.ANY)
    piece_rows = own_rows * lon_total // 128 + own_rows
    partial_sum, lat_ring = pl.pallas_call(
        localize_kernel,
        out_shape=[
            jax.ShapeDtypeStruct((peers, piece_rows, 128), jnp.int16),
            jax.ShapeDtypeStruct((rings, wide_count, coarse_total), jnp.bfloat16),
        ],
        in_specs=[scalars] + [whole] * (4 + rings),
        out_specs=[whole] * 2,
        compiler_params=roomy,
    )(
        where_side,
        columns,
        lon_matrix,
        perturbations,
        other_members,
        *[blocks[d] for d in range(rings)],
    )
    arrived = swapped(partial_sum, "mem", 0)

    wide_rows = own_rows + 2 * HALO
    wide_wind, gains, values = pl.pallas_call(
        spread_kernel,
        out_shape=[
            jax.ShapeDtypeStruct((count, wide_rows, lon_total), jnp.float32)
            for count in (2, STEPS, STEPS)
        ],
        in_specs=[whole] * 3,
        out_specs=[whole] * 3,
        compiler_params=roomy,
    )(seen_before, local, seen_after)

    scale = (members_here * peers - 1) ** -0.5
    own = pl.pallas_call(
        functools.partial(add_kernel, scale),
        out_shape=jax.ShapeDtypeStruct((own_rows, lon_total), jnp.float32),
        in_specs=[whole],
        out_specs=whole,
        compiler_params=roomy,
    )(arrived)

    before = lax.ppermute(own[-HALO:], ALL, forward)
    after = lax.ppermute(own[:HALO], ALL, backward)
    place = jnp.stack(
        [ring * wide_count + quarter * own_rows - HALO, jnp.int32(row_count * bands)]
    ).astype(jnp.int32)
    copies = pl.pallas_call(
        stencil_kernel,
        out_shape=jax.ShapeDtypeStruct((peers, piece_rows + 16, 128), jnp.int16),
        in_specs=[scalars] + [whole] * 6,
        out_specs=anywhere,
        scratch_shapes=[
            pltpu.VMEM((piece_rows, 128), jnp.int16),
            pltpu.VMEM((peers, 16, 128), jnp.int16),
            pltpu.SemaphoreType.DMA((peers + 1,)),
        ],
        compiler_params=roomy,
    )(place, own, before, after, wide_wind, gains, values)

    adjoint_all = swapped(copies, "mem", 0)
    repeats = pairs // rings
    projected, tiles = pl.pallas_call(
        project_kernel,
        out_shape=[
            jax.ShapeDtypeStruct((rings, repeats * wide_count + 16, coarse_lons), jnp.int16),
            jax.ShapeDtypeStruct((sides, levels_here, row_count, col_count), jnp.float32),
        ],
        in_specs=[scalars] + [whole] * 4,
        out_specs=[whole] * 2,
        compiler_params=roomy,
    )(where_side, adjoint_all, jnp.transpose(lon_matrix), perturbations, other_members)
    _, lat_ring = lax.optimization_barrier((projected, lat_ring))
    lat_all = lax.dynamic_slice_in_dim(
        jnp.concatenate([lat_ring, lat_ring], axis=0), rings - ring, rings, axis=0
    )
    lat_all = jnp.broadcast_to(lat_all[:, None], (rings, repeats, wide_count, coarse_total))
    lat_all = jnp.transpose(lat_all.reshape(rings * repeats * wide_count, coarse_total))
    by_pair = swapped(projected, "lat_0", 0)
    full = pl.pallas_call(
        functools.partial(gather_kernel, scale),
        out_shape=jax.ShapeDtypeStruct((bands, repeats, coarse_rows, coarse_lons), jnp.float32),
        in_specs=[whole] * 2,
        out_specs=whole,
        compiler_params=roomy,
    )(by_pair, lat_all)
    full = swapped(full, LAT, 0)
    full = full.reshape(
        members_here, rings // members_here, sides, pairs // rings, coarse_rows, coarse_lons
    )
    full = jnp.transpose(full, (4, 0, 2, 1, 3, 5)).reshape(coarse_weights.shape)
    gradient = full + coarse_weights.astype(jnp.float32)

    kept = jnp.where(first, tiles[0], tiles[1])
    sent = jnp.where(first, tiles[1], tiles[0])
    increment = in_order(kept, lax.ppermute(sent, "lat_1", across), 0)
    return (gradient, increment)


def solution(mesh):
    split = Mesh(mesh.devices.reshape(mesh.shape["mem"], 8, 2), ("mem", "lat_0", "lat_1"))
    placed = (
        P(LAT, "mem", None, None),
        P("mem", None, LAT, None),
        P(LAT, None),
        P(),
        P(None, LAT, "mem"),
        P(None, None, LAT, "mem"),
        P(None, None, LAT, "mem"),
        P(None, None, LAT, "mem"),
    )
    return jax.shard_map(
        body,
        mesh=split,
        in_specs=placed,
        out_specs=(P(LAT, "mem", None, None), P(None, LAT, "mem")),
        check_vma=False,
    )
```

```python
import functools

import jax
import jax.numpy as jnp
from jax import lax
from jax.experimental import pallas as pl
from jax.experimental.pallas import tpu as pltpu
from jax.sharding import Mesh
from jax.sharding import PartitionSpec as P

STEPS = 4
OBLK = 8
HALO = 8
LN2 = 0.6931471805599453
STEPS_16 = 32767.0
LAT = ("lat_0", "lat_1")
ALL = ("mem", "lat_0", "lat_1")

def swapped(value, axis, dim):
    return lax.all_to_all(value, axis, split_axis=dim, concat_axis=dim, tiled=True)


def two_terms(value):
    high = value.astype(jnp.bfloat16)
    low = (value - high.astype(jnp.float32)).astype(jnp.bfloat16)
    return jnp.concatenate([high, low], axis=0)


def dot(a, b):
    return jnp.dot(a, b, preferred_element_type=jnp.float32)


def row_codes(value):
    largest = jnp.maximum(jnp.max(jnp.abs(value), axis=1, keepdims=True), 1e-30)
    return jnp.ceil(jnp.log(largest) * (256.0 / LN2)) + 1.0


def code_scale(codes):
    return jnp.exp(codes * (LN2 / 256.0))


def rounded(value, codes):
    return jnp.round(value * (STEPS_16 / code_scale(codes)))


def to_16(value):
    return value.astype(jnp.int32).astype(jnp.int16)


def from_16(value):
    return value.astype(jnp.int32).astype(jnp.float32)


def as_tiles(value):
    rows, cols = value.shape
    return jnp.concatenate(
        [
            value[t * 8 : (t + 1) * 8, at * 128 : (at + 1) * 128]
            for t in range(rows // 8)
            for at in range(cols // 128)
        ],
        axis=0,
    )


def from_tiles(value, row_tiles):
    lane_tiles = value.shape[0] // 8 // row_tiles
    rows = []
    for t in range(row_tiles):
        start = t * lane_tiles * 8
        strips = [value[start + at * 8 : start + (at + 1) * 8] for at in range(lane_tiles)]
        rows.append(jnp.concatenate(strips, axis=1))
    return jnp.concatenate(rows, axis=0)


def tile_scales(codes, lane_tiles):
    scales = code_scale(codes) * (1.0 / STEPS_16)
    parts = []
    for t in range(scales.shape[0] // 8):
        parts += [scales[t * 8 : (t + 1) * 8]] * lane_tiles
    return jnp.concatenate(parts, axis=0)


def member_rows(side, own_ref, other_ref, member, level):
    levels_here = other_ref.shape[1]
    own = own_ref[member, side * levels_here + level].astype(jnp.float32)
    other = other_ref[member, level].astype(jnp.float32)
    low = jnp.where(side == 0, own, other)
    high = jnp.where(side == 0, other, own)
    return jnp.concatenate([low, high], axis=0)


def localize_kernel(side_ref, columns_ref, lon_ref, own_ref, other_ref, *refs):
    block_refs, sum_ref, lat_ref = refs[:-2], refs[-2], refs[-1]
    members, levels_here, row_count, lon_total = other_ref.shape
    tall = 2 * row_count
    side = side_ref[0]
    per_block = columns_ref.shape[1] // len(block_refs)
    columns = columns_ref[...]
    lon = lon_ref[...]
    for level in range(levels_here):
        narrow = []
        for member in range(members):
            start = (member * levels_here + level) * per_block
            weights = jnp.concatenate([ref[start : start + per_block] for ref in block_refs], axis=0)
            narrow.append(dot(columns, weights))
        localized = dot(two_terms(jnp.concatenate(narrow, axis=0)), lon)
        total = None
        for member in range(members):
            at = member * tall
            term = localized[at : at + tall] + localized[at + members * tall : at + (members + 1) * tall]
            term = term * member_rows(side, own_ref, other_ref, member, level)
            total = term if total is None else total + term
        count = sum_ref.shape[0] // levels_here
        piece_rows = tall // count
        data = piece_rows * lon_total // 128
        codes = row_codes(total)
        total = rounded(total, codes)
        for piece in range(count):
            part = slice(piece * piece_rows, (piece + 1) * piece_rows)
            sum_ref[level * count + piece, :data] = to_16(as_tiles(total[part]))
            sum_ref[level * count + piece, data:] = to_16(
                jnp.broadcast_to(codes[part], (piece_rows, 128))
            )
    half = row_count // 2
    for at, ref in enumerate(block_refs):
        lat = ref[ref.shape[0] - row_count :]
        for part in range(4):
            rows = lat[part // 2 * half : (part // 2 + 1) * half]
            lat_ref[at, part * half : (part + 1) * half] = rows[
                :, part % 2 * lat_ref.shape[2] : (part % 2 + 1) * lat_ref.shape[2]
            ]


def add_kernel(scale, message_ref, out_ref):
    sources, rows, _ = message_ref.shape
    own_rows, lon_total = out_ref.shape
    total = None
    for source in range(sources):
        value = from_16(message_ref[source, : rows - own_rows])
        codes = from_16(message_ref[source, rows - own_rows :])
        value = value * tile_scales(codes, lon_total // 128)
        total = value if total is None else total + value
    out_ref[...] = from_tiles(total, own_rows // 8) * scale


def project_kernel(side_ref, message_ref, lon_ref, own_ref, other_ref, out_ref, tile_ref):
    members, levels_here, row_count, lon_total = other_ref.shape
    rings, _, coarse_lons = out_ref.shape
    tall = 2 * row_count
    side = side_ref[0]
    lon = lon_ref[...]
    quarters = message_ref.shape[0] // levels_here
    own_rows = tall // quarters
    lane_tiles = lon_total // 128
    data = own_rows * lane_tiles
    width = tile_ref.shape[3]
    per_message = members * levels_here // rings
    row = lax.broadcasted_iota(jnp.int32, (tall, 128), 0)
    lane = lax.broadcasted_iota(jnp.int32, (tall, 128), 1)
    tails = [jnp.zeros((1, 128), jnp.float32) for _ in range(rings)]
    for level in range(levels_here):
        pieces = []
        for q in range(quarters):
            value = from_16(message_ref[level * quarters + q, :data])
            codes = from_16(message_ref[level * quarters + q, data : data + own_rows])
            pieces.append(from_tiles(value * tile_scales(codes, lane_tiles), own_rows // 8))
            tail = from_16(message_ref[level * quarters + q, data + own_rows :])
            tile = tail[:8] * (code_scale(tail[8:]) * (1.0 / STEPS_16))
            band, start = q * own_rows // row_count, q * own_rows % row_count
            tile_ref[band, level, start : start + 8] = tile[:, :width]
            tile_ref[band, level, start + 8 : start + 16] = tile[:, width:]
        adjoint = jnp.concatenate(pieces, axis=0)
        product = [
            member_rows(side, own_ref, other_ref, member, level) * adjoint for member in range(members)
        ]
        projected = dot(two_terms(jnp.concatenate(product, axis=0)), lon)
        for member in range(members):
            at = member * tall
            value = projected[at : at + tall] + projected[at + members * tall : at + (members + 1) * tall]
            pair = member * levels_here + level
            ring, place = pair // per_message, pair % per_message
            codes = row_codes(value)
            whole = jnp.round(value * (STEPS_16 / code_scale(codes))).astype(jnp.int32)
            out_ref[ring, place * tall : (place + 1) * tall] = whole.astype(jnp.int16)
            mark = jnp.where(lane == row + place * tall, codes, 0.0)
            tails[ring] = tails[ring] + jnp.sum(mark, axis=0, keepdims=True)
    end = per_message * tall
    for ring in range(rings):
        tail = jnp.broadcast_to(tails[ring], (16, 128)).astype(jnp.int32).astype(jnp.int16)
        out_ref[ring, end : end + 16] = jnp.concatenate([tail] * (coarse_lons // 128), axis=1)


def gather_kernel(scale, message_ref, lat_ref, out_ref):
    rings, rows, lons = message_ref.shape
    bands, places, coarse_rows, _ = out_ref.shape
    data = rows - 16
    coarse = bands * coarse_rows
    high, low, scales = [], [], []
    for ring in range(rings):
        value = message_ref[ring, :data].astype(jnp.int32).astype(jnp.float32)
        upper = jnp.floor(value * (1.0 / 256.0)) * 256.0
        high.append(upper.astype(jnp.bfloat16))
        low.append((value - upper).astype(jnp.bfloat16))
        codes = message_ref[ring, data:].astype(jnp.int32).astype(jnp.float32)[:1, :data]
        scales.append(code_scale(codes) * (scale / STEPS_16))
    high = jnp.concatenate(high, axis=0)
    low = jnp.concatenate(low, axis=0)
    lat = lat_ref[...].astype(jnp.float32) * jnp.concatenate(scales, axis=1)
    place = lax.broadcasted_iota(jnp.int32, lat.shape, 1) % data // (data // places)
    lat = jnp.concatenate([jnp.where(place == p, lat, 0.0) for p in range(places)], axis=0)
    terms = two_terms(lat)
    total = dot(terms, high)
    total = total[: places * coarse] + (total[places * coarse :] + dot(terms[: places * coarse], low))
    for band in range(bands):
        for p in range(places):
            at = p * coarse + band * coarse_rows
            out_ref[band, p] = total[at : at + coarse_rows]


def arrange_kernel(side_ref, own_ref, other_ref, out_ref):
    peers, _, row_count, lanes = own_ref.shape
    side = side_ref[0]
    is_own = side_ref[1] == 1
    lane = lax.broadcasted_iota(jnp.int32, (row_count, lanes), 1)
    width = lanes // 2
    pick = lambda peer, which, mine: jnp.where(is_own, own_ref[peer, mine], other_ref[peer, which])
    winds = [pick(peer, 1, 2) for peer in range(peers)]
    seen = [pick(peer, 0, side) for peer in range(peers)]
    lon_total = peers * width
    for at in range(peers // 2):
        even, odd = winds[2 * at], winds[2 * at + 1]
        spot = slice(at * lanes, (at + 1) * lanes)
        out_ref[:, spot] = jnp.where(lane < width, even, pltpu.roll(odd, width, 1))
        spot = slice(lon_total + at * lanes, lon_total + (at + 1) * lanes)
        out_ref[:, spot] = jnp.where(lane < width, pltpu.roll(even, width, 1), odd)
    blocks = lanes // peers
    kinds = (out_ref.shape[1] - 2 * lon_total) // lanes
    owner = lane // blocks
    for kind in range(kinds):
        total = jnp.zeros((row_count, lanes), jnp.float32)
        for peer in range(peers):
            shift = (peer - kind) * blocks % lanes
            value = seen[peer] if shift == 0 else pltpu.roll(seen[peer], shift, 1)
            total = jnp.where(owner == peer, value, total)
        spot = slice(2 * lon_total + kind * lanes, 2 * lon_total + (kind + 1) * lanes)
        out_ref[:, spot] = total


def spread_kernel(before_ref, local_ref, after_ref, wind_ref, gain_ref, value_ref):
    _, rows, cols = wind_ref.shape
    lanes = cols // OBLK
    width = local_ref.shape[1]
    local = jnp.concatenate(
        [before_ref[:, :width], local_ref[...], after_ref[:, :width]], axis=0
    )
    wind_ref[0] = local[:, :cols]
    wind_ref[1] = local[:, cols : 2 * cols]
    sights = [local[:, 2 * cols + k * lanes : 2 * cols + (k + 1) * lanes] for k in range(3 * STEPS)]
    cells = jnp.concatenate(sights[:STEPS], axis=0).astype(jnp.bfloat16)
    others = jnp.concatenate(sights[STEPS:], axis=0)
    high = others.astype(jnp.bfloat16)
    rest = others - high.astype(jnp.float32)
    middle = rest.astype(jnp.bfloat16)
    low = (rest - middle.astype(jnp.float32)).astype(jnp.bfloat16)
    block = lax.broadcasted_iota(jnp.int32, (lanes, cols), 0)
    spread = (lax.broadcasted_iota(jnp.int32, (lanes, cols), 1) // OBLK == block).astype(jnp.bfloat16)
    cells = dot(cells, spread)
    wide = dot(high, spread) + (dot(middle, spread) + dot(low, spread))
    offset = lax.broadcasted_iota(jnp.int32, (rows, cols), 1) % OBLK
    offset = offset.astype(jnp.float32)
    for step in range(STEPS):
        value_ref[step] = wide[step * rows : (step + 1) * rows]
        hit = jnp.abs(cells[step * rows : (step + 1) * rows] - offset) < 0.5
        weight = wide[(STEPS + step) * rows : (STEPS + step + 1) * rows]
        gain_ref[step] = jnp.where(hit, weight, 0.0)


def stencil_kernel(place_ref, own_ref, before_ref, after_ref, wind_ref, gain_ref, value_ref, out_hbm, adjoint_ref, piece_ref, sems):
    rows, cols = wind_ref.shape[1:]
    first_row = place_ref[0]
    last_row = place_ref[1]
    skip = before_ref.shape[1] - cols
    state = jnp.concatenate([before_ref[:, skip:], own_ref[...], after_ref[:, skip:]], axis=0)
    row = lax.broadcasted_iota(jnp.int32, (rows, cols), 0) + first_row
    col = lax.broadcasted_iota(jnp.int32, (rows, cols), 1)
    inside = ((row >= 0) & (row < last_row)).astype(jnp.float32)
    not_first = (col > 0).astype(jnp.float32)
    not_last = (col < cols - 1).astype(jnp.float32)
    lon_wind = 0.5 * wind_ref[0]
    lat_wind = 0.5 * wind_ref[1]

    def north(x):
        return pltpu.roll(x, rows - 1, 0)

    def south(x):
        return pltpu.roll(x, 1, 0)

    def east(x):
        return pltpu.roll(x, cols - 1, 1)

    def west(x):
        return pltpu.roll(x, 1, 1)

    from_north = (0.2 - lat_wind) * inside
    from_south = (0.2 + lat_wind) * inside
    from_east = (0.2 - lon_wind) * inside * not_last
    from_west = (0.2 + lon_wind) * inside * not_first
    centre = 0.2 * inside
    forcings = []
    for step in range(STEPS):
        state = (
            centre * state
            + from_north * north(state)
            + from_south * south(state)
            + from_east * east(state)
            + from_west * west(state)
        )
        forcings.append(gain_ref[step] * (state - value_ref[step]))
    to_south = 0.2 + lat_wind
    to_north = 0.2 - lat_wind
    to_west = (0.2 + lon_wind) * not_first
    to_east = (0.2 - lon_wind) * not_last
    adjoint = None
    for step in reversed(range(STEPS)):
        pushed = forcings[step] if adjoint is None else adjoint + forcings[step]
        adjoint = inside * (
            0.2 * pushed
            + north(to_south * pushed)
            + south(to_north * pushed)
            + east(to_west * pushed)
            + west(to_east * pushed)
        )
    adjoint = adjoint[HALO : rows - HALO]
    own_rows = rows - 2 * HALO
    data = own_rows * cols // 128
    codes = row_codes(adjoint)
    adjoint_ref[:data] = to_16(as_tiles(rounded(adjoint, codes)))
    adjoint_ref[data:] = to_16(jnp.broadcast_to(codes, (own_rows, 128)))
    count = out_hbm.shape[0]
    copies = [
        pltpu.make_async_copy(
            adjoint_ref, out_hbm.at[copy, pl.ds(0, data + own_rows)], sems.at[copy]
        )
        for copy in range(count)
    ]
    for copy in copies:
        copy.start()
    width = cols // count
    lane = lax.broadcasted_iota(jnp.int32, (8, 128), 1)
    own = own_ref[...]
    codes = row_codes(own)
    own = rounded(own, codes)
    codes = jnp.where(lane < width, codes[:8], codes[8:])
    for copy in range(count):
        strip = slice(copy * width // 128 * 128, copy * width // 128 * 128 + 128)
        top, bottom = own[0:8, strip], own[8:16, strip]
        if copy % 2 == 0:
            piece = jnp.where(lane < width, top, pltpu.roll(bottom, width, 1))
        else:
            piece = jnp.where(lane < width, pltpu.roll(top, width, 1), bottom)
        piece_ref[copy] = to_16(jnp.concatenate([piece, codes], axis=0))
    last = pltpu.make_async_copy(
        piece_ref, out_hbm.at[:, pl.ds(data + own_rows, 16)], sems.at[count]
    )
    last.start()
    for copy in copies:
        copy.wait()
    last.wait()


def body(
    coarse_weights,
    perturbations,
    lat_matrix,
    lon_matrix,
    wind_field,
    observed_cell,
    observed_value,
    observed_weight,
):
    members_here, levels, row_count, lon_total = perturbations.shape
    coarse_rows, _, _, coarse_lons = coarse_weights.shape
    col_count = wind_field.shape[2]
    peers = lax.axis_size("mem")
    rings = lax.axis_size("lat_0")
    sides = lax.axis_size("lat_1")
    bands = rings * sides
    levels_here = levels // sides
    wide_count = row_count * sides
    pairs = members_here * levels_here
    quarters = peers // levels_here
    own_rows = wide_count // quarters
    quarter = lax.axis_index("mem") % quarters
    ring = lax.axis_index("lat_0")
    first = lax.axis_index("lat_1") == 0
    across = [(0, 1), (1, 0)]

    forward = []
    for m in range(peers):
        for z in range(rings):
            for x in range(sides):
                here = (m * rings + z) * sides + x
                if m % quarters < quarters - 1:
                    forward.append((here, here + bands))
                elif z < rings - 1:
                    forward.append((here, here - (quarters - 1) * bands + sides))
    backward = [(b, a) for a, b in forward]

    def halves(value, dim):
        low = lax.slice_in_dim(value, 0, levels_here, axis=dim)
        high = lax.slice_in_dim(value, levels_here, levels, axis=dim)
        return jnp.where(first, low, high), jnp.where(first, high, low)

    def in_order(mine, theirs, dim):
        return jnp.where(
            first, jnp.concatenate([mine, theirs], dim), jnp.concatenate([theirs, mine], dim)
        )

    weight_rows = pairs * coarse_rows
    coarse_total = bands * coarse_rows
    mine, theirs = halves(coarse_weights, 2)
    lat_rows = jnp.concatenate([lat_matrix[: row_count // 2], lat_matrix[row_count // 2 :]], axis=1)

    def by_pair_first(value):
        value = value.reshape(coarse_rows, pairs, coarse_lons)
        return jnp.transpose(value, (1, 0, 2))

    theirs = by_pair_first(theirs).reshape(weight_rows, coarse_lons)
    from_side = lax.ppermute(jnp.concatenate([theirs, lat_rows], axis=0), "lat_1", across)
    both = in_order(
        by_pair_first(mine), from_side[:weight_rows].reshape(pairs, coarse_rows, coarse_lons), 1
    ).reshape(sides * weight_rows, coarse_lons)
    both = jnp.concatenate([both, in_order(lat_rows, from_side[weight_rows:], 0)], axis=0)

    packed = jnp.concatenate(
        [observed_cell.astype(jnp.float32), observed_value, observed_weight], axis=0
    )
    kinds, _, _, block_count = packed.shape
    lanes = 2 * col_count
    packed = jnp.transpose(packed, (1, 2, 0, 3)).reshape(levels, row_count, kinds * block_count)
    packed = jnp.pad(packed, ((0, 0), (0, 0), (0, lanes - kinds * block_count)))
    winds = jnp.transpose(wind_field, (1, 0, 2)).reshape(1, row_count, lanes)
    parts = row_count // own_rows
    packed = packed.reshape(sides, levels_here, 1, parts, own_rows, lanes)
    winds = jnp.broadcast_to(
        winds.reshape(1, 1, 1, parts, own_rows, lanes), (1, levels_here, 1, parts, own_rows, lanes)
    )
    packed = jnp.transpose(jnp.concatenate([packed, winds], axis=0), (1, 2, 3, 0, 4, 5))
    packed = jnp.broadcast_to(
        packed, (levels_here, quarters // parts, parts, sides + 1, own_rows, lanes)
    )
    packed = swapped(packed.reshape(peers, sides + 1, own_rows, lanes), "mem", 0)

    side = lax.axis_index("lat_1")
    other_members = lax.dynamic_slice_in_dim(
        perturbations, (1 - side) * levels_here, levels_here, axis=1
    )
    other_members = lax.ppermute(other_members, "lat_1", across)
    up = [(i, (i + 1) % rings) for i in range(rings)]
    down = [(b, a) for a, b in up]
    blocks = {0: both}
    rising = falling = both
    for hop in range(1, rings // 2 + 1):
        rising = lax.ppermute(rising, "lat_0", up)
        if hop < rings - hop:
            falling = lax.ppermute(falling, "lat_0", down)
        if hop == 2:
            rising, falling, packed = lax.optimization_barrier((rising, falling, packed))
            passed = jnp.where(first, packed[:, 1:], jnp.stack([packed[:, 0], packed[:, 2]], axis=1))
            passed = lax.ppermute(passed, "lat_1", across)
        blocks[-hop % rings] = rising
        if hop < rings - hop:
            blocks[hop] = falling

    def lat_of(block):
        rows = block[sides * weight_rows :].reshape(sides, row_count // 2, coarse_lons)
        rows = jnp.concatenate([rows[..., :coarse_total], rows[..., coarse_total:]], 1)
        return rows.reshape(1, wide_count, coarse_total)

    columns = lat_of(both)[0].reshape(wide_count, rings, sides * coarse_rows)
    columns = lax.dynamic_slice_in_dim(
        jnp.concatenate([columns, columns], axis=1), ring, rings, axis=1
    ).reshape(wide_count, coarse_total)

    scalars = pl.BlockSpec(memory_space=pltpu.SMEM)
    whole = pl.BlockSpec(memory_space=pltpu.VMEM)
    roomy = pltpu.CompilerParams(vmem_limit_bytes=48 * 1024 * 1024)
    where_side = jnp.reshape(side, (1,)).astype(jnp.int32)
    anywhere = pl.BlockSpec(memory_space=pl.ANY)
    piece_rows = own_rows * lon_total // 128 + own_rows
    partial_sum, lat_ring = pl.pallas_call(
        localize_kernel,
        out_shape=[
            jax.ShapeDtypeStruct((peers, piece_rows, 128), jnp.int16),
            jax.ShapeDtypeStruct((rings, wide_count, coarse_total), jnp.bfloat16),
        ],
        in_specs=[scalars] + [whole] * (4 + rings),
        out_specs=[whole] * 2,
        compiler_params=roomy,
    )(
        where_side,
        columns,
        lon_matrix,
        perturbations,
        other_members,
        *[blocks[d] for d in range(rings)],
    )
    partial_sum, packed, passed = lax.optimization_barrier((partial_sum, packed, passed))
    arrived = swapped(partial_sum, "mem", 0)

    is_own = (quarter // parts == side).astype(jnp.int32)
    local = pl.pallas_call(
        arrange_kernel,
        out_shape=jax.ShapeDtypeStruct(
            (own_rows, 2 * lon_total + kinds * peers * block_count), jnp.float32
        ),
        in_specs=[scalars, whole, whole],
        out_specs=whole,
        compiler_params=roomy,
    )(jnp.stack([side.astype(jnp.int32), is_own]), packed, passed)
    scale = (members_here * peers - 1) ** -0.5
    own = pl.pallas_call(
        functools.partial(add_kernel, scale),
        out_shape=jax.ShapeDtypeStruct((own_rows, lon_total), jnp.float32),
        in_specs=[whole],
        out_specs=whole,
        compiler_params=roomy,
    )(arrived)

    before = lax.ppermute(jnp.concatenate([local[-HALO:], own[-HALO:]], axis=1), ALL, forward)
    after = lax.ppermute(jnp.concatenate([local[:HALO], own[:HALO]], axis=1), ALL, backward)
    wide_rows = own_rows + 2 * HALO
    wide_wind, gains, values = pl.pallas_call(
        spread_kernel,
        out_shape=[
            jax.ShapeDtypeStruct((count, wide_rows, lon_total), jnp.float32)
            for count in (2, STEPS, STEPS)
        ],
        in_specs=[whole] * 3,
        out_specs=[whole] * 3,
        compiler_params=roomy,
    )(before, local, after)

    place = jnp.stack(
        [ring * wide_count + quarter * own_rows - HALO, jnp.int32(row_count * bands)]
    ).astype(jnp.int32)
    copies = pl.pallas_call(
        stencil_kernel,
        out_shape=jax.ShapeDtypeStruct((peers, piece_rows + 16, 128), jnp.int16),
        in_specs=[scalars] + [whole] * 6,
        out_specs=anywhere,
        scratch_shapes=[
            pltpu.VMEM((piece_rows, 128), jnp.int16),
            pltpu.VMEM((peers, 16, 128), jnp.int16),
            pltpu.SemaphoreType.DMA((peers + 1,)),
        ],
        compiler_params=roomy,
    )(place, own, before, after, wide_wind, gains, values)

    adjoint_all = swapped(copies, "mem", 0)
    repeats = pairs // rings
    projected, tiles = pl.pallas_call(
        project_kernel,
        out_shape=[
            jax.ShapeDtypeStruct((rings, repeats * wide_count + 16, coarse_lons), jnp.int16),
            jax.ShapeDtypeStruct((sides, levels_here, row_count, col_count), jnp.float32),
        ],
        in_specs=[scalars] + [whole] * 4,
        out_specs=[whole] * 2,
        compiler_params=roomy,
    )(where_side, adjoint_all, jnp.transpose(lon_matrix), perturbations, other_members)
    _, lat_ring = lax.optimization_barrier((projected, lat_ring))
    lat_all = lax.dynamic_slice_in_dim(
        jnp.concatenate([lat_ring, lat_ring], axis=0), rings - ring, rings, axis=0
    )
    lat_all = jnp.broadcast_to(lat_all[:, None], (rings, repeats, wide_count, coarse_total))
    lat_all = jnp.transpose(lat_all.reshape(rings * repeats * wide_count, coarse_total))
    by_pair = swapped(projected, "lat_0", 0)
    full = pl.pallas_call(
        functools.partial(gather_kernel, scale),
        out_shape=jax.ShapeDtypeStruct((bands, repeats, coarse_rows, coarse_lons), jnp.float32),
        in_specs=[whole] * 2,
        out_specs=whole,
        compiler_params=roomy,
    )(by_pair, lat_all)
    full = swapped(full, LAT, 0)
    full = full.reshape(
        members_here, rings // members_here, sides, pairs // rings, coarse_rows, coarse_lons
    )
    full = jnp.transpose(full, (4, 0, 2, 1, 3, 5)).reshape(coarse_weights.shape)
    gradient = full + coarse_weights.astype(jnp.float32)

    kept = jnp.where(first, tiles[0], tiles[1])
    sent = jnp.where(first, tiles[1], tiles[0])
    increment = in_order(kept, lax.ppermute(sent, "lat_1", across), 0)
    return (gradient, increment)


def solution(mesh):
    split = Mesh(mesh.devices.reshape(mesh.shape["mem"], 8, 2), ("mem", "lat_0", "lat_1"))
    placed = (
        P(LAT, "mem", None, None),
        P("mem", None, LAT, None),
        P(LAT, None),
        P(),
        P(None, LAT, "mem"),
        P(None, None, LAT, "mem"),
        P(None, None, LAT, "mem"),
        P(None, None, LAT, "mem"),
    )
    return jax.shard_map(
        body,
        mesh=split,
        in_specs=placed,
        out_specs=(P(LAT, "mem", None, None), P(None, LAT, "mem")),
        check_vma=False,
    )
```
